32 devices in a mesh: expert: 8 (over z, y), tensor: 4 (over x, core).
Axes of the slice: x: 2, y: 2, z: 4, core: 2. Of those that a mesh axis runs over, the one named last changes fastest.
Arguments:
- tokens: bfloat16 [6144, 768], P('expert'), may hold values from -6 to 6
- order: int32 [6144], replicated, may hold values from 0 to 6143, as said below
- lengths: int32 [8, 3], P('expert'), may hold values from 1 to 512, 768 in all within a row
- routes: int32 [6144, 2], P('expert'), may hold values from 0 to 15, all different within a row
- attn_gain: bfloat16 [768], replicated, may hold values from 0.5 to 1.5
- w_query: bfloat16 [768, 768], P(None, 'tensor'), may hold values from -0.21875 to 0.21875
- w_key: bfloat16 [768, 768], P(None, 'tensor'), may hold values from -0.21875 to 0.21875
- w_value: bfloat16 [768, 768], P(None, 'tensor'), may hold values from -0.21875 to 0.21875
- w_out: bfloat16 [768, 768], P('tensor'), may hold values from -1.25 to 1.25
- ffn_gain: bfloat16 [768], replicated, may hold values from 0.5 to 1.5
- w_router: bfloat16 [768, 16], replicated, may hold values from -0.21875 to 0.21875
- shared_gate: bfloat16 [768, 2048], P(None, 'tensor'), may hold values from -0.21875 to 0.21875
- shared_up: bfloat16 [768, 2048], P(None, 'tensor'), may hold values from -0.21875 to 0.21875
- shared_down: bfloat16 [2048, 768], P('tensor'), may hold values from -0.125 to 0.125
- expert_gate: bfloat16 [16, 768, 2048], P('expert', None, 'tensor'), may hold values from -0.21875 to 0.21875
- expert_up: bfloat16 [16, 768, 2048], P('expert', None, 'tensor'), may hold values from -0.21875 to 0.21875
- expert_down: bfloat16 [16, 2048, 768], P('expert', 'tensor'), may hold values from -0.125 to 0.125
- cotangent: bfloat16 [6144, 768], P('expert'), may hold values from -6 to 6
Outputs:
- output: bfloat16 [6144, 768], P('expert')
- d_tokens: bfloat16 [6144, 768], P('expert')
- g_attn_gain: float32 [768], replicated
- g_query: float32 [768, 768], P(None, 'tensor')
- g_key: float32 [768, 768], P(None, 'tensor')
- g_value: float32 [768, 768], P(None, 'tensor')
- g_out: float32 [768, 768], P('tensor')
- g_ffn_gain: float32 [768], replicated
- g_router: float32 [768, 16], replicated
- g_shared_gate: float32 [768, 2048], P(None, 'tensor')
- g_shared_up: float32 [768, 2048], P(None, 'tensor')
- g_shared_down: float32 [2048, 768], P('tensor')
- g_expert_gate: float32 [16, 768, 2048], P('expert', None, 'tensor')
- g_expert_up: float32 [16, 768, 2048], P('expert', None, 'tensor')
- g_expert_down: float32 [16, 2048, 768], P('expert', 'tensor')
The draws below stay inside these ranges and needn't reach their ends.
Inputs may be any that keep to these rules, and one draw needn't show every extreme that they name: `order`: a permutation; of the 768 given rows of each aligned block, exactly 96 go to each group, group g being grouped rows g * 768 to (g + 1) * 768 - 1. Row g holds the lengths of group g's sequences, summing to 768, the largest exactly 512. `routes`: each row names two different experts.
All inputs are finite; a program needn't handle non-finite values.
Results may differ from the reference program's by a relative error of at most 0.015.
Values may be sent and summed in bfloat16 or wider, within the bound.
No kernel may reach another device: no remote copies, remote signals or barrier semaphores. Data moves between devices by JAX's collectives and lax.ppermute only.
A program may use at most 384 MiB of HBM per device.

```python
import math
import jax
import jax.numpy as jnp
import numpy as np
from jax import lax

D = 768
HEADS = 12
HD = 64
FF_S = 2048
EXPERTS = 16
FF_E = 2048
TOK_DEV = 768
LONGEST = 512
SEQS = 3
CAP = 120
GROUPS = 8
TOKENS = 6144
REPL = 1
SLABS = 16
N_TENSOR = 4


def shuffled(single_key):
    return jax.random.permutation(single_key, TOK_DEV)


def draw_order(key, part):
    key = jax.random.fold_in(key, 11)
    share_rows = TOK_DEV // GROUPS
    deal_keys = jax.random.split(jax.random.fold_in(key, 1), GROUPS)
    place_keys = jax.random.split(jax.random.fold_in(key, 2), GROUPS)
    dealt = jax.vmap(shuffled)(deal_keys).astype(jnp.int32)
    placed = jax.vmap(shuffled)(place_keys).astype(jnp.int32)
    target = dealt // share_rows
    within = dealt % share_rows
    source = jnp.arange(GROUPS, dtype=jnp.int32)[:, None]
    landing = placed[target, source * share_rows + within]
    return (target * TOK_DEV + landing).reshape(-1).astype(jnp.int32)


def block_levels(rng, extent, pieces, least, high):
    def one(axis_at, blocks):
        steps = jax.random.uniform(jax.random.fold_in(jax.random.fold_in(rng, 6), axis_at), (blocks,), jnp.float32, least / len(pieces), high / len(pieces))
        return jnp.repeat(jnp.exp(steps), extent[axis_at] // blocks).reshape((-1,) + (1,) * (len(extent) - axis_at - 1))

    gain = one(*pieces[0])
    for cut in pieces[1:]:
        gain = gain * one(*cut)
    return gain


def choose_distinct(key, rows, number_of, top, lift):
    order = jax.random.permutation(jax.random.fold_in(key, 1), number_of)
    pull = order
    for power in range(3):
        pull = pull * pull // number_of
    pull = pull * lift // number_of
    lots = jax.random.randint(jax.random.fold_in(key, 2), (rows, number_of), 0, 4096) + pull
    sure = jax.random.permutation(jax.random.fold_in(key, 3), rows)[jnp.arange(number_of) % rows]
    lots = jnp.where(jnp.arange(rows)[:, None] == sure[None, :], 1 << 14, lots)
    score = lots * number_of + jnp.arange(number_of)
    return lax.top_k(score.astype(jnp.int32), top)[1].astype(jnp.int32)


def split_up(count, total, reach, slope):
    loads = [(1 << 20) // math.isqrt(grade ** slope) + 1 for grade in range(2, count + 1)]
    rest, holding = total - reach - (count - 1), [1] * (count - 1)
    while rest > 0:
        movable = [i for i in range(count - 1) if holding[i] < reach]
        pool, budget = sum([loads[i] for i in movable]), rest
        for i in movable:
            more = min(reach - holding[i], max(1, budget * loads[i] // pool), rest)
            holding[i] = holding[i] + more
            rest = rest - more
    return np.array([reach] + holding)


def ragged_sizes(key, count, total, most, skew):
    if count == 2:
        one = jax.random.randint(key, (), max(1, total - most), min(most, total - 1) + 1)
        return jnp.stack([one, total - one])
    tallies = jnp.asarray(split_up(count, total, most, skew), jnp.int32)
    couples = (count - 1) // 2
    donor, receiver = tallies[1:1 + 2 * couples:2], tallies[2:2 + 2 * couples:2]
    margin = jnp.minimum(donor - 1, most - receiver)
    moved = jax.random.randint(jax.random.fold_in(key, 1), (couples,), 0, 1 << 20) % (margin + 1)
    tallies = tallies.at[1:1 + 2 * couples:2].set(donor - moved).at[2:2 + 2 * couples:2].set(receiver + moved)
    return tallies[jax.random.permutation(jax.random.fold_in(key, 2), count)]


def bell_draw(own_key, shape, width, limit, cuts=(), kind=jnp.bfloat16):
    drawn = width * jax.random.normal(own_key, shape, jnp.float32)
    if cuts:
        drawn = drawn * block_levels(own_key, shape, cuts, -0.22, 0.18)
    return jnp.clip(drawn, -limit, limit).astype(kind)


def setup_inputs(seed: int = 0) -> dict:
    streams_of = jax.random.split(jax.random.key(seed), 19)
    tokens = bell_draw(streams_of[0], (TOKENS, D), 1.0, 6.0, ((0, 8),))
    order = draw_order(jax.random.fold_in(streams_of[18], 71), 0)
    lengths = jax.vmap(lambda own: ragged_sizes(own, SEQS, TOK_DEV, LONGEST, 2))(jax.random.split(streams_of[2], GROUPS)).reshape((GROUPS, SEQS)).astype(jnp.int32)
    routes = choose_distinct(streams_of[3], TOKENS, EXPERTS, 2, 1024)
    attn_gain = jnp.clip(1.0 + 0.1 * jax.random.normal(streams_of[4], (D,), jnp.float32), 0.5, 1.5).astype(jnp.bfloat16)
    w_query = bell_draw(streams_of[5], (D, HEADS * HD), D ** -0.5, 0.21875, ((1, 4),))
    w_key = bell_draw(streams_of[6], (D, HEADS * HD), D ** -0.5, 0.21875, ((1, 4),))
    w_value = bell_draw(streams_of[7], (D, HEADS * HD), D ** -0.5, 0.21875, ((1, 4),))
    w_out = bell_draw(streams_of[8], (HEADS * HD, D), (D // 32) ** -0.5, 1.25, ((0, 4),))
    ffn_gain = jnp.clip(1.0 + 0.1 * jax.random.normal(streams_of[9], (D,), jnp.float32), 0.5, 1.5).astype(jnp.bfloat16)
    w_router = bell_draw(streams_of[10], (D, EXPERTS), D ** -0.5, 0.21875)
    shared_gate = bell_draw(streams_of[11], (D, FF_S), D ** -0.5, 0.21875, ((1, 4),))
    shared_up = bell_draw(streams_of[12], (D, FF_S), D ** -0.5, 0.21875, ((1, 4),))
    shared_down = bell_draw(streams_of[13], (FF_S, D), FF_S ** -0.5, 0.125, ((0, 4),))
    expert_gate = bell_draw(streams_of[14], (SLABS, D, FF_E // REPL), D ** -0.5, 0.21875, ((0, 8), (2, 4)))
    expert_up = bell_draw(streams_of[15], (SLABS, D, FF_E // REPL), D ** -0.5, 0.21875, ((0, 8), (2, 4)))
    expert_down = bell_draw(streams_of[16], (SLABS, FF_E // REPL, D), FF_E ** -0.5, 0.125, ((0, 8), (1, 4)))
    cotangent = bell_draw(streams_of[17], (TOKENS, D), 1.0, 6.0, ((0, 8),))
    return {"tokens": tokens, "order": order, "lengths": lengths, "routes": routes, "attn_gain": attn_gain, "w_query": w_query, "w_key": w_key, "w_value": w_value, "w_out": w_out, "ffn_gain": ffn_gain, "w_router": w_router, "shared_gate": shared_gate, "shared_up": shared_up, "shared_down": shared_down, "expert_gate": expert_gate, "expert_up": expert_up, "expert_down": expert_down, "cotangent": cotangent}


EPSILON = 1e-05
ROPE_BASE = 10000.0
MASKED = -1e+30

@jax.custom_vjp
def low(v):
    return lax.optimization_barrier(v.astype(jnp.bfloat16)).astype(jnp.float32)

@jax.custom_vjp
def low_back(v):
    return v

def low_keep(v):
    return (low(v), None)

def low_pass(kept, grad):
    return (grad,)

def back_keep(v):
    return (v, None)

def back_low(kept, grad):
    return (low(grad),)
low.defvjp(low_keep, low_pass)
low_back.defvjp(back_keep, back_low)

def exact_dot(left_side, right_side):
    return jnp.dot(left_side, right_side, precision=lax.Precision.HIGHEST, preferred_element_type=jnp.float32)

def normalize(values, gain_row):
    return values * lax.rsqrt(lax.optimization_barrier(jnp.mean(values * values, axis=-1, keepdims=True)) + EPSILON) * gain_row

def layout(seq_lengths):
    seq_ends = jnp.cumsum(seq_lengths).astype(jnp.int32)
    row_ids = jnp.arange(TOK_DEV, dtype=jnp.int32)
    passed = row_ids[:, None] >= seq_ends[None, :]
    sequence_segment = lax.optimization_barrier(jnp.sum(passed.astype(jnp.int32), axis=1)).astype(jnp.int32)
    position = (row_ids - lax.optimization_barrier(jnp.sum(jnp.where(passed, seq_lengths[None, :], 0), axis=1))).astype(jnp.int32)
    return (position, sequence_segment)

def rotate(values, position):
    half_size = HD // 2
    frequency = ROPE_BASE ** (-jnp.arange(half_size, dtype=jnp.float32) / half_size)
    angles = position.astype(jnp.float32)[:, None] * frequency[None, :]
    cos_table = jnp.cos(angles)[:, None, :]
    sin_table = jnp.sin(angles)[:, None, :]
    shaped = values.reshape(values.shape[0], -1, HD)
    front_half = shaped[..., :half_size]
    back_half = shaped[..., half_size:]
    turned = jnp.concatenate([front_half * cos_table - back_half * sin_table, back_half * cos_table + front_half * sin_table], axis=-1)
    return turned.reshape(values.shape)

def assign_slots(chosen_routes):
    flat_routes = chosen_routes.reshape(-1).astype(jnp.int32)
    onehot = (flat_routes[:, None] == jnp.arange(EXPERTS, dtype=jnp.int32)[None, :]).astype(jnp.int32)
    slot_rank = (lax.optimization_barrier(jnp.sum(onehot * jnp.cumsum(onehot, axis=0), axis=1)) - 1).astype(jnp.int32)
    index_of_slot = jnp.where(slot_rank < CAP, flat_routes * CAP + slot_rank, EXPERTS * CAP).astype(jnp.int32)
    pair_rows = (jnp.arange(2 * TOK_DEV, dtype=jnp.int32) // 2).astype(jnp.int32)
    source_rows = jnp.full((EXPERTS * CAP + 1,), TOK_DEV, jnp.int32).at[index_of_slot].set(pair_rows)[:EXPERTS * CAP]
    return (index_of_slot, source_rows)

def take_rows(table, indices):
    return table[indices]

def attend(packed):
    query, key, value, sequence_segment = packed
    q_heads = query.reshape(TOK_DEV, HEADS, HD)
    k_heads = key.reshape(TOK_DEV, HEADS, HD)
    v_heads = value.reshape(TOK_DEV, HEADS, HD)
    scores = low_back(jnp.einsum('qhd,khd->hqk', q_heads, k_heads, precision=lax.Precision.HIGHEST) * HD ** (-0.5))
    row_ids = jnp.arange(TOK_DEV, dtype=jnp.int32)
    allowed = (sequence_segment[:, None] == sequence_segment[None, :]) & (row_ids[:, None] >= row_ids[None, :])
    scores = jnp.where(allowed[None], scores, MASKED)
    row_max = lax.optimization_barrier(jnp.max(scores, axis=-1, keepdims=True))
    log_total = row_max + jnp.log(lax.optimization_barrier(jnp.sum(jnp.exp(scores - row_max), axis=-1, keepdims=True)))
    weights = low(jnp.exp(scores - log_total))
    mixture = jnp.einsum('hqk,khd->qhd', weights, v_heads, precision=lax.Precision.HIGHEST)
    return mixture.reshape(TOK_DEV, HEADS * HD)

def expert(packed):
    rows_in, gate_pieces, up_pieces, down_pieces = packed
    produced = jnp.zeros(rows_in.shape, jnp.float32)
    for piece_id in range(N_TENSOR):
        taken_rows = low_back(rows_in)
        gate_lin = low_back(exact_dot(taken_rows, gate_pieces[piece_id]))
        up_lin = low_back(exact_dot(taken_rows, up_pieces[piece_id]))
        piece_mid = low(jax.nn.silu(gate_lin) * up_lin)
        produced = produced + low(exact_dot(piece_mid, down_pieces[piece_id]))
    return produced

def by_group(values):
    return values.reshape(GROUPS, TOK_DEV, values.shape[-1])

def forward_pass(grouped, attn_gain, w_query, w_key, w_value, w_out, ffn_gain, w_router, shared_gate, shared_up, shared_down, expert_gate, expert_up, expert_down, position, sequence_segment, routes, index_of_slot, source_rows):
    hidden_one = low(normalize(grouped, attn_gain))
    query = low(rotate(low_back(exact_dot(hidden_one, w_query)), position))
    key = low(rotate(low_back(exact_dot(hidden_one, w_key)), position))
    value = low(low_back(exact_dot(hidden_one, w_value)))
    mixture = lax.map(jax.checkpoint(attend), (by_group(query), by_group(key), by_group(value), sequence_segment))
    attended = low(low_back(mixture.reshape(TOKENS, HEADS * HD)))
    resid_two = grouped + low_back(exact_dot(attended, w_out))
    hidden_two = low(normalize(resid_two, ffn_gain))
    gate_shared = low_back(exact_dot(hidden_two, shared_gate))
    up_shared = low_back(exact_dot(hidden_two, shared_up))
    shared_out = exact_dot(low(jax.nn.silu(gate_shared) * up_shared), shared_down)
    logits = low_back(exact_dot(hidden_two, w_router))
    picked = routes[:, :, None] == jnp.arange(EXPERTS, dtype=jnp.int32)[None, None, :]
    chosen = lax.optimization_barrier(jnp.sum(jnp.where(picked, logits[:, None, :], 0.0), axis=-1))
    raised = jnp.exp(chosen - lax.optimization_barrier(jnp.max(chosen, axis=-1, keepdims=True)))
    gate_weights = raised / lax.optimization_barrier(jnp.sum(raised, axis=-1, keepdims=True))
    padded = jnp.concatenate([by_group(hidden_two), jnp.zeros((GROUPS, 1, D), jnp.float32)], axis=1)
    gathered = jax.vmap(take_rows)(padded, source_rows)
    per_expert = gathered.reshape(GROUPS, EXPERTS, CAP, D).transpose(1, 0, 2, 3).reshape(EXPERTS, GROUPS * CAP, D)
    piece_width = FF_E // (REPL * N_TENSOR)
    gate_pieces = expert_gate.reshape(EXPERTS, REPL, D, N_TENSOR, piece_width).transpose(0, 3, 2, 1, 4).reshape(EXPERTS, N_TENSOR, D, REPL * piece_width)
    up_pieces = expert_up.reshape(EXPERTS, REPL, D, N_TENSOR, piece_width).transpose(0, 3, 2, 1, 4).reshape(EXPERTS, N_TENSOR, D, REPL * piece_width)
    down_pieces = expert_down.reshape(EXPERTS, REPL, N_TENSOR, piece_width, D).transpose(0, 2, 1, 3, 4).reshape(EXPERTS, N_TENSOR, REPL * piece_width, D)
    produced = lax.map(jax.checkpoint(expert), (per_expert, gate_pieces, up_pieces, down_pieces))
    returned = produced.reshape(EXPERTS, GROUPS, CAP, D).transpose(1, 0, 2, 3).reshape(GROUPS, EXPERTS * CAP, D)
    returned = jnp.concatenate([returned, jnp.zeros((GROUPS, 1, D), jnp.float32)], axis=1)
    pair_out = low_back(jax.vmap(take_rows)(returned, index_of_slot).reshape(TOKENS, 2, D))
    mixed_experts = lax.optimization_barrier(jnp.sum(gate_weights[:, :, None] * pair_out, axis=1))
    return resid_two + shared_out + mixed_experts

def reference(tokens, order, lengths, routes, attn_gain, w_query, w_key, w_value, w_out, ffn_gain, w_router, shared_gate, shared_up, shared_down, expert_gate, expert_up, expert_down, cotangent):
    position, sequence_segment = jax.vmap(layout)(lengths)
    index_of_slot, source_rows = jax.vmap(assign_slots)(routes.reshape(GROUPS, TOK_DEV, 2))
    flattened_position = position.reshape(TOKENS)
    inverse = jnp.zeros((TOKENS,), jnp.int32).at[order].set(jnp.arange(TOKENS, dtype=jnp.int32))
    grouped = tokens[inverse]
    grouped_cot = cotangent[inverse]

    def layer_apply(tokens_function, attention_function, query_function, key_function, value_function, output_function, feedforward_function, router_function, shared_gate_function, shared_up_function, shared_down_function, expert_gate_function, expert_up_function, expert_down_function):
        return forward_pass(tokens_function, attention_function, query_function, key_function, value_function, output_function, feedforward_function, router_function, shared_gate_function, shared_up_function, shared_down_function, expert_gate_function, expert_up_function, expert_down_function, flattened_position, sequence_segment, routes, index_of_slot, source_rows)
    floats = tuple((item.astype(jnp.float32) for item in (grouped, attn_gain, w_query, w_key, w_value, w_out, ffn_gain, w_router, shared_gate, shared_up, shared_down, expert_gate, expert_up, expert_down)))
    result, pullback = jax.vjp(layer_apply, *floats)
    gradients = pullback(grouped_cot.astype(jnp.float32))
    output = result.astype(jnp.bfloat16)[order]
    d_tokens = gradients[0].astype(jnp.bfloat16)[order]
    return (output, d_tokens, gradients[1], gradients[2], gradients[3], gradients[4], gradients[5], gradients[6], gradients[7], gradients[8], gradients[9], gradients[10], gradients[11], gradients[12], gradients[13])
```

```python
import jax
import jax.numpy as jnp
from jax import lax
from jax.sharding import PartitionSpec as P

HD = 64
EXPERTS = 16
CAP = 120


EPSILON = 1e-05
ROPE_BASE = 10000.0
MASKED = -1e30


def rms_scale(values):
    return lax.rsqrt(jnp.mean(values * values, axis=-1, keepdims=True) + EPSILON)


def matmul(left_side, right_side):
    return jnp.dot(left_side, right_side, preferred_element_type=jnp.float32)


def matmul_bt(left_side, right_side):
    return lax.dot_general(
        left_side, right_side, (((1,), (1,)), ((), ())), preferred_element_type=jnp.float32
    )


def matmul_at(left_side, right_side):
    return lax.dot_general(
        left_side, right_side, (((0,), (0,)), ((), ())), preferred_element_type=jnp.float32
    )


def silu_value(gate_in):
    return gate_in * jax.nn.sigmoid(gate_in)


def silu_slope(gate_in):
    sigma = jax.nn.sigmoid(gate_in)
    return sigma * (1.0 + gate_in * (1.0 - sigma))


def rotate(values, cos_table, sin_table):
    half_size = HD // 2
    shaped = values.reshape(values.shape[0], -1, HD)
    front_half = shaped[..., :half_size]
    back_half = shaped[..., half_size:]
    cos_wide = cos_table[:, None, :]
    sin_wide = sin_table[:, None, :]
    turned = jnp.concatenate(
        [
            front_half * cos_wide - back_half * sin_wide,
            back_half * cos_wide + front_half * sin_wide,
        ],
        axis=-1,
    )
    return turned.reshape(values.shape)


def block_scores(query, key, sequence_segment, block_index, block_rows, score_scale):
    start_row = block_index * block_rows
    end_row = start_row + block_rows
    q_part = query[start_row:end_row].reshape(block_rows, -1, HD)
    k_part = key[:end_row].reshape(end_row, -1, HD)
    scores = (
        jnp.einsum("qhd,khd->hqk", q_part, k_part, preferred_element_type=jnp.float32) * score_scale
    )
    q_rows = jnp.arange(start_row, end_row, dtype=jnp.int32)
    k_rows = jnp.arange(end_row, dtype=jnp.int32)
    allowed = (sequence_segment[start_row:end_row, None] == sequence_segment[None, :end_row]) & (
        q_rows[:, None] >= k_rows[None, :]
    )
    return (jnp.where(allowed[None], scores, MASKED), q_part, k_part)


def core_swap(values):
    return lax.ppermute(values, "tensor", [(i, i ^ 1) for i in range(4)])


def far_swap(values):
    return lax.ppermute(values, "tensor", [(i, i ^ 2) for i in range(4)])


def exchange(values):
    return lax.all_to_all(values, "expert", split_axis=0, concat_axis=0, tiled=True)


def in_order(bit, own, other, axis=0):
    return jnp.where(
        bit == 0,
        jnp.concatenate([own, other], axis=axis),
        jnp.concatenate([other, own], axis=axis),
    )


def gather_four(bit_low, bit_high, own, axis):
    far = far_swap(own)
    near = core_swap(own)
    far_near = core_swap(far)
    here = in_order(bit_low, own, near, axis)
    there = in_order(bit_low, far, far_near, axis)
    return in_order(bit_high, here, there, axis)


def select(onehot, values):
    return jnp.dot(onehot, values, preferred_element_type=jnp.float32).astype(jnp.bfloat16)


def total_over_tensor(values, bit_low):
    half = values.shape[0] // 2
    kept = lax.dynamic_slice_in_dim(values, bit_low * half, half, 0)
    given = lax.dynamic_slice_in_dim(values, (1 - bit_low) * half, half, 0)
    pair = (kept.astype(jnp.float32) + core_swap(given).astype(jnp.float32)).astype(jnp.bfloat16)
    four = (pair.astype(jnp.float32) + far_swap(pair).astype(jnp.float32)).astype(jnp.bfloat16)
    return in_order(bit_low, four, core_swap(four))


def half_over_tensor(values, bit_low):
    half = values.shape[0] // 2
    kept = lax.dynamic_slice_in_dim(values, bit_low * half, half, 0)
    given = lax.dynamic_slice_in_dim(values, (1 - bit_low) * half, half, 0)
    pair = (kept.astype(jnp.float32) + core_swap(given).astype(jnp.float32)).astype(jnp.bfloat16)
    return pair.astype(jnp.float32) + far_swap(pair).astype(jnp.float32)


def body(
    tokens,
    order,
    lengths,
    routes,
    attn_gain,
    w_query,
    w_key,
    w_value,
    w_out,
    ffn_gain,
    w_router,
    shared_gate,
    shared_up,
    shared_down,
    expert_gate,
    expert_up,
    expert_down,
    cotangent,
):
    row_count, feat_width = tokens.shape
    group_count = lax.axis_size("expert")
    share_rows = row_count // group_count
    half_share = share_rows // 2
    half_rows = row_count // 2
    my_group = lax.axis_index("expert")
    my_tensor = lax.axis_index("tensor")
    bit_low = lax.rem(my_tensor, 2)
    bit_high = my_tensor // 2
    slab_dev = expert_gate.shape[0]
    slab_total = slab_dev * group_count
    replicas = max(1, slab_total // EXPERTS)
    half_slots = slab_dev * CAP // 2
    block_rows = 256
    block_count = row_count // block_rows
    score_scale = HD ** (-0.5)
    row_ids = jnp.arange(row_count, dtype=jnp.int32)
    earlier = (row_ids[:, None] < row_ids[None, :]).astype(jnp.bfloat16)

    local_order = lax.dynamic_slice_in_dim(order, my_group * row_count, row_count, 0)
    groups = jnp.arange(group_count, dtype=jnp.int32)
    dest_group = local_order // row_count
    dest_onehot = (groups[:, None] == dest_group[None, :]).astype(jnp.bfloat16)
    dest_before = matmul(dest_onehot, earlier)
    send_rank = jnp.sum(dest_onehot.astype(jnp.float32) * dest_before, axis=0).astype(jnp.int32)
    send_half = send_rank // half_share
    send_slot = send_half * half_rows + dest_group * half_share + send_rank % half_share
    send_pick = send_slot[None, :] == (
        bit_low * half_rows + jnp.arange(half_rows, dtype=jnp.int32)[:, None]
    )
    send_pick = send_pick.astype(jnp.bfloat16)
    in_tokens = exchange(select(send_pick, tokens))
    in_cot = exchange(select(send_pick, cotangent))

    all_order = order.reshape(group_count, row_count)
    mine = all_order // row_count == my_group
    arrive_rank = matmul(mine.astype(jnp.bfloat16), earlier).astype(jnp.int32)
    arrive_rank = jnp.where(mine, arrive_rank, -1)
    landing = all_order - my_group * row_count
    target = jnp.sum(
        jnp.where(
            arrive_rank[:, None, :] == jnp.arange(share_rows, dtype=jnp.int32)[None, :, None],
            landing[:, None, :],
            0,
        ),
        axis=-1,
    )
    target = target.reshape(group_count, 2, half_share).transpose(1, 0, 2).reshape(2, half_rows)
    target_own = lax.dynamic_index_in_dim(target, bit_low, 0, keepdims=False)
    target_other = lax.dynamic_index_in_dim(target, 1 - bit_low, 0, keepdims=False)
    place_own = (row_ids[:, None] == target_own[None, :]).astype(jnp.bfloat16)
    place_other = (row_ids[:, None] == target_other[None, :]).astype(jnp.bfloat16)

    def place(own):
        other = core_swap(own)
        return (matmul(place_own, own) + matmul(place_other, other)).astype(jnp.bfloat16)

    expert_ids = jnp.arange(EXPERTS, dtype=jnp.int32)
    member_one = expert_ids[:, None] == routes[None, :, 0]
    member_two = expert_ids[:, None] == routes[None, :, 1]
    member = member_one | member_two
    slot_rank = matmul(member.astype(jnp.bfloat16), earlier).astype(jnp.int32)
    slot_rank = jnp.where(member, slot_rank, -1)

    def slots_of(half):
        ranks = jnp.repeat(slot_rank, replicas, axis=0).reshape(group_count, slab_dev, row_count)
        ranks = lax.dynamic_index_in_dim(ranks, half * half_slots // CAP, 1, keepdims=False)
        slot = half * half_slots % CAP + jnp.arange(half_slots, dtype=jnp.int32)
        picked = ranks[:, None, :] == slot[None, :, None]
        return picked.reshape(group_count * half_slots, row_count)

    slots_own = slots_of(bit_low)
    slots_one = slots_own.astype(jnp.bfloat16)

    whole_out = gather_four(bit_low, bit_high, w_out, 0)

    seq_lengths = lengths[0]
    seq_ends = jnp.cumsum(seq_lengths)
    passed = row_ids[:, None] >= seq_ends[None, :]
    sequence_segment = jnp.sum(passed.astype(jnp.int32), axis=1)
    position = row_ids - jnp.sum(jnp.where(passed, seq_lengths[None, :], 0), axis=1)
    half_size = HD // 2
    frequency = ROPE_BASE ** (-jnp.arange(half_size, dtype=jnp.float32) / half_size)
    angles = position.astype(jnp.float32)[:, None] * frequency[None, :]
    cos_table = jnp.cos(angles)
    sin_table = jnp.sin(angles)

    grouped = place(in_tokens)
    grouped_cot = place(in_cot)
    cot_rows = exchange(select(slots_one, grouped_cot))

    resid = grouped.astype(jnp.float32)
    scale_one = rms_scale(resid)
    normed_one = resid * scale_one
    gain_one = attn_gain.astype(jnp.float32)
    hidden_one = (normed_one * gain_one).astype(jnp.bfloat16)
    query = rotate(matmul(hidden_one, w_query), cos_table, sin_table).astype(jnp.bfloat16)
    key = rotate(matmul(hidden_one, w_key), cos_table, sin_table).astype(jnp.bfloat16)
    value = matmul(hidden_one, w_value).astype(jnp.bfloat16)
    block_outputs = []
    log_totals = []
    for block_index in range(block_count):
        scores, q_part, k_part = block_scores(
            query, key, sequence_segment, block_index, block_rows, score_scale
        )
        row_max = jnp.max(scores, axis=-1, keepdims=True)
        log_total = row_max + jnp.log(jnp.sum(jnp.exp(scores - row_max), axis=-1, keepdims=True))
        weights = jnp.exp(scores - log_total).astype(jnp.bfloat16)
        end_row = (block_index + 1) * block_rows
        v_part = value[:end_row].reshape(end_row, -1, HD)
        mixture = jnp.einsum("hqk,khd->qhd", weights, v_part, preferred_element_type=jnp.float32)
        block_outputs.append(mixture.reshape(block_rows, -1))
        log_totals.append(log_total)
    attended = jnp.concatenate(block_outputs, axis=0).astype(jnp.bfloat16)
    whole_attended = gather_four(bit_low, bit_high, attended, 1)
    resid_two = resid + matmul(whole_attended, whole_out)
    scale_two = rms_scale(resid_two)
    normed_two = resid_two * scale_two
    gain_two = ffn_gain.astype(jnp.float32)
    hidden_two = (normed_two * gain_two).astype(jnp.bfloat16)

    hidden_rows = exchange(select(slots_one, hidden_two))
    logits = matmul(hidden_two, w_router)
    picked = routes[:, :, None] == expert_ids[None, None, :]
    chosen = jnp.sum(jnp.where(picked, logits[:, None, :], 0.0), axis=-1)
    raised = jnp.exp(chosen - jnp.max(chosen, axis=-1, keepdims=True))
    gate_weights = raised / jnp.sum(raised, axis=-1, keepdims=True)
    dest_slab = jnp.arange(group_count, dtype=jnp.int32) * slab_dev + bit_low * half_slots // CAP
    dest_expert = dest_slab // replicas
    first_here = routes[None, :, 0] == dest_expert[:, None]
    gate_of = jnp.where(first_here, gate_weights[None, :, 0], gate_weights[None, :, 1])
    slots_cube = slots_own.reshape(group_count, half_slots, row_count)
    gate_slots = jnp.sum(jnp.where(slots_cube, gate_of[:, None, :], 0.0), axis=-1)
    gate_rows = exchange(gate_slots).reshape(group_count * half_slots, 1)

    def both(own):
        return in_order(bit_low, own[None], core_swap(own)[None])

    gate_shared = matmul(hidden_two, shared_gate)
    up_shared = matmul(hidden_two, shared_up)
    act_shared = silu_value(gate_shared)
    shared_mid = (act_shared * up_shared).astype(jnp.bfloat16)
    shared_out = matmul(shared_mid, shared_down)
    d_mid_shared = matmul_bt(grouped_cot, shared_down)
    g_shared_down = matmul_at(shared_mid, grouped_cot)
    d_up_shared = (d_mid_shared * act_shared).astype(jnp.bfloat16)
    d_gate_shared = (d_mid_shared * up_shared * silu_slope(gate_shared)).astype(jnp.bfloat16)
    g_shared_gate = matmul_at(hidden_two, d_gate_shared)
    g_shared_up = matmul_at(hidden_two, d_up_shared)
    d_hidden_shared = matmul_bt(d_gate_shared, shared_gate) + matmul_bt(d_up_shared, shared_up)

    rows_h = both(hidden_rows)
    rows_c = both(cot_rows)
    rows_g = both(gate_rows)
    if slab_dev == 2:
        gate_w, up_w, down_w = (expert_gate, expert_up, expert_down)
    else:
        rows_h = rows_h.reshape(1, -1, feat_width)
        rows_c = rows_c.reshape(1, -1, feat_width)
        rows_g = rows_g.reshape(1, -1, 1)
        gate_w, up_w, down_w = (expert_gate, expert_up, expert_down)
    gate_lin = jnp.einsum("kci,kif->kcf", rows_h, gate_w, preferred_element_type=jnp.float32)
    up_lin = jnp.einsum("kci,kif->kcf", rows_h, up_w, preferred_element_type=jnp.float32)
    act = silu_value(gate_lin)
    mid32 = act * up_lin
    mid = mid32.astype(jnp.bfloat16)
    out_rows = jnp.einsum("kcf,kfd->kcd", mid, down_w, preferred_element_type=jnp.float32)
    out_rows = (out_rows * rows_g).astype(jnp.bfloat16)
    d_raw = jnp.einsum("kcd,kfd->kcf", rows_c, down_w, preferred_element_type=jnp.float32)
    d_gate_rows = jnp.sum(d_raw * mid.astype(jnp.float32), axis=-1)
    d_act = d_raw * rows_g
    d_up = (d_act * act).astype(jnp.bfloat16)
    d_gate = (d_act * up_lin * silu_slope(gate_lin)).astype(jnp.bfloat16)
    back_rows = jnp.einsum("kcf,kif->kci", d_gate, gate_w, preferred_element_type=jnp.float32)
    back_rows = back_rows + jnp.einsum(
        "kcf,kif->kci", d_up, up_w, preferred_element_type=jnp.float32
    )
    back_rows = back_rows.astype(jnp.bfloat16)
    mid_g = (mid.astype(jnp.float32) * rows_g).astype(jnp.bfloat16)
    g_expert_gate = jnp.einsum("kci,kcf->kif", rows_h, d_gate, preferred_element_type=jnp.float32)
    g_expert_up = jnp.einsum("kci,kcf->kif", rows_h, d_up, preferred_element_type=jnp.float32)
    g_expert_down = jnp.einsum("kcf,kcd->kfd", mid_g, rows_c, preferred_element_type=jnp.float32)

    def give_back(values, dtype):
        values = values.reshape((2, group_count * half_slots) + values.shape[2:])
        kept = lax.dynamic_index_in_dim(values, bit_low, 0, keepdims=False)
        given = lax.dynamic_index_in_dim(values, 1 - bit_low, 0, keepdims=False)
        total = kept.astype(jnp.float32) + core_swap(given).astype(jnp.float32)
        return exchange(total.astype(dtype))

    back_own = give_back(back_rows, jnp.bfloat16)
    dg_own = give_back(d_gate_rows[..., None].reshape(2, -1, 1), jnp.float32)
    out_own = give_back(out_rows, jnp.bfloat16)

    d_hidden_part = (matmul_at(slots_one, back_own) + d_hidden_shared).astype(jnp.bfloat16)
    d_hidden = total_over_tensor(d_hidden_part, bit_low).astype(jnp.float32)
    dg_cube = dg_own.reshape(group_count, half_slots, 1)
    dg_of = jnp.sum(jnp.where(slots_cube, dg_cube, 0.0), axis=1)
    dg_one = jnp.sum(jnp.where(first_here, dg_of, 0.0), axis=0)
    dg_two = jnp.sum(jnp.where(routes[None, :, 1] == dest_expert[:, None], dg_of, 0.0), axis=0)
    dg_part = jnp.stack([dg_one, dg_two], axis=0)
    dg_part = dg_part + core_swap(dg_part)
    dg_part = dg_part + far_swap(dg_part)
    d_gates = dg_part.T
    d_chosen = gate_weights * (d_gates - jnp.sum(gate_weights * d_gates, axis=-1, keepdims=True))
    d_logits = jnp.sum(jnp.where(picked, d_chosen[:, :, None], 0.0), axis=1).astype(jnp.bfloat16)
    g_router = matmul_at(hidden_two, d_logits)
    d_two = d_hidden + matmul_bt(d_logits, w_router)
    g_ffn_gain = jnp.sum(d_two * normed_two, axis=0)
    e_two = d_two * gain_two
    grad_out = grouped_cot.astype(jnp.float32)
    d_resid = grad_out + scale_two * (
        e_two - normed_two * jnp.mean(e_two * normed_two, axis=-1, keepdims=True)
    )
    d_proj = d_resid.astype(jnp.bfloat16)
    g_out = matmul_at(attended, d_proj)
    d_attended = matmul_bt(d_proj, w_out).astype(jnp.bfloat16)
    query_grads = []
    key_grad = jnp.zeros((row_count, query.shape[1]), jnp.float32)
    value_grad = jnp.zeros((row_count, query.shape[1]), jnp.float32)
    for block_index in range(block_count):
        scores, q_part, k_part = block_scores(
            query, key, sequence_segment, block_index, block_rows, score_scale
        )
        weights = jnp.exp(scores - log_totals[block_index])
        start_row = block_index * block_rows
        end_row = start_row + block_rows
        grad_part = d_attended[start_row:end_row].reshape(block_rows, -1, HD)
        v_part = value[:end_row].reshape(end_row, -1, HD)
        d_weights = jnp.einsum(
            "qhd,khd->hqk", grad_part, v_part, preferred_element_type=jnp.float32
        )
        row_inner = jnp.sum(weights * d_weights, axis=-1, keepdims=True)
        d_scores = (weights * (d_weights - row_inner)).astype(jnp.bfloat16)
        query_grads.append(
            (
                jnp.einsum("hqk,khd->qhd", d_scores, k_part, preferred_element_type=jnp.float32)
                * score_scale
            ).reshape(block_rows, -1)
        )
        key_term = (
            jnp.einsum("hqk,qhd->khd", d_scores, q_part, preferred_element_type=jnp.float32)
            * score_scale
        )
        key_grad = key_grad.at[:end_row].add(key_term.reshape(end_row, -1))
        value_term = jnp.einsum(
            "hqk,qhd->khd",
            weights.astype(jnp.bfloat16),
            grad_part,
            preferred_element_type=jnp.float32,
        )
        value_grad = value_grad.at[:end_row].add(value_term.reshape(end_row, -1))
    d_query = rotate(jnp.concatenate(query_grads, axis=0), cos_table, -sin_table).astype(
        jnp.bfloat16
    )
    d_key = rotate(key_grad, cos_table, -sin_table).astype(jnp.bfloat16)
    d_value = value_grad.astype(jnp.bfloat16)
    g_query = matmul_at(hidden_one, d_query)
    g_key = matmul_at(hidden_one, d_key)
    g_value = matmul_at(hidden_one, d_value)
    d_one = matmul_bt(d_query, w_query) + matmul_bt(d_key, w_key) + matmul_bt(d_value, w_value)
    d_one = total_over_tensor(d_one.astype(jnp.bfloat16), bit_low).astype(jnp.float32)
    g_attn_gain = jnp.sum(d_one * normed_one, axis=0)
    e_one = d_one * gain_one
    d_group = (
        d_resid
        + scale_one * (e_one - normed_one * jnp.mean(e_one * normed_one, axis=-1, keepdims=True))
    ).astype(jnp.bfloat16)

    ffn_part = (matmul_at(slots_one, out_own) + shared_out).astype(jnp.bfloat16)
    ffn_sum = total_over_tensor(ffn_part, bit_low).astype(jnp.float32)
    output_group = (resid_two + ffn_sum).astype(jnp.bfloat16)
    unsend = (
        send_slot[:, None] == jnp.arange(row_count, dtype=jnp.int32)[None, :]
    ).astype(jnp.bfloat16)

    def give_rows(values):
        own = exchange(matmul_at(place_own, values).astype(jnp.bfloat16))
        return select(unsend, in_order(bit_low, own, core_swap(own)))

    output = give_rows(output_group)
    d_tokens = give_rows(d_group)

    def total_over_groups(members):
        wide = jnp.concatenate([m.astype(jnp.bfloat16) for m in members], axis=0)
        return lax.psum(wide, "expert").astype(jnp.float32)

    hidden_s = shared_gate.shape[1]
    early = total_over_groups([g_shared_gate, g_shared_up])
    g_shared_gate, g_shared_up = early[:feat_width], early[feat_width:]
    gains = jnp.stack([g_ffn_gain, g_attn_gain], axis=0)
    late_down = total_over_groups([g_shared_down, g_out, g_router.T, gains])
    g_shared_down = late_down[:hidden_s]
    head_rows = w_out.shape[0]
    g_out = late_down[hidden_s : hidden_s + head_rows]
    at = hidden_s + head_rows
    g_router = late_down[at : at + EXPERTS].T
    g_ffn_gain = late_down[at + EXPERTS]
    g_attn_gain = late_down[at + EXPERTS + 1]
    late = total_over_groups([g_query, g_key, g_value])
    g_query = late[:feat_width]
    g_key = late[feat_width : 2 * feat_width]
    g_value = late[2 * feat_width :]
    return (
        output,
        d_tokens,
        g_attn_gain,
        g_query,
        g_key,
        g_value,
        g_out,
        g_ffn_gain,
        g_router,
        g_shared_gate,
        g_shared_up,
        g_shared_down,
        g_expert_gate,
        g_expert_up,
        g_expert_down,
    )


def solution(mesh):
    return jax.shard_map(
        body,
        mesh=mesh,
        in_specs=(
            P("expert", None),
            P(),
            P("expert", None),
            P("expert", None),
            P(),
            P(None, "tensor"),
            P(None, "tensor"),
            P(None, "tensor"),
            P("tensor", None),
            P(),
            P(),
            P(None, "tensor"),
            P(None, "tensor"),
            P("tensor", None),
            P("expert", None, "tensor"),
            P("expert", None, "tensor"),
            P("expert", "tensor", None),
            P("expert", None),
        ),
        out_specs=(
            P("expert", None),
            P("expert", None),
            P(),
            P(None, "tensor"),
            P(None, "tensor"),
            P(None, "tensor"),
            P("tensor", None),
            P(),
            P(),
            P(None, "tensor"),
            P(None, "tensor"),
            P("tensor", None),
            P("expert", None, "tensor"),
            P("expert", None, "tensor"),
            P("expert", "tensor", None),
        ),
        check_vma=False,
    )
```

```python
import functools

import jax
import jax.numpy as jnp
from jax import lax
from jax.experimental import pallas as pl
from jax.experimental.pallas import tpu as pltpu
from jax.sharding import PartitionSpec as P

HD = 64
EXPERTS = 16
CAP = 120


EPSILON = 1e-05
ROPE_BASE = 10000.0
MASKED = -1e30


def rms_scale(values):
    return lax.rsqrt(jnp.mean(values * values, axis=-1, keepdims=True) + EPSILON)


def matmul(left_side, right_side):
    return jnp.dot(left_side, right_side, preferred_element_type=jnp.float32)


def matmul_bt(left_side, right_side):
    return lax.dot_general(
        left_side, right_side, (((1,), (1,)), ((), ())), preferred_element_type=jnp.float32
    )


def matmul_at(left_side, right_side):
    return lax.dot_general(
        left_side, right_side, (((0,), (0,)), ((), ())), preferred_element_type=jnp.float32
    )


def silu_value(gate_in):
    return gate_in * jax.nn.sigmoid(gate_in)


def silu_slope(gate_in):
    sigma = jax.nn.sigmoid(gate_in)
    return sigma * (1.0 + gate_in * (1.0 - sigma))


def tie(*values):
    return lax.optimization_barrier(values)


def core_swap(values):
    return lax.ppermute(values, "tensor", [(i, i ^ 1) for i in range(4)])


def far_swap(values):
    return lax.ppermute(values, "tensor", [(i, i ^ 2) for i in range(4)])


def exchange(values):
    return lax.all_to_all(values, "expert", split_axis=0, concat_axis=0, tiled=True)


def in_order(bit, own, other, axis=0):
    return jnp.where(
        bit == 0,
        jnp.concatenate([own, other], axis=axis),
        jnp.concatenate([other, own], axis=axis),
    )


def gather_four(bit_low, bit_high, own, axis):
    far = far_swap(own)
    near = core_swap(own)
    far_near = core_swap(far)
    here = in_order(bit_low, own, near, axis)
    there = in_order(bit_low, far, far_near, axis)
    return in_order(bit_high, here, there, axis)


def select(onehot, values):
    return jnp.dot(onehot, values, preferred_element_type=jnp.float32).astype(jnp.bfloat16)


def pair_of_halves(kept, given, meanwhile=lambda pair: None):
    pair = (kept.astype(jnp.float32) + core_swap(given).astype(jnp.float32)).astype(jnp.bfloat16)
    far = far_swap(pair)
    meanwhile(pair)
    return pair.astype(jnp.float32) + far.astype(jnp.float32)


def after(values, *anchors):
    return lax.optimization_barrier((values, *anchors))[0]


def group_swap(values, step):
    size = lax.axis_size("expert")
    return lax.ppermute(values, "expert", [(i, i ^ (1 << step)) for i in range(size)])


class GroupSum:
    def __init__(self, values):
        self.steps = lax.axis_size("expert").bit_length() - 1
        self.me = lax.axis_index("expert")
        self.shape = values.shape
        self.part = values.astype(jnp.bfloat16).reshape(1 << self.steps, -1, values.shape[1])
        self.stage = 0
        self.split()

    def split(self):
        bit = (self.me >> self.stage) & 1
        pairs = self.part.reshape((-1, 2) + self.part.shape[1:])
        self.kept = lax.dynamic_index_in_dim(pairs, bit, 1, keepdims=False)
        self.given = lax.dynamic_index_in_dim(pairs, 1 - bit, 1, keepdims=False)

    def start(self, *anchors):
        if self.stage < self.steps:
            self.came = group_swap(after(self.given, *anchors), self.stage)
        else:
            step = 2 * self.steps - 1 - self.stage
            self.came = group_swap(after(self.part, *anchors), step)

    def end(self, *anchors):
        came = after(self.came, *anchors)
        if self.stage < self.steps:
            total = self.kept.astype(jnp.float32) + came.astype(jnp.float32)
            self.part = total.astype(jnp.bfloat16)
            self.stage += 1
            if self.stage < self.steps:
                self.split()
        else:
            bit = (self.me >> (2 * self.steps - 1 - self.stage)) & 1
            both = in_order(bit, self.part[:, None], came[:, None], 1)
            self.part = both.reshape((-1,) + self.part.shape[1:])
            self.stage += 1

    def advance(self, *anchors):
        self.end(*anchors)
        self.start()

    def finish(self, *anchors):
        while self.stage < 2 * self.steps:
            self.end(*anchors)
            if self.stage < 2 * self.steps:
                self.start()
        return self.part.reshape(self.shape)


def three_parts(values):
    high = lax.reduce_precision(values, 8, 7)
    rest = values - high
    middle = lax.reduce_precision(rest, 8, 7)
    return [part.astype(jnp.bfloat16) for part in (high, middle, rest - middle)]


def expert_kernel(
    half_slots,
    block,
    which_ref,
    rows_ref,
    cot_ref,
    gate_ref,
    up_ref,
    down_ref,
    back_ref,
    out_ref,
    mid_ref,
    d_gate_ref,
    d_up_ref,
):
    rows = rows_ref[...]
    count = rows.shape[0]
    gate_w, up_w, down_w = (gate_ref[0], up_ref[0], down_ref[0])
    gate_lin = matmul(rows, gate_w)
    up_lin = matmul(rows, up_w)
    raw = matmul_bt(cot_ref[...], down_w)
    sigma = 1.0 / (1.0 + jnp.exp(-gate_lin))
    act = gate_lin * sigma
    mid = act * up_lin
    scalar = jnp.sum(raw * mid, axis=1, keepdims=True)
    lanes = lax.broadcasted_iota(jnp.int32, (block, 128), 1)
    subs = lax.broadcasted_iota(jnp.int32, (block, 128), 0)
    diagonal = (lanes == subs) & (lanes < half_slots)
    last = 16
    at = half_slots - (block - last)
    sub_last = lax.broadcasted_iota(jnp.int32, (last, 128), 0)
    gates = []
    for b in range(count // block):
        tail = rows_ref[(b + 1) * block - last : (b + 1) * block, 0:384].astype(jnp.float32)
        total = tail[:, 0:128] + tail[:, 128:256] + tail[:, 256:384]
        line = jnp.sum(jnp.where(sub_last == at, total, 0.0), axis=0, keepdims=True)
        gates.append(jnp.sum(jnp.where(diagonal, line, 0.0), axis=1, keepdims=True))
    gate = jnp.concatenate(gates, axis=0) if len(gates) > 1 else gates[0]
    d_act = raw * gate
    d_up = (d_act * act).astype(jnp.bfloat16)
    d_gate = (d_act * up_lin * (sigma * (1.0 + gate_lin * (1.0 - sigma)))).astype(jnp.bfloat16)
    mid_g = (mid * gate).astype(jnp.bfloat16)
    mid_ref[...] = mid_g
    d_gate_ref[...] = d_gate
    d_up_ref[...] = d_up
    back = matmul_bt(d_gate, gate_w) + matmul_bt(d_up, up_w)
    back_ref[...] = back.astype(jnp.bfloat16)
    for b in range(count // block):
        part = jnp.where(diagonal, scalar[b * block : (b + 1) * block], 0.0)
        line = jnp.sum(part, axis=0, keepdims=True)
        high = line.astype(jnp.bfloat16).astype(jnp.float32)
        rest = line - high
        middle = rest.astype(jnp.bfloat16).astype(jnp.float32)
        for i, piece in enumerate((high, middle, rest - middle)):
            old = back[(b + 1) * block - last : (b + 1) * block, i * 128 : (i + 1) * 128]
            back_ref[(b + 1) * block - last : (b + 1) * block, i * 128 : (i + 1) * 128] = jnp.where(
                sub_last == at, piece, old
            ).astype(jnp.bfloat16)
    out_ref[...] = matmul(mid_g, down_w).astype(jnp.bfloat16)


def run_expert(which, rows, cots, gate_w, up_w, down_w, half_slots, block):
    count, feat = rows.shape
    hidden = gate_w.shape[2]
    step_rows = min(256, count)
    row_spec = pl.BlockSpec((step_rows, feat), lambda i, w: (i, 0))
    mid_spec = pl.BlockSpec((step_rows, hidden), lambda i, w: (i, 0))
    return pl.pallas_call(
        functools.partial(expert_kernel, half_slots, block),
        grid_spec=pltpu.PrefetchScalarGridSpec(
            num_scalar_prefetch=1,
            grid=(count // step_rows,),
            in_specs=[
                row_spec,
                row_spec,
                pl.BlockSpec((1, feat, hidden), lambda i, w: (w[0], 0, 0)),
                pl.BlockSpec((1, feat, hidden), lambda i, w: (w[0], 0, 0)),
                pl.BlockSpec((1, hidden, feat), lambda i, w: (w[0], 0, 0)),
            ],
            out_specs=[row_spec, row_spec, mid_spec, mid_spec, mid_spec],
        ),
        out_shape=[jax.ShapeDtypeStruct((count, feat), jnp.bfloat16)] * 2
        + [jax.ShapeDtypeStruct((count, hidden), jnp.bfloat16)] * 3,
        compiler_params=pltpu.CompilerParams(vmem_limit_bytes=50 << 20),
        cost_estimate=pl.CostEstimate(
            flops=12 * count * feat * hidden,
            bytes_accessed=8 * count * feat + 6 * feat * hidden + 6 * count * hidden,
            transcendentals=count * hidden,
        ),
        name="expert_rows",
    )(which, rows, cots, gate_w, up_w, down_w)


def weight_kernel(
    which_ref,
    rows_own,
    rows_other,
    cot_own,
    cot_other,
    mid_own,
    mid_other,
    dg_own,
    dg_other,
    du_own,
    du_other,
    g_gate_ref,
    g_up_ref,
    g_down_ref,
):
    def fill(rows, cots, mid, d_gate, d_up):
        turned = rows[...].T
        g_gate_ref[0] = matmul(turned, d_gate[...])
        g_up_ref[0] = matmul(turned, d_up[...])
        g_down_ref[0] = matmul_at(mid[...], cots[...])

    @pl.when(pl.program_id(0) == 0)
    def _():
        fill(rows_own, cot_own, mid_own, dg_own, du_own)

    @pl.when(pl.program_id(0) == 1)
    def _():
        fill(rows_other, cot_other, mid_other, dg_other, du_other)


def run_weights(bit_low, own, other):
    count, feat = own[0].shape
    hidden = own[2].shape[1]
    width = min(256, hidden)
    whole = pl.BlockSpec((count, feat), lambda s, j, w: (0, 0))
    first = pl.BlockSpec((count, width), lambda s, j, w: (0, jnp.where(s == 0, j, 0)))
    second = pl.BlockSpec((count, width), lambda s, j, w: (0, jnp.where(s == 1, j, 0)))

    def slab(s, w):
        return jnp.where(s == 0, w[0], 1 - w[0])

    wide = pl.BlockSpec((1, feat, width), lambda s, j, w: (slab(s, w), 0, j))
    tall = pl.BlockSpec((1, width, feat), lambda s, j, w: (slab(s, w), j, 0))
    return pl.pallas_call(
        weight_kernel,
        grid_spec=pltpu.PrefetchScalarGridSpec(
            num_scalar_prefetch=1,
            grid=(2, hidden // width),
            in_specs=[whole, whole, whole, whole, first, second, first, second, first, second],
            out_specs=[wide, wide, tall],
        ),
        out_shape=[
            jax.ShapeDtypeStruct((2, feat, hidden), jnp.float32),
            jax.ShapeDtypeStruct((2, feat, hidden), jnp.float32),
            jax.ShapeDtypeStruct((2, hidden, feat), jnp.float32),
        ],
        compiler_params=pltpu.CompilerParams(vmem_limit_bytes=56 << 20),
        cost_estimate=pl.CostEstimate(
            flops=12 * count * feat * hidden,
            bytes_accessed=8 * count * feat + 12 * count * hidden + 24 * feat * hidden,
            transcendentals=0,
        ),
        name="expert_weights",
    )(
        bit_low.reshape(1),
        own[0],
        other[0],
        own[1],
        other[1],
        own[2],
        other[2],
        own[3],
        other[3],
        own[4],
        other[4],
    )


def swap_halves(values):
    lanes = lax.broadcasted_iota(jnp.int32, values.shape, 1)
    return jnp.where(lanes % HD < HD // 2, pltpu.roll(values, 96, 1), pltpu.roll(values, 32, 1))


def fill_bias(bias_ref, start_ref):
    rows = bias_ref.shape[0]
    row_at = lax.broadcasted_iota(jnp.int32, (rows, 128), 0)
    lane_at = lax.broadcasted_iota(jnp.int32, (rows, 128), 1)
    start = start_ref[...]
    for part in range(rows // 128):
        key_at = lane_at + part * 128
        allowed = (key_at >= start) & (key_at <= row_at)
        bias_ref[:, part * 128 : part * 128 + 128] = jnp.where(allowed, 0.0, MASKED)


def fixed(shape):
    return pl.BlockSpec(shape, lambda *_: tuple(0 for _ in shape))


def pad_rows(piece, rows):
    return jnp.concatenate([piece, jnp.zeros((rows - piece.shape[0], piece.shape[1]), piece.dtype)], 0)


def heads_of(piece_rows, pair):
    return min(2, (piece_rows - pair * 128) // HD)


def attend_piece(hidden, weights, cos, sin, bias_ref, outs):
    q_ref, k_ref, v_ref, mixed_ref, lse_ref = outs
    rows = hidden.shape[0]
    width = q_ref.shape[1]
    span = 256
    lane_ids = lax.broadcasted_iota(jnp.int32, (rows, 128), 1)
    lse_ref[...] = jnp.zeros_like(lse_ref)
    linear = matmul_bt(
        hidden, jnp.concatenate([pad_rows(weight[...], width) for weight in weights], axis=0)
    )
    for pair in range(width // 128):
        at = slice(pair * 128, pair * 128 + 128)
        q_lin = linear[:, pair * 128 : pair * 128 + 128]
        k_lin = linear[:, width + pair * 128 : width + pair * 128 + 128]
        v_pair = linear[:, 2 * width + pair * 128 : 2 * width + pair * 128 + 128]
        v_pair = v_pair.astype(jnp.bfloat16)
        q_pair = (q_lin * cos + swap_halves(q_lin) * sin).astype(jnp.bfloat16)
        k_pair = (k_lin * cos + swap_halves(k_lin) * sin).astype(jnp.bfloat16)
        q_ref[:, at] = q_pair
        k_ref[:, at] = k_pair
        v_ref[:, at] = v_pair
        q_scaled = q_pair * jnp.bfloat16(HD ** (-0.5))
        zero = jnp.zeros_like(q_scaled)
        q_heads = [jnp.where(lane_ids < HD, q_scaled, zero), jnp.where(lane_ids < HD, zero, q_scaled)]
        q_heads = q_heads[: heads_of(weights[0].shape[0], pair)]
        for start in range(0, rows, span):
            end = start + span
            ids = lane_ids[start:end]
            mixed = None
            for head, q_head in enumerate(q_heads):
                scores = matmul_bt(q_head[start:end], k_pair[:end]) + bias_ref[start:end, :end]
                top = jnp.max(scores, axis=-1, keepdims=True)
                raised = jnp.exp(scores - top)
                total = jnp.sum(raised, axis=-1, keepdims=True)
                out = matmul(raised.astype(jnp.bfloat16), v_pair[:end]) / total
                mixed = out if mixed is None else jnp.where(ids < HD, mixed, out)
                lse = top + jnp.log(total)
                lse_ref[start:end, :] = jnp.where(
                    ids == pair * 2 + head, lse, lse_ref[start:end, :]
                )
            mixed_ref[start:end, at] = mixed.astype(jnp.bfloat16)


def attention_near_kernel(
    own_ref,
    other_ref,
    place_own_ref,
    place_other_ref,
    gain_ref,
    wq_ref,
    wk_ref,
    wv_ref,
    cos_ref,
    sin_ref,
    start_ref,
    grouped_ref,
    hidden_ref,
    q_ref,
    k_ref,
    v_ref,
    mixed_ref,
    lse_ref,
    bias_ref,
):
    fill_bias(bias_ref, start_ref)
    placed = matmul(place_own_ref[...], own_ref[...])
    placed = placed + matmul(place_other_ref[...], other_ref[...])
    grouped_ref[...] = placed.astype(jnp.bfloat16)
    hidden_ref[...] = (placed * rms_scale(placed) * gain_ref[...]).astype(jnp.bfloat16)
    attend_piece(
        hidden_ref[...],
        (wq_ref, wk_ref, wv_ref),
        cos_ref[...],
        sin_ref[...],
        bias_ref,
        (q_ref, k_ref, v_ref, mixed_ref, lse_ref),
    )


def attention_far_kernel(
    hidden_ref,
    wq_ref,
    wk_ref,
    wv_ref,
    cos_ref,
    sin_ref,
    start_ref,
    q_ref,
    k_ref,
    v_ref,
    mixed_ref,
    lse_ref,
    bias_ref,
):
    fill_bias(bias_ref, start_ref)
    attend_piece(
        hidden_ref[...],
        (wq_ref, wk_ref, wv_ref),
        cos_ref[...],
        sin_ref[...],
        bias_ref,
        (q_ref, k_ref, v_ref, mixed_ref, lse_ref),
    )


def call_whole(kernel, name, ins, outs, scratch, flops, transcendentals=0, prefetch=()):
    moved = sum(array.size * array.dtype.itemsize for array in (*ins, *outs))
    return pl.pallas_call(
        kernel,
        grid_spec=pltpu.PrefetchScalarGridSpec(
            num_scalar_prefetch=len(prefetch),
            grid=(1,),
            in_specs=[fixed(array.shape) for array in ins],
            out_specs=[fixed(out.shape) for out in outs],
            scratch_shapes=scratch,
        ),
        out_shape=list(outs),
        compiler_params=pltpu.CompilerParams(vmem_limit_bytes=56 << 20),
        cost_estimate=pl.CostEstimate(
            flops=flops, bytes_accessed=moved, transcendentals=transcendentals
        ),
        name=name,
    )(*prefetch, *ins)


def padded(piece_rows):
    return -(-piece_rows // 128) * 128


def run_attention(near, ins):
    rows = ins[-1].shape[0]
    feat = ins[0].shape[1]
    piece = ins[-4].shape[0]
    width = padded(piece)
    outs = [jax.ShapeDtypeStruct((rows, feat), jnp.bfloat16)] * (2 if near else 0)
    outs = outs + [jax.ShapeDtypeStruct((rows, width), jnp.bfloat16)] * 4
    outs = outs + [jax.ShapeDtypeStruct((rows, 128), jnp.float32)]
    return call_whole(
        attention_near_kernel if near else attention_far_kernel,
        "attention_near" if near else "attention_far",
        ins,
        outs,
        [pltpu.VMEM((rows, rows), jnp.float32)],
        6 * rows * feat * width + 4 * rows * rows * width + (2 * rows * rows * feat if near else 0),
        rows * rows * piece // HD,
    )


def middle_kernel(
    half_slots,
    block,
    turn_ref,
    m0_ref,
    m1_ref,
    m2_ref,
    m3_ref,
    grouped_ref,
    o0_ref,
    o1_ref,
    o2_ref,
    o3_ref,
    gain_ref,
    router_ref,
    slots_ref,
    one_ref,
    two_ref,
    first_ref,
    second_ref,
    resid_ref,
    hidden_ref,
    sent_ref,
    weight_ref,
    mixed_ref,
    whole_ref,
):
    mixed = (m0_ref, m1_ref, m2_ref, m3_ref)
    parts = (o0_ref, o1_ref, o2_ref, o3_ref)
    width = m0_ref.shape[1]
    for turn in range(4):

        @pl.when(turn_ref[0] == turn)
        def _():
            for i in range(4):
                mixed_ref[:, i * width : (i + 1) * width] = mixed[i ^ turn][...]
                whole_ref[i * width : (i + 1) * width, :] = pad_rows(parts[i ^ turn][...], width)

    resid = grouped_ref[...].astype(jnp.float32) + matmul(mixed_ref[...], whole_ref[...])
    resid_ref[...] = resid
    hidden = (resid * rms_scale(resid) * gain_ref[...]).astype(jnp.bfloat16)
    hidden_ref[...] = hidden
    logits = matmul_bt(router_ref[...], hidden)
    chosen_one = jnp.sum(one_ref[...] * logits, axis=0, keepdims=True)
    chosen_two = jnp.sum(two_ref[...] * logits, axis=0, keepdims=True)
    top = jnp.maximum(chosen_one, chosen_two)
    raised_one = jnp.exp(chosen_one - top)
    raised_two = jnp.exp(chosen_two - top)
    weight_one = raised_one / (raised_one + raised_two)
    weight_two = raised_two / (raised_one + raised_two)
    weight_ref[0:1, :] = weight_one
    weight_ref[1:2, :] = weight_two
    gate_of = first_ref[...] * weight_one + second_ref[...] * weight_two
    high = gate_of.astype(jnp.bfloat16).astype(jnp.float32)
    rest = gate_of - high
    middle = rest.astype(jnp.bfloat16).astype(jnp.float32)
    three = jnp.concatenate([high, middle, rest - middle], axis=0).astype(jnp.bfloat16)
    lines = matmul_bt(three, slots_ref[...])
    dests = first_ref.shape[0]
    last = 16
    at = half_slots - (block - last)
    sub_last = lax.broadcasted_iota(jnp.int32, (last, block), 0)
    chunk = 256
    for base in range(0, slots_ref.shape[0], chunk):
        rows = matmul(slots_ref[base : base + chunk, :], hidden)
        sent_ref[base : base + chunk, :] = rows.astype(jnp.bfloat16)
        for inner in range(block, chunk + 1, block):
            dest = (base + inner) // block - 1
            for i in range(3):
                line = lines[i * dests + dest : i * dests + dest + 1, dest * block : (dest + 1) * block]
                old = rows[inner - last : inner, i * 128 : i * 128 + block]
                sent_ref[base + inner - last : base + inner, i * 128 : i * 128 + block] = jnp.where(
                    sub_last == at, line, old
                ).astype(jnp.bfloat16)


def run_middle(half_slots, block, turn, *ins):
    rows, width = ins[0].shape
    feat = ins[4].shape[1]
    slots = ins[11]
    outs = [
        jax.ShapeDtypeStruct((rows, feat), jnp.float32),
        jax.ShapeDtypeStruct((rows, feat), jnp.bfloat16),
        jax.ShapeDtypeStruct((slots.shape[0], feat), jnp.bfloat16),
        jax.ShapeDtypeStruct((8, rows), jnp.float32),
    ]
    return call_whole(
        functools.partial(middle_kernel, half_slots, block),
        "middle",
        ins,
        outs,
        [pltpu.VMEM((rows, 4 * width), jnp.bfloat16), pltpu.VMEM((4 * width, feat), jnp.bfloat16)],
        2 * rows * feat * (4 * width + slots.shape[0]),
        4 * rows,
        (turn,),
    )


def piece_gradients(d_proj, w_out, q_ref, k_ref, v_ref, lse_ref, bias_ref, cos, sin, all_ref):
    rows, width = q_ref.shape
    span = 256
    scale = HD ** (-0.5)
    lane_ids = lax.broadcasted_iota(jnp.int32, (rows, 128), 1)
    d_all = matmul_bt(d_proj, pad_rows(w_out, width)).astype(jnp.bfloat16)
    blocks = rows // span

    def unturn(values):
        return (values * cos - swap_halves(values) * sin).astype(jnp.bfloat16)

    for pair in range(width // 128):
        at = slice(pair * 128, pair * 128 + 128)
        k = k_ref[:, at]
        v = v_ref[:, at]
        q_scaled = q_ref[:, at] * jnp.bfloat16(scale)
        d_mixed = d_all[:, at]
        zero = jnp.zeros_like(q_scaled)
        d_q = [jnp.zeros((span, 128), jnp.float32) for _ in range(blocks)]
        d_k = [jnp.zeros((span, 128), jnp.float32) for _ in range(blocks)]
        d_v = [jnp.zeros((span, 128), jnp.float32) for _ in range(blocks)]
        for head in range(heads_of(w_out.shape[0], pair)):
            mask = (lane_ids < HD) if head == 0 else (lane_ids >= HD)
            q_head = jnp.where(mask, q_scaled, zero)
            k_head = jnp.where(mask, k, zero)
            d_head = jnp.where(mask, d_mixed, zero)
            which = pair * 2 + head
            for block in range(blocks):
                start, end = block * span, block * span + span
                lse = jnp.sum(
                    jnp.where(lane_ids[start:end] == which, lse_ref[start:end, :], 0.0),
                    axis=-1,
                    keepdims=True,
                )
                scores = matmul_bt(q_head[start:end], k[:end]) + bias_ref[start:end, :end]
                probs = jnp.exp(scores - lse)
                d_probs = matmul_bt(d_head[start:end], v[:end])
                inner = jnp.sum(probs * d_probs, axis=-1, keepdims=True)
                d_scores = (probs * (d_probs - inner)).astype(jnp.bfloat16)
                probs = probs.astype(jnp.bfloat16)
                d_q[block] = d_q[block] + matmul(d_scores, k_head[:end])
                key_term = matmul_at(d_scores, q_head[start:end])
                value_term = matmul_at(probs, d_head[start:end])
                for other in range(block + 1):
                    part = slice(other * span, other * span + span)
                    d_k[other] = d_k[other] + key_term[part]
                    d_v[other] = d_v[other] + value_term[part]
        at_k = slice(width + pair * 128, width + pair * 128 + 128)
        at_v = slice(2 * width + pair * 128, 2 * width + pair * 128 + 128)
        all_ref[:, at] = unturn(jnp.concatenate(d_q, axis=0) * scale)
        all_ref[:, at_k] = unturn(jnp.concatenate(d_k, axis=0))
        all_ref[:, at_v] = jnp.concatenate(d_v, axis=0).astype(jnp.bfloat16)


def back_near_kernel(
    turn_ref,
    dh_own_ref,
    dh_other_ref,
    dg_ref,
    weight_ref,
    one_ref,
    two_ref,
    router_ref,
    resid_ref,
    hidden_two_ref,
    cot_ref,
    gain_ref,
    hidden_ref,
    mixed_ref,
    start_ref,
    cos_ref,
    sin_ref,
    lse_ref,
    w_out_ref,
    q_ref,
    k_ref,
    v_ref,
    wq_ref,
    wk_ref,
    wv_ref,
    d_resid_ref,
    d_proj_ref,
    g_ffn_ref,
    g_router_ref,
    late_ref,
    term_ref,
    bias_ref,
    all_ref,
    dh_ref,
):
    half = dh_own_ref.shape[0]

    @pl.when(turn_ref[0] % 2 == 0)
    def _():
        dh_ref[:half, :] = dh_own_ref[...]
        dh_ref[half:, :] = dh_other_ref[...]

    @pl.when(turn_ref[0] % 2 == 1)
    def _():
        dh_ref[:half, :] = dh_other_ref[...]
        dh_ref[half:, :] = dh_own_ref[...]

    fill_bias(bias_ref, start_ref)
    weight_one, weight_two = (weight_ref[0:1, :], weight_ref[1:2, :])
    d_one, d_two = (dg_ref[0:1, :], dg_ref[1:2, :])
    inner = weight_one * d_one + weight_two * d_two
    d_logits = one_ref[...] * (weight_one * (d_one - inner))
    d_logits = d_logits + two_ref[...] * (weight_two * (d_two - inner))
    d_logits = d_logits.astype(jnp.bfloat16)
    g_router_ref[...] = matmul(d_logits, hidden_two_ref[...])
    d_rows = dh_ref[...].astype(jnp.float32) + matmul_at(d_logits, router_ref[...])
    resid = resid_ref[...]
    scale = rms_scale(resid)
    normed = resid * scale
    g_ffn_ref[...] = jnp.sum(d_rows * normed, axis=0, keepdims=True)
    grown = d_rows * gain_ref[...]
    shift = jnp.mean(grown * normed, axis=-1, keepdims=True)
    d_resid = cot_ref[...].astype(jnp.float32) + scale * (grown - normed * shift)
    d_resid_ref[...] = d_resid
    d_proj_ref[...] = d_resid.astype(jnp.bfloat16)
    piece_gradients(
        d_proj_ref[...],
        w_out_ref[...],
        q_ref,
        k_ref,
        v_ref,
        lse_ref,
        bias_ref,
        cos_ref[...],
        sin_ref[...],
        all_ref,
    )
    piece, width = (w_out_ref.shape[0], q_ref.shape[1])
    grads = matmul_at(all_ref[...], hidden_ref[...]).astype(jnp.bfloat16)
    for i in range(3):
        late_ref[i * piece : (i + 1) * piece, :] = grads[i * width : i * width + piece, :]
    g_out = matmul_at(mixed_ref[...], d_proj_ref[...]).astype(jnp.bfloat16)
    late_ref[3 * piece : 4 * piece, :] = g_out[:piece, :]
    whole = jnp.concatenate([pad_rows(w[...], width) for w in (wq_ref, wk_ref, wv_ref)], axis=0)
    term_ref[...] = matmul(all_ref[...], whole)


def run_back_near(turn, *ins):
    rows, feat = ins[7].shape
    piece = ins[17].shape[0]
    width = padded(piece)
    outs = [
        jax.ShapeDtypeStruct((rows, feat), jnp.float32),
        jax.ShapeDtypeStruct((rows, feat), jnp.bfloat16),
        jax.ShapeDtypeStruct((1, feat), jnp.float32),
        jax.ShapeDtypeStruct((EXPERTS, feat), jnp.float32),
        jax.ShapeDtypeStruct((4 * piece, feat), jnp.bfloat16),
        jax.ShapeDtypeStruct((rows, feat), jnp.float32),
    ]
    return call_whole(
        back_near_kernel,
        "back_near",
        ins,
        outs,
        [
            pltpu.VMEM((rows, rows), jnp.float32),
            pltpu.VMEM((rows, 3 * width), jnp.bfloat16),
            pltpu.VMEM((rows, feat), jnp.bfloat16),
        ],
        rows * width * (16 * feat + 10 * rows),
        rows * rows * piece // HD,
        (turn,),
    )


def back_far_kernel(
    d_proj_ref,
    start_ref,
    cos_ref,
    sin_ref,
    lse_ref,
    w_out_ref,
    q_ref,
    k_ref,
    v_ref,
    all_ref,
    bias_ref,
):
    fill_bias(bias_ref, start_ref)
    piece_gradients(
        d_proj_ref[...],
        w_out_ref[...],
        q_ref,
        k_ref,
        v_ref,
        lse_ref,
        bias_ref,
        cos_ref[...],
        sin_ref[...],
        all_ref,
    )


def run_back_far(*ins):
    rows, feat = ins[0].shape
    piece = ins[5].shape[0]
    width = padded(piece)
    return call_whole(
        back_far_kernel,
        "back_far",
        ins,
        [jax.ShapeDtypeStruct((rows, 3 * width), jnp.bfloat16)],
        [pltpu.VMEM((rows, rows), jnp.float32)],
        rows * width * (2 * feat + 10 * rows),
        rows * rows * piece // HD,
    )[0]


def back_rows_kernel(
    all_ref,
    d_resid_ref,
    term_ref,
    place_own_ref,
    place_other_ref,
    wq_ref,
    wk_ref,
    wv_ref,
    give_ref,
    keep_ref,
    d_half_ref,
    sum_ref,
):
    width = all_ref.shape[1] // 3
    whole = jnp.concatenate([pad_rows(w[...], width) for w in (wq_ref, wk_ref, wv_ref)], axis=0)
    sum_ref[...] = matmul(all_ref[...], whole)
    total = (term_ref[...] + sum_ref[...]).astype(jnp.bfloat16)
    give_ref[...] = matmul_at(place_other_ref[...], total).astype(jnp.bfloat16)
    keep_ref[...] = matmul_at(place_own_ref[...], total).astype(jnp.bfloat16)
    d_resid = d_resid_ref[...]
    high = d_resid.astype(jnp.bfloat16)
    low = (d_resid - high.astype(jnp.float32)).astype(jnp.bfloat16)
    d_half_ref[...] = matmul_at(place_own_ref[...], high) + matmul_at(place_own_ref[...], low)


def run_back_rows(*ins):
    rows, width = ins[0].shape
    feat = ins[1].shape[1]
    half = ins[3].shape[1]
    outs = [
        jax.ShapeDtypeStruct((half, feat), jnp.bfloat16),
        jax.ShapeDtypeStruct((half, feat), jnp.bfloat16),
        jax.ShapeDtypeStruct((half, feat), jnp.float32),
    ]
    return call_whole(
        back_rows_kernel,
        "back_rows",
        ins,
        outs,
        [pltpu.VMEM((rows, feat), jnp.float32)],
        2 * rows * width * feat + 8 * rows * half * feat,
    )


def body(
    tokens,
    order,
    lengths,
    routes,
    attn_gain,
    w_query,
    w_key,
    w_value,
    w_out,
    ffn_gain,
    w_router,
    shared_gate,
    shared_up,
    shared_down,
    expert_gate,
    expert_up,
    expert_down,
    cotangent,
):
    row_count, feat_width = tokens.shape
    group_count = lax.axis_size("expert")
    share_rows = row_count // group_count
    half_share = share_rows // 2
    half_rows = row_count // 2
    my_group = lax.axis_index("expert")
    my_tensor = lax.axis_index("tensor")
    bit_low = lax.rem(my_tensor, 2)
    bit_high = my_tensor // 2
    slab_dev = expert_gate.shape[0]
    slab_total = slab_dev * group_count
    replicas = max(1, slab_total // EXPERTS)
    half_slots = slab_dev * CAP // 2
    row_ids = jnp.arange(row_count, dtype=jnp.int32)
    earlier = (row_ids[:, None] < row_ids[None, :]).astype(jnp.bfloat16)

    local_order = lax.dynamic_slice_in_dim(order, my_group * row_count, row_count, 0)
    groups = jnp.arange(group_count, dtype=jnp.int32)
    dest_group = local_order // row_count
    dest_onehot = (groups[:, None] == dest_group[None, :]).astype(jnp.bfloat16)
    dest_before = matmul(dest_onehot, earlier)
    send_rank = jnp.sum(dest_onehot.astype(jnp.float32) * dest_before, axis=0).astype(jnp.int32)
    send_half = send_rank // half_share
    send_slot = send_half * half_rows + dest_group * half_share + send_rank % half_share
    send_pick = send_slot[None, :] == (
        bit_low * half_rows + jnp.arange(half_rows, dtype=jnp.int32)[:, None]
    )
    send_pick = send_pick.astype(jnp.bfloat16)
    in_tokens = exchange(select(send_pick, tokens))
    cot_send, in_tokens = tie(select(send_pick, cotangent), in_tokens)
    in_cot = exchange(cot_send)

    near_weights = (w_query.T, w_key.T, w_value.T)
    far_weights = tuple(far_swap(weight) for weight in near_weights)
    out_far = far_swap(after(w_out, far_weights[1]))
    tokens_other = core_swap(in_tokens)
    turn = my_tensor.reshape(1)

    all_order = order.reshape(group_count, row_count)
    mine = all_order // row_count == my_group
    arrive_rank = matmul(mine.astype(jnp.bfloat16), earlier).astype(jnp.int32)
    arrive_rank = jnp.where(mine, arrive_rank, -1)
    landing = all_order - my_group * row_count
    target = jnp.sum(
        jnp.where(
            arrive_rank[:, None, :] == jnp.arange(share_rows, dtype=jnp.int32)[None, :, None],
            landing[:, None, :],
            0,
        ),
        axis=-1,
    )
    target = target.reshape(group_count, 2, half_share).transpose(1, 0, 2).reshape(2, half_rows)
    target_own = lax.dynamic_index_in_dim(target, bit_low, 0, keepdims=False)
    target_other = lax.dynamic_index_in_dim(target, 1 - bit_low, 0, keepdims=False)
    place_own = (row_ids[:, None] == target_own[None, :]).astype(jnp.bfloat16)
    place_other = (row_ids[:, None] == target_other[None, :]).astype(jnp.bfloat16)

    expert_ids = jnp.arange(EXPERTS, dtype=jnp.int32)
    member_one = expert_ids[:, None] == routes[None, :, 0]
    member_two = expert_ids[:, None] == routes[None, :, 1]
    member = member_one | member_two
    slot_rank = matmul(member.astype(jnp.bfloat16), earlier).astype(jnp.int32)
    slot_rank = jnp.where(member, slot_rank, -1)

    block = (half_slots + 16) // 16 * 16
    ranks = jnp.repeat(slot_rank, replicas, axis=0).reshape(group_count, slab_dev, row_count)
    ranks = lax.dynamic_index_in_dim(ranks, bit_low * half_slots // CAP, 1, keepdims=False)
    slot_ids = jnp.arange(block, dtype=jnp.int32)
    slots = bit_low * half_slots % CAP + slot_ids
    slots = jnp.where(slot_ids < half_slots, slots, -2)
    slots_cube = (ranks[:, None, :] == slots[None, :, None]).astype(jnp.bfloat16)
    slots_one = slots_cube.reshape(group_count * block, row_count)

    quarter = block // 2
    slots_part = lax.dynamic_slice_in_dim(slots_cube, bit_high * quarter, quarter, 1)
    slots_part = slots_part.reshape(-1, row_count)
    cot_pick_own = select(slots_part, place_own)
    cot_pick_other = select(slots_part, place_other)

    seq_lengths = lengths[0]
    seq_ends = jnp.cumsum(seq_lengths)
    passed = row_ids[:, None] >= seq_ends[None, :]
    sequence_segment = jnp.sum(passed.astype(jnp.int32), axis=1)
    position = row_ids - jnp.sum(jnp.where(passed, seq_lengths[None, :], 0), axis=1)
    half_size = HD // 2
    lanes = jnp.arange(128, dtype=jnp.int32)
    frequency = ROPE_BASE ** (-(lanes % half_size).astype(jnp.float32) / half_size)
    angles = position.astype(jnp.float32)[:, None] * frequency[None, :]
    cos_table = jnp.cos(angles)
    sin_table = jnp.where(lanes % HD < half_size, -1.0, 1.0) * jnp.sin(angles)
    seq_start = jnp.broadcast_to((row_ids - position)[:, None], (row_count, 128))
    gain_one = attn_gain.astype(jnp.float32)[None, :]
    gain_two = ffn_gain.astype(jnp.float32)[None, :]
    tables = (cos_table, sin_table, seq_start)
    grouped, hidden_one, *near_heads, near_mixed, near_lse = run_attention(
        True,
        (in_tokens, tokens_other, place_own, place_other, gain_one, *near_weights, *tables),
    )
    near_swapped = core_swap(near_mixed)
    far_weights = after(far_weights, near_mixed)
    *far_heads, far_mixed, far_lse = run_attention(False, (hidden_one, *far_weights, *tables))
    far_swapped = core_swap(far_mixed)
    out_pieces = (w_out, core_swap(w_out), out_far, core_swap(out_far))
    in_cot = after(in_cot, far_mixed)
    cot_half = core_swap(in_cot)
    cot_part = matmul(cot_pick_own, in_cot) + matmul(cot_pick_other, cot_half)
    cot_part = cot_part.astype(jnp.bfloat16)
    far_swapped = after(far_swapped, cot_part)
    cot_part = exchange(cot_part)

    dest_slab = jnp.arange(group_count, dtype=jnp.int32) * slab_dev + bit_low * half_slots // CAP
    dest_expert = dest_slab // replicas
    first_here = (routes[None, :, 0] == dest_expert[:, None]).astype(jnp.float32)
    second_here = (routes[None, :, 1] == dest_expert[:, None]).astype(jnp.float32)
    one_of = member_one.astype(jnp.float32)
    two_of = member_two.astype(jnp.float32)
    router_rows = w_router.T
    resid_two, hidden_two, sent, gate_weights = run_middle(
        half_slots,
        block,
        turn,
        near_mixed,
        near_swapped,
        far_mixed,
        far_swapped,
        grouped,
        *out_pieces,
        gain_two,
        router_rows,
        slots_one,
        one_of,
        two_of,
        first_here,
        second_here,
    )
    hidden_rows = exchange(after(sent, cot_part))
    cot_part = cot_part.reshape(group_count, quarter, feat_width)
    cot_own = in_order(bit_high, cot_part, far_swap(cot_part), 1).reshape(-1, feat_width)
    cot_other = core_swap(cot_own)
    grouped_cot = matmul(place_own, after(in_cot, sent)) + matmul(place_other, cot_half)
    grouped_cot = grouped_cot.astype(jnp.bfloat16)
    hidden_late = hidden_two

    gate_shared = matmul(hidden_late, shared_gate)
    up_shared = matmul(hidden_late, shared_up)
    act_shared = silu_value(gate_shared)
    shared_mid = (act_shared * up_shared).astype(jnp.bfloat16)
    shared_out = matmul(shared_mid, shared_down)
    d_mid_shared = matmul_bt(grouped_cot, shared_down)
    d_up_shared = (d_mid_shared * act_shared).astype(jnp.bfloat16)
    d_gate_shared = (d_mid_shared * up_shared * silu_slope(gate_shared)).astype(jnp.bfloat16)
    d_hidden_shared = matmul_bt(d_gate_shared, shared_gate) + matmul_bt(d_up_shared, shared_up)
    d_both = jnp.concatenate([d_gate_shared, d_up_shared], axis=1)
    early = GroupSum(
        jnp.concatenate([matmul_at(d_both, hidden_late), matmul_at(shared_mid, grouped_cot)], axis=0)
    )
    shared_send = shared_out.astype(jnp.bfloat16)
    shared_own = matmul_at(place_own, shared_send)
    shared_other = matmul_at(place_other, shared_send)
    resid_high, resid_low = three_parts(resid_two)[:2]
    resid_half = matmul_at(place_own, resid_high) + matmul_at(place_own, resid_low)
    hidden_rows = after(hidden_rows, early.given, shared_own, shared_other, resid_half)
    early.start()

    rows_other = core_swap(hidden_rows)
    which_own = (bit_low * half_slots // CAP).reshape(1)
    which_other = ((1 - bit_low) * half_slots // CAP).reshape(1)
    weights_here = (expert_gate, expert_up, expert_down, half_slots, block)
    back_kept, out_kept, mid_own, dg_own, du_own = run_expert(
        which_own, hidden_rows, cot_own, *weights_here
    )
    back_given, out_given, mid_other, dg_other, du_other = run_expert(
        which_other, rows_other, cot_other, *weights_here
    )
    early.advance(back_given)
    stack_own = (hidden_rows, cot_own, mid_own, dg_own, du_own)
    stack_other = (rows_other, cot_other, mid_other, dg_other, du_other)

    def pair_sum(kept, given):
        return kept.astype(jnp.float32) + core_swap(given).astype(jnp.float32)

    back_sum = pair_sum(back_kept, back_given).reshape(group_count, block, feat_width)
    lines = back_sum[:, half_slots, :384].reshape(group_count, 3, 128)
    lines = jnp.stack(three_parts(jnp.sum(lines, axis=1)), axis=1).astype(jnp.float32)
    lines = jnp.pad(lines.reshape(group_count, 1, 384), ((0, 0), (0, 0), (0, feat_width - 384)))
    back_sum = jnp.where(slot_ids[None, :, None] == half_slots, lines, back_sum)
    back_send = back_sum.astype(jnp.bfloat16).reshape(-1, feat_width)
    back_own = exchange(back_send)
    early.end(back_send)
    out_sum = pair_sum(out_kept, after(out_given, back_send)).astype(jnp.bfloat16)
    out_sum = out_sum.reshape(group_count, block, feat_width)
    out_kept = lax.dynamic_slice_in_dim(out_sum, bit_high * quarter, quarter, 1)
    out_given = lax.dynamic_slice_in_dim(out_sum, (1 - bit_high) * quarter, quarter, 1)
    out_send = out_kept.astype(jnp.float32) + far_swap(out_given).astype(jnp.float32)
    out_send = out_send.astype(jnp.bfloat16).reshape(-1, feat_width)
    if slab_dev == 2:
        own_late = after(stack_own[0], out_given)
        stack_own = (own_late,) + stack_own[1:]
        g_expert_gate, g_expert_up, g_expert_down = run_weights(bit_low, stack_own, stack_other)
    else:
        wide = [jnp.concatenate(pair, axis=0) for pair in zip(stack_own, stack_other)]
        g_expert_gate = matmul_at(wide[0], wide[3])[None]
        g_expert_up = matmul_at(wide[0], wide[4])[None]
        g_expert_down = matmul_at(wide[2], wide[1])[None]


    back_own = after(back_own, g_expert_gate, out_send)
    d_hidden_part = (matmul_at(slots_one, back_own) + d_hidden_shared).astype(jnp.bfloat16)
    out_own = exchange(after(out_send, d_hidden_part))
    early.start(d_hidden_part)
    kept = lax.dynamic_slice_in_dim(d_hidden_part, bit_low * half_rows, half_rows, 0)
    given = lax.dynamic_slice_in_dim(d_hidden_part, (1 - bit_low) * half_rows, half_rows, 0)
    d_hidden_half = pair_of_halves(kept, given).astype(jnp.bfloat16)
    d_hidden_other = core_swap(d_hidden_half)
    dg_lines = back_own.reshape(group_count, block, feat_width)[:, half_slots, :384]
    dg_lines = dg_lines.reshape(group_count, 3, 128)[:, :, :block]
    dg_of = jnp.einsum("dps,dsr->dpr", dg_lines, slots_cube, preferred_element_type=jnp.float32)
    dg_of = jnp.sum(dg_of, axis=1)
    dg_part = jnp.stack(
        [jnp.sum(first_here * dg_of, axis=0), jnp.sum(second_here * dg_of, axis=0)], axis=0
    )
    dg_part = jnp.pad(dg_part, ((0, 6), (0, 0)))
    dg_part = dg_part + core_swap(dg_part)
    dg_part = dg_part + far_swap(dg_part)
    early.end(d_hidden_half, dg_part)
    early.start()

    d_resid, d_proj, g_ffn_gain, g_router, late, term = run_back_near(
        turn,
        d_hidden_half,
        d_hidden_other,
        dg_part,
        gate_weights,
        one_of,
        two_of,
        router_rows,
        resid_two,
        hidden_two,
        grouped_cot,
        gain_two,
        hidden_one,
        near_mixed,
        seq_start,
        cos_table,
        sin_table,
        near_lse,
        w_out,
        *near_heads,
        *near_weights,
    )
    late = GroupSum(late)
    late.start()
    early.advance(d_proj)
    ffn_rows = after(out_own, d_proj)
    ffn_given = (matmul_at(cot_pick_other, ffn_rows) + shared_other).astype(jnp.bfloat16)
    ffn_kept = (matmul_at(cot_pick_own, ffn_rows) + shared_own).astype(jnp.bfloat16)
    ffn_half = pair_of_halves(ffn_kept, ffn_given)
    output_send = (resid_half + ffn_half).astype(jnp.bfloat16)
    far_all = run_back_far(
        after(d_proj, ffn_given, ffn_kept),
        seq_start,
        cos_table,
        sin_table,
        far_lse,
        out_far,
        *far_heads,
    )
    late.advance(far_all)
    d_one_given, d_one_kept, d_resid_half = run_back_rows(
        after(far_all, output_send, late.part), d_resid, term, place_own, place_other, *far_weights
    )
    late.advance(d_one_given)
    early.advance(d_one_given)
    d_one = d_one_kept.astype(jnp.float32) + core_swap(d_one_given).astype(jnp.float32)
    resid = in_tokens.astype(jnp.float32)
    scale_one = rms_scale(resid)
    normed_one = resid * scale_one
    e_one = d_one * gain_one
    shift_one = jnp.mean(e_one * normed_one, axis=-1, keepdims=True)
    d_tokens_send = (d_resid_half + scale_one * (e_one - normed_one * shift_one)).astype(jnp.bfloat16)
    g_attn_gain = jnp.sum(d_one * normed_one, axis=0, keepdims=True)
    both_send = jnp.concatenate(
        [
            d_tokens_send.reshape(group_count, half_share, feat_width),
            output_send.reshape(group_count, half_share, feat_width),
        ],
        axis=1,
    )
    both_own = exchange(both_send)
    both_other = core_swap(both_own)

    unsend = (send_slot[:, None] == row_ids[None, :]).astype(jnp.bfloat16)

    def arrive_back(part):
        own = both_own[:, part].reshape(half_rows, feat_width)
        other = both_other[:, part].reshape(half_rows, feat_width)
        return select(unsend, in_order(bit_low, own, other))

    g_attn_gain = g_attn_gain + core_swap(g_attn_gain)
    small = jnp.concatenate([g_router, g_ffn_gain, g_attn_gain], axis=0)
    small = jnp.pad(small, ((0, -small.shape[0] % 8), (0, 0)))
    for step in range(group_count.bit_length() - 1):
        small = small + group_swap(small, step)
    g_router = small[:EXPERTS].T
    g_ffn_gain = small[EXPERTS]
    g_attn_gain = small[EXPERTS + 1]
    late = late.finish(both_send).astype(jnp.float32)
    shared = early.finish(both_send).astype(jnp.float32)
    hidden_s = shared_gate.shape[1]
    g_shared_gate = shared[:hidden_s].T
    g_shared_up = shared[hidden_s : 2 * hidden_s].T
    g_shared_down = shared[2 * hidden_s :]
    head_rows = w_out.shape[0]
    g_query = late[:head_rows].T
    g_key = late[head_rows : 2 * head_rows].T
    g_value = late[2 * head_rows : 3 * head_rows].T
    g_out = late[3 * head_rows :]
    d_tokens = arrive_back(slice(0, half_share))
    output = arrive_back(slice(half_share, 2 * half_share))
    return (
        output,
        d_tokens,
        g_attn_gain,
        g_query,
        g_key,
        g_value,
        g_out,
        g_ffn_gain,
        g_router,
        g_shared_gate,
        g_shared_up,
        g_shared_down,
        g_expert_gate,
        g_expert_up,
        g_expert_down,
    )


def solution(mesh):
    return jax.shard_map(
        body,
        mesh=mesh,
        in_specs=(
            P("expert", None),
            P(),
            P("expert", None),
            P("expert", None),
            P(),
            P(None, "tensor"),
            P(None, "tensor"),
            P(None, "tensor"),
            P("tensor", None),
            P(),
            P(),
            P(None, "tensor"),
            P(None, "tensor"),
            P("tensor", None),
            P("expert", None, "tensor"),
            P("expert", None, "tensor"),
            P("expert", "tensor", None),
            P("expert", None),
        ),
        out_specs=(
            P("expert", None),
            P("expert", None),
            P(),
            P(None, "tensor"),
            P(None, "tensor"),
            P(None, "tensor"),
            P("tensor", None),
            P(),
            P(),
            P(None, "tensor"),
            P(None, "tensor"),
            P("tensor", None),
            P("expert", None, "tensor"),
            P("expert", None, "tensor"),
            P("expert", "tensor", None),
        ),
        check_vma=False,
    )
```

```python
import functools

import jax
import jax.numpy as jnp
from jax import lax
from jax.experimental import pallas as pl
from jax.experimental.pallas import tpu as pltpu
from jax.sharding import PartitionSpec as P

HD = 64
EXPERTS = 16
CAP = 120


EPSILON = 1e-05
ROPE_BASE = 10000.0
MASKED = -1e30


def rms_scale(values):
    return lax.rsqrt(jnp.mean(values * values, axis=-1, keepdims=True) + EPSILON)


def matmul(left_side, right_side):
    return jnp.dot(left_side, right_side, preferred_element_type=jnp.float32)


def matmul_bt(left_side, right_side):
    return lax.dot_general(
        left_side, right_side, (((1,), (1,)), ((), ())), preferred_element_type=jnp.float32
    )


def matmul_at(left_side, right_side):
    return lax.dot_general(
        left_side, right_side, (((0,), (0,)), ((), ())), preferred_element_type=jnp.float32
    )


def silu_value(gate_in):
    return gate_in * jax.nn.sigmoid(gate_in)


def silu_slope(gate_in):
    sigma = jax.nn.sigmoid(gate_in)
    return sigma * (1.0 + gate_in * (1.0 - sigma))


def tie(*values):
    return lax.optimization_barrier(values)


def core_swap(values):
    return lax.ppermute(values, "tensor", [(i, i ^ 1) for i in range(4)])


def far_swap(values):
    return lax.ppermute(values, "tensor", [(i, i ^ 2) for i in range(4)])


def exchange(values):
    return lax.all_to_all(values, "expert", split_axis=0, concat_axis=0, tiled=True)


def in_order(bit, own, other, axis=0):
    return jnp.where(
        bit == 0,
        jnp.concatenate([own, other], axis=axis),
        jnp.concatenate([other, own], axis=axis),
    )


def gather_four(bit_low, bit_high, own, axis):
    far = far_swap(own)
    near = core_swap(own)
    far_near = core_swap(far)
    here = in_order(bit_low, own, near, axis)
    there = in_order(bit_low, far, far_near, axis)
    return in_order(bit_high, here, there, axis)


def select(onehot, values):
    return jnp.dot(onehot, values, preferred_element_type=jnp.float32).astype(jnp.bfloat16)


def pair_sum(kept, given):
    return (kept.astype(jnp.float32) + core_swap(given).astype(jnp.float32)).astype(jnp.bfloat16)


def after(values, *anchors):
    return lax.optimization_barrier((values, *anchors))[0]


def group_swap(values, step):
    size = lax.axis_size("expert")
    return lax.ppermute(values, "expert", [(i, i ^ (1 << step)) for i in range(size)])


class GroupSum:
    def __init__(self, values, whole_last=False):
        self.bits = lax.axis_size("expert").bit_length() - 1
        self.steps = list(range(self.bits)) + list(reversed(range(self.bits)))
        if whole_last:
            self.steps[self.bits - 1 : self.bits + 1] = [self.bits - 1]
        self.halvings = self.bits - 1 if whole_last else self.bits
        self.whole_last = whole_last
        self.me = lax.axis_index("expert")
        self.shape = values.shape
        pieces = 1 << self.halvings
        self.part = values.astype(jnp.bfloat16).reshape(pieces, -1, values.shape[1])
        self.stage = 0
        self.pending = False
        self.prepare()

    def prepare(self):
        if self.stage < self.halvings:
            bit = (self.me >> self.stage) & 1
            pairs = self.part.reshape((-1, 2) + self.part.shape[1:])
            self.kept = lax.dynamic_index_in_dim(pairs, bit, 1, keepdims=False)
            self.given = lax.dynamic_index_in_dim(pairs, 1 - bit, 1, keepdims=False)
        else:
            self.kept = self.given = self.part

    def start_first(self, share):
        self.cut = self.given.shape[1] // share
        self.first = group_swap(self.given[:, : self.cut], self.steps[self.stage])

    def start_second(self, *anchors):
        self.first, second = tie(self.first, self.given[:, self.cut :], *anchors)[:2]
        self.second = group_swap(second, self.steps[self.stage])

    def end_second(self, *anchors):
        self.came = jnp.concatenate([self.first, after(self.second, *anchors)], axis=1)
        self.end()

    def done(self):
        return self.stage == len(self.steps)

    def start(self, *anchors):
        self.pending = True
        self.came = group_swap(after(self.given, *anchors), self.steps[self.stage])

    def end(self, *anchors):
        came = after(self.came, *anchors)
        self.pending = False
        if self.stage < self.bits:
            total = self.kept.astype(jnp.float32) + came.astype(jnp.float32)
            self.part = total.astype(jnp.bfloat16)
        else:
            bit = (self.me >> self.steps[self.stage]) & 1
            both = in_order(bit, self.part[:, None], came[:, None], 1)
            self.part = both.reshape((-1,) + self.part.shape[1:])
        self.stage += 1
        if not self.done():
            self.prepare()

    def finish(self, *anchors):
        while not self.done():
            if not self.pending:
                self.start()
            self.end(*anchors)
        return self.part.reshape(self.shape)


def three_parts(values):
    high = lax.reduce_precision(values, 8, 7)
    rest = values - high
    middle = lax.reduce_precision(rest, 8, 7)
    return [part.astype(jnp.bfloat16) for part in (high, middle, rest - middle)]


def expert_kernel(
    half_slots,
    block,
    which_ref,
    rows_ref,
    cot_ref,
    gate_ref,
    up_ref,
    down_ref,
    back_ref,
    out_ref,
    mid_ref,
    d_gate_ref,
    d_up_ref,
):
    rows = rows_ref[...]
    count = rows.shape[0]
    gate_w, up_w, down_w = (gate_ref[0], up_ref[0], down_ref[0])
    gate_lin = matmul(rows, gate_w)
    up_lin = matmul(rows, up_w)
    raw = matmul_bt(cot_ref[...], down_w)
    sigma = 1.0 / (1.0 + jnp.exp(-gate_lin))
    act = gate_lin * sigma
    mid = act * up_lin
    scalar = jnp.sum(raw * mid, axis=1, keepdims=True)
    lanes = lax.broadcasted_iota(jnp.int32, (block, 128), 1)
    subs = lax.broadcasted_iota(jnp.int32, (block, 128), 0)
    diagonal = (lanes == subs) & (lanes < half_slots)
    last = 16
    at = half_slots - (block - last)
    sub_last = lax.broadcasted_iota(jnp.int32, (last, 128), 0)
    gates = []
    for b in range(count // block):
        tail = rows_ref[(b + 1) * block - last : (b + 1) * block, 0:384].astype(jnp.float32)
        total = tail[:, 0:128] + tail[:, 128:256] + tail[:, 256:384]
        line = jnp.sum(jnp.where(sub_last == at, total, 0.0), axis=0, keepdims=True)
        gates.append(jnp.sum(jnp.where(diagonal, line, 0.0), axis=1, keepdims=True))
    gate = jnp.concatenate(gates, axis=0) if len(gates) > 1 else gates[0]
    d_act = raw * gate
    d_up = (d_act * act).astype(jnp.bfloat16)
    d_gate = (d_act * up_lin * (sigma * (1.0 + gate_lin * (1.0 - sigma)))).astype(jnp.bfloat16)
    mid_g = (mid * gate).astype(jnp.bfloat16)
    mid_ref[...] = mid_g
    d_gate_ref[...] = d_gate
    d_up_ref[...] = d_up
    back = matmul_bt(d_gate, gate_w) + matmul_bt(d_up, up_w)
    back_ref[...] = back.astype(jnp.bfloat16)
    for b in range(count // block):
        part = jnp.where(diagonal, scalar[b * block : (b + 1) * block], 0.0)
        line = jnp.sum(part, axis=0, keepdims=True)
        high = line.astype(jnp.bfloat16).astype(jnp.float32)
        rest = line - high
        middle = rest.astype(jnp.bfloat16).astype(jnp.float32)
        for i, piece in enumerate((high, middle, rest - middle)):
            old = back[(b + 1) * block - last : (b + 1) * block, i * 128 : (i + 1) * 128]
            back_ref[(b + 1) * block - last : (b + 1) * block, i * 128 : (i + 1) * 128] = jnp.where(
                sub_last == at, piece, old
            ).astype(jnp.bfloat16)
    out_ref[...] = matmul(mid_g, down_w).astype(jnp.bfloat16)


def run_expert(which, rows, cots, gate_w, up_w, down_w, half_slots, block):
    count, feat = rows.shape
    hidden = gate_w.shape[2]
    step_rows = min(256, count)
    row_spec = pl.BlockSpec((step_rows, feat), lambda i, w: (i, 0))
    mid_spec = pl.BlockSpec((step_rows, hidden), lambda i, w: (i, 0))
    return pl.pallas_call(
        functools.partial(expert_kernel, half_slots, block),
        grid_spec=pltpu.PrefetchScalarGridSpec(
            num_scalar_prefetch=1,
            grid=(count // step_rows,),
            in_specs=[
                row_spec,
                row_spec,
                pl.BlockSpec((1, feat, hidden), lambda i, w: (w[0], 0, 0)),
                pl.BlockSpec((1, feat, hidden), lambda i, w: (w[0], 0, 0)),
                pl.BlockSpec((1, hidden, feat), lambda i, w: (w[0], 0, 0)),
            ],
            out_specs=[row_spec, row_spec, mid_spec, mid_spec, mid_spec],
        ),
        out_shape=[jax.ShapeDtypeStruct((count, feat), jnp.bfloat16)] * 2
        + [jax.ShapeDtypeStruct((count, hidden), jnp.bfloat16)] * 3,
        compiler_params=pltpu.CompilerParams(vmem_limit_bytes=50 << 20),
        cost_estimate=pl.CostEstimate(
            flops=12 * count * feat * hidden,
            bytes_accessed=8 * count * feat + 6 * feat * hidden + 6 * count * hidden,
            transcendentals=count * hidden,
        ),
        name="expert_rows",
    )(which, rows, cots, gate_w, up_w, down_w)


def weight_kernel(
    which_ref,
    rows_own,
    rows_other,
    cot_own,
    cot_other,
    mid_own,
    mid_other,
    dg_own,
    dg_other,
    du_own,
    du_other,
    g_gate_ref,
    g_up_ref,
    g_down_ref,
):
    def fill(rows, cots, mid, d_gate, d_up):
        turned = rows[...].T
        g_gate_ref[0] = matmul(turned, d_gate[...])
        g_up_ref[0] = matmul(turned, d_up[...])
        g_down_ref[0] = matmul_at(mid[...], cots[...])

    @pl.when(pl.program_id(0) == 0)
    def _():
        fill(rows_own, cot_own, mid_own, dg_own, du_own)

    @pl.when(pl.program_id(0) == 1)
    def _():
        fill(rows_other, cot_other, mid_other, dg_other, du_other)


def run_weights(bit_low, own, other):
    count, feat = own[0].shape
    hidden = own[2].shape[1]
    width = min(256, hidden)
    whole = pl.BlockSpec((count, feat), lambda s, j, w: (0, 0))
    first = pl.BlockSpec((count, width), lambda s, j, w: (0, jnp.where(s == 0, j, 0)))
    second = pl.BlockSpec((count, width), lambda s, j, w: (0, jnp.where(s == 1, j, 0)))

    def slab(s, w):
        return jnp.where(s == 0, w[0], 1 - w[0])

    wide = pl.BlockSpec((1, feat, width), lambda s, j, w: (slab(s, w), 0, j))
    tall = pl.BlockSpec((1, width, feat), lambda s, j, w: (slab(s, w), j, 0))
    return pl.pallas_call(
        weight_kernel,
        grid_spec=pltpu.PrefetchScalarGridSpec(
            num_scalar_prefetch=1,
            grid=(2, hidden // width),
            in_specs=[whole, whole, whole, whole, first, second, first, second, first, second],
            out_specs=[wide, wide, tall],
        ),
        out_shape=[
            jax.ShapeDtypeStruct((2, feat, hidden), jnp.float32),
            jax.ShapeDtypeStruct((2, feat, hidden), jnp.float32),
            jax.ShapeDtypeStruct((2, hidden, feat), jnp.float32),
        ],
        compiler_params=pltpu.CompilerParams(vmem_limit_bytes=56 << 20),
        cost_estimate=pl.CostEstimate(
            flops=12 * count * feat * hidden,
            bytes_accessed=8 * count * feat + 12 * count * hidden + 24 * feat * hidden,
            transcendentals=0,
        ),
        name="expert_weights",
    )(
        bit_low.reshape(1),
        own[0],
        other[0],
        own[1],
        other[1],
        own[2],
        other[2],
        own[3],
        other[3],
        own[4],
        other[4],
    )


def swap_halves(values):
    lanes = lax.broadcasted_iota(jnp.int32, values.shape, 1)
    return jnp.where(lanes % HD < HD // 2, pltpu.roll(values, 96, 1), pltpu.roll(values, 32, 1))


def fill_bias(bias_ref, start_ref):
    rows = bias_ref.shape[0]
    row_at = lax.broadcasted_iota(jnp.int32, (rows, 128), 0)
    lane_at = lax.broadcasted_iota(jnp.int32, (rows, 128), 1)
    start = start_ref[...]
    for part in range(rows // 128):
        key_at = lane_at + part * 128
        allowed = (key_at >= start) & (key_at <= row_at)
        bias_ref[:, part * 128 : part * 128 + 128] = jnp.where(allowed, 0.0, MASKED)


def fixed(shape):
    return pl.BlockSpec(shape, lambda *_: tuple(0 for _ in shape))


def pad_rows(piece, rows):
    return jnp.concatenate([piece, jnp.zeros((rows - piece.shape[0], piece.shape[1]), piece.dtype)], 0)


def heads_of(piece_rows, pair):
    return min(2, (piece_rows - pair * 128) // HD)


def attend_piece(hidden, weights, cos, sin, bias_ref, outs):
    q_ref, k_ref, v_ref, mixed_ref, lse_ref = outs
    rows = hidden.shape[0]
    width = q_ref.shape[1]
    span = 256
    lane_ids = lax.broadcasted_iota(jnp.int32, (rows, 128), 1)
    lse_ref[...] = jnp.zeros_like(lse_ref)
    linear = matmul_bt(
        hidden, jnp.concatenate([pad_rows(weight[...], width) for weight in weights], axis=0)
    )
    for pair in range(width // 128):
        at = slice(pair * 128, pair * 128 + 128)
        q_lin = linear[:, pair * 128 : pair * 128 + 128]
        k_lin = linear[:, width + pair * 128 : width + pair * 128 + 128]
        v_pair = linear[:, 2 * width + pair * 128 : 2 * width + pair * 128 + 128]
        v_pair = v_pair.astype(jnp.bfloat16)
        q_pair = (q_lin * cos + swap_halves(q_lin) * sin).astype(jnp.bfloat16)
        k_pair = (k_lin * cos + swap_halves(k_lin) * sin).astype(jnp.bfloat16)
        q_ref[:, at] = q_pair
        k_ref[:, at] = k_pair
        v_ref[:, at] = v_pair
        q_scaled = q_pair * jnp.bfloat16(HD ** (-0.5))
        zero = jnp.zeros_like(q_scaled)
        q_heads = [jnp.where(lane_ids < HD, q_scaled, zero), jnp.where(lane_ids < HD, zero, q_scaled)]
        q_heads = q_heads[: heads_of(weights[0].shape[0], pair)]
        for start in range(0, rows, span):
            end = start + span
            ids = lane_ids[start:end]
            mixed = None
            for head, q_head in enumerate(q_heads):
                scores = matmul_bt(q_head[start:end], k_pair[:end]) + bias_ref[start:end, :end]
                top = jnp.max(scores, axis=-1, keepdims=True)
                raised = jnp.exp(scores - top)
                total = jnp.sum(raised, axis=-1, keepdims=True)
                out = matmul(raised.astype(jnp.bfloat16), v_pair[:end]) / total
                mixed = out if mixed is None else jnp.where(ids < HD, mixed, out)
                lse = top + jnp.log(total)
                lse_ref[start:end, :] = jnp.where(
                    ids == pair * 2 + head, lse, lse_ref[start:end, :]
                )
            mixed_ref[start:end, at] = mixed.astype(jnp.bfloat16)


def attention_near_kernel(
    own_ref,
    other_ref,
    place_own_ref,
    place_other_ref,
    gain_ref,
    wq_ref,
    wk_ref,
    wv_ref,
    cos_ref,
    sin_ref,
    start_ref,
    grouped_ref,
    hidden_ref,
    q_ref,
    k_ref,
    v_ref,
    mixed_ref,
    lse_ref,
    bias_ref,
):
    fill_bias(bias_ref, start_ref)
    placed = matmul(place_own_ref[...], own_ref[...])
    placed = placed + matmul(place_other_ref[...], other_ref[...])
    grouped_ref[...] = placed.astype(jnp.bfloat16)
    hidden_ref[...] = (placed * rms_scale(placed) * gain_ref[...]).astype(jnp.bfloat16)
    attend_piece(
        hidden_ref[...],
        (wq_ref, wk_ref, wv_ref),
        cos_ref[...],
        sin_ref[...],
        bias_ref,
        (q_ref, k_ref, v_ref, mixed_ref, lse_ref),
    )


def attention_far_kernel(
    hidden_ref,
    wq_ref,
    wk_ref,
    wv_ref,
    cos_ref,
    sin_ref,
    start_ref,
    q_ref,
    k_ref,
    v_ref,
    mixed_ref,
    lse_ref,
    bias_ref,
):
    fill_bias(bias_ref, start_ref)
    attend_piece(
        hidden_ref[...],
        (wq_ref, wk_ref, wv_ref),
        cos_ref[...],
        sin_ref[...],
        bias_ref,
        (q_ref, k_ref, v_ref, mixed_ref, lse_ref),
    )


def call_whole(kernel, name, ins, outs, scratch, flops, transcendentals=0, prefetch=()):
    moved = sum(array.size * array.dtype.itemsize for array in (*ins, *outs))
    return pl.pallas_call(
        kernel,
        grid_spec=pltpu.PrefetchScalarGridSpec(
            num_scalar_prefetch=len(prefetch),
            grid=(1,),
            in_specs=[fixed(array.shape) for array in ins],
            out_specs=[fixed(out.shape) for out in outs],
            scratch_shapes=scratch,
        ),
        out_shape=list(outs),
        compiler_params=pltpu.CompilerParams(vmem_limit_bytes=56 << 20),
        cost_estimate=pl.CostEstimate(
            flops=flops, bytes_accessed=moved, transcendentals=transcendentals
        ),
        name=name,
    )(*prefetch, *ins)


def padded(piece_rows):
    return -(-piece_rows // 128) * 128


def run_attention(near, ins):
    rows = ins[-1].shape[0]
    feat = ins[0].shape[1]
    piece = ins[-4].shape[0]
    width = padded(piece)
    outs = [jax.ShapeDtypeStruct((rows, feat), jnp.bfloat16)] * (2 if near else 0)
    outs = outs + [jax.ShapeDtypeStruct((rows, width), jnp.bfloat16)] * 4
    outs = outs + [jax.ShapeDtypeStruct((rows, 128), jnp.float32)]
    return call_whole(
        attention_near_kernel if near else attention_far_kernel,
        "attention_near" if near else "attention_far",
        ins,
        outs,
        [pltpu.VMEM((rows, rows), jnp.float32)],
        6 * rows * feat * width + 4 * rows * rows * width + (2 * rows * rows * feat if near else 0),
        rows * rows * piece // HD,
    )


def middle_kernel(
    half_slots,
    block,
    turn_ref,
    m0_ref,
    m1_ref,
    m2_ref,
    m3_ref,
    grouped_ref,
    o0_ref,
    o1_ref,
    o2_ref,
    o3_ref,
    gain_ref,
    router_ref,
    slots_ref,
    one_ref,
    two_ref,
    first_ref,
    second_ref,
    resid_ref,
    hidden_ref,
    sent_ref,
    weight_ref,
    mixed_ref,
    whole_ref,
):
    mixed = (m0_ref, m1_ref, m2_ref, m3_ref)
    parts = (o0_ref, o1_ref, o2_ref, o3_ref)
    width = m0_ref.shape[1]
    for turn in range(4):

        @pl.when(turn_ref[0] == turn)
        def _():
            for i in range(4):
                mixed_ref[:, i * width : (i + 1) * width] = mixed[i ^ turn][...]
                whole_ref[i * width : (i + 1) * width, :] = pad_rows(parts[i ^ turn][...], width)

    resid = grouped_ref[...].astype(jnp.float32) + matmul(mixed_ref[...], whole_ref[...])
    resid_ref[...] = resid
    hidden = (resid * rms_scale(resid) * gain_ref[...]).astype(jnp.bfloat16)
    hidden_ref[...] = hidden
    logits = matmul_bt(router_ref[...], hidden)
    chosen_one = jnp.sum(one_ref[...] * logits, axis=0, keepdims=True)
    chosen_two = jnp.sum(two_ref[...] * logits, axis=0, keepdims=True)
    top = jnp.maximum(chosen_one, chosen_two)
    raised_one = jnp.exp(chosen_one - top)
    raised_two = jnp.exp(chosen_two - top)
    weight_one = raised_one / (raised_one + raised_two)
    weight_two = raised_two / (raised_one + raised_two)
    weight_ref[0:1, :] = weight_one
    weight_ref[1:2, :] = weight_two
    gate_of = first_ref[...] * weight_one + second_ref[...] * weight_two
    high = gate_of.astype(jnp.bfloat16).astype(jnp.float32)
    rest = gate_of - high
    middle = rest.astype(jnp.bfloat16).astype(jnp.float32)
    three = jnp.concatenate([high, middle, rest - middle], axis=0).astype(jnp.bfloat16)
    lines = matmul_bt(three, slots_ref[...])
    dests = first_ref.shape[0]
    last = 16
    at = half_slots - (block - last)
    sub_last = lax.broadcasted_iota(jnp.int32, (last, block), 0)
    chunk = 256
    for base in range(0, slots_ref.shape[0], chunk):
        rows = matmul(slots_ref[base : base + chunk, :], hidden)
        sent_ref[base : base + chunk, :] = rows.astype(jnp.bfloat16)
        for inner in range(block, chunk + 1, block):
            dest = (base + inner) // block - 1
            for i in range(3):
                line = lines[i * dests + dest : i * dests + dest + 1, dest * block : (dest + 1) * block]
                old = rows[inner - last : inner, i * 128 : i * 128 + block]
                sent_ref[base + inner - last : base + inner, i * 128 : i * 128 + block] = jnp.where(
                    sub_last == at, line, old
                ).astype(jnp.bfloat16)


def run_middle(half_slots, block, turn, *ins):
    rows, width = ins[0].shape
    feat = ins[4].shape[1]
    slots = ins[11]
    outs = [
        jax.ShapeDtypeStruct((rows, feat), jnp.float32),
        jax.ShapeDtypeStruct((rows, feat), jnp.bfloat16),
        jax.ShapeDtypeStruct((slots.shape[0], feat), jnp.bfloat16),
        jax.ShapeDtypeStruct((8, rows), jnp.float32),
    ]
    return call_whole(
        functools.partial(middle_kernel, half_slots, block),
        "middle",
        ins,
        outs,
        [pltpu.VMEM((rows, 4 * width), jnp.bfloat16), pltpu.VMEM((4 * width, feat), jnp.bfloat16)],
        2 * rows * feat * (4 * width + slots.shape[0]),
        4 * rows,
        (turn,),
    )


def piece_gradients(d_proj, w_out, q_ref, k_ref, v_ref, lse_ref, bias_ref, cos, sin, all_ref):
    rows, width = q_ref.shape
    span = 256
    scale = HD ** (-0.5)
    lane_ids = lax.broadcasted_iota(jnp.int32, (rows, 128), 1)
    d_all = matmul_bt(d_proj, pad_rows(w_out, width)).astype(jnp.bfloat16)
    blocks = rows // span

    def unturn(values):
        return (values * cos - swap_halves(values) * sin).astype(jnp.bfloat16)

    for pair in range(width // 128):
        at = slice(pair * 128, pair * 128 + 128)
        k = k_ref[:, at]
        v = v_ref[:, at]
        q_scaled = q_ref[:, at] * jnp.bfloat16(scale)
        d_mixed = d_all[:, at]
        zero = jnp.zeros_like(q_scaled)
        d_q = [jnp.zeros((span, 128), jnp.float32) for _ in range(blocks)]
        d_k = [jnp.zeros((span, 128), jnp.float32) for _ in range(blocks)]
        d_v = [jnp.zeros((span, 128), jnp.float32) for _ in range(blocks)]
        for head in range(heads_of(w_out.shape[0], pair)):
            mask = (lane_ids < HD) if head == 0 else (lane_ids >= HD)
            q_head = jnp.where(mask, q_scaled, zero)
            k_head = jnp.where(mask, k, zero)
            d_head = jnp.where(mask, d_mixed, zero)
            which = pair * 2 + head
            for block in range(blocks):
                start, end = block * span, block * span + span
                lse = jnp.sum(
                    jnp.where(lane_ids[start:end] == which, lse_ref[start:end, :], 0.0),
                    axis=-1,
                    keepdims=True,
                )
                scores = matmul_bt(q_head[start:end], k[:end]) + bias_ref[start:end, :end]
                probs = jnp.exp(scores - lse)
                d_probs = matmul_bt(d_head[start:end], v[:end])
                inner = jnp.sum(probs * d_probs, axis=-1, keepdims=True)
                d_scores = (probs * (d_probs - inner)).astype(jnp.bfloat16)
                probs = probs.astype(jnp.bfloat16)
                d_q[block] = d_q[block] + matmul(d_scores, k_head[:end])
                key_term = matmul_at(d_scores, q_head[start:end])
                value_term = matmul_at(probs, d_head[start:end])
                for other in range(block + 1):
                    part = slice(other * span, other * span + span)
                    d_k[other] = d_k[other] + key_term[part]
                    d_v[other] = d_v[other] + value_term[part]
        at_k = slice(width + pair * 128, width + pair * 128 + 128)
        at_v = slice(2 * width + pair * 128, 2 * width + pair * 128 + 128)
        all_ref[:, at] = unturn(jnp.concatenate(d_q, axis=0) * scale)
        all_ref[:, at_k] = unturn(jnp.concatenate(d_k, axis=0))
        all_ref[:, at_v] = jnp.concatenate(d_v, axis=0).astype(jnp.bfloat16)


def back_near_kernel(
    turn_ref,
    dh_own_ref,
    dh_other_ref,
    dg_ref,
    weight_ref,
    one_ref,
    two_ref,
    router_ref,
    resid_ref,
    hidden_two_ref,
    cot_ref,
    gain_ref,
    hidden_ref,
    mixed_ref,
    start_ref,
    cos_ref,
    sin_ref,
    lse_ref,
    w_out_ref,
    q_ref,
    k_ref,
    v_ref,
    wq_ref,
    wk_ref,
    wv_ref,
    d_resid_ref,
    d_proj_ref,
    g_ffn_ref,
    g_router_ref,
    late_ref,
    term_ref,
    bias_ref,
    all_ref,
    dh_ref,
):
    half = dh_own_ref.shape[0]

    @pl.when(turn_ref[0] % 2 == 0)
    def _():
        dh_ref[:half, :] = dh_own_ref[...]
        dh_ref[half:, :] = dh_other_ref[...]

    @pl.when(turn_ref[0] % 2 == 1)
    def _():
        dh_ref[:half, :] = dh_other_ref[...]
        dh_ref[half:, :] = dh_own_ref[...]

    fill_bias(bias_ref, start_ref)
    weight_one, weight_two = (weight_ref[0:1, :], weight_ref[1:2, :])
    d_one, d_two = (dg_ref[0:1, :], dg_ref[1:2, :])
    inner = weight_one * d_one + weight_two * d_two
    d_logits = one_ref[...] * (weight_one * (d_one - inner))
    d_logits = d_logits + two_ref[...] * (weight_two * (d_two - inner))
    d_logits = d_logits.astype(jnp.bfloat16)
    g_router_ref[...] = matmul(d_logits, hidden_two_ref[...])
    d_rows = dh_ref[...].astype(jnp.float32) + matmul_at(d_logits, router_ref[...])
    resid = resid_ref[...]
    scale = rms_scale(resid)
    normed = resid * scale
    g_ffn_ref[...] = jnp.sum(d_rows * normed, axis=0, keepdims=True)
    grown = d_rows * gain_ref[...]
    shift = jnp.mean(grown * normed, axis=-1, keepdims=True)
    d_resid = cot_ref[...].astype(jnp.float32) + scale * (grown - normed * shift)
    d_resid_ref[...] = d_resid
    d_proj_ref[...] = d_resid.astype(jnp.bfloat16)
    piece_gradients(
        d_proj_ref[...],
        w_out_ref[...],
        q_ref,
        k_ref,
        v_ref,
        lse_ref,
        bias_ref,
        cos_ref[...],
        sin_ref[...],
        all_ref,
    )
    piece, width = (w_out_ref.shape[0], q_ref.shape[1])
    grads = matmul_at(all_ref[...], hidden_ref[...]).astype(jnp.bfloat16)
    for i in range(3):
        late_ref[i * piece : (i + 1) * piece, :] = grads[i * width : i * width + piece, :]
    g_out = matmul_at(mixed_ref[...], d_proj_ref[...]).astype(jnp.bfloat16)
    late_ref[3 * piece : 4 * piece, :] = g_out[:piece, :]
    whole = jnp.concatenate([pad_rows(w[...], width) for w in (wq_ref, wk_ref, wv_ref)], axis=0)
    term_ref[...] = matmul(all_ref[...], whole)


def run_back_near(turn, *ins):
    rows, feat = ins[7].shape
    piece = ins[17].shape[0]
    width = padded(piece)
    outs = [
        jax.ShapeDtypeStruct((rows, feat), jnp.float32),
        jax.ShapeDtypeStruct((rows, feat), jnp.bfloat16),
        jax.ShapeDtypeStruct((1, feat), jnp.float32),
        jax.ShapeDtypeStruct((EXPERTS, feat), jnp.float32),
        jax.ShapeDtypeStruct((4 * piece, feat), jnp.bfloat16),
        jax.ShapeDtypeStruct((rows, feat), jnp.float32),
    ]
    return call_whole(
        back_near_kernel,
        "back_near",
        ins,
        outs,
        [
            pltpu.VMEM((rows, rows), jnp.float32),
            pltpu.VMEM((rows, 3 * width), jnp.bfloat16),
            pltpu.VMEM((rows, feat), jnp.bfloat16),
        ],
        rows * width * (16 * feat + 10 * rows),
        rows * rows * piece // HD,
        (turn,),
    )


def back_far_kernel(
    d_proj_ref,
    start_ref,
    cos_ref,
    sin_ref,
    lse_ref,
    w_out_ref,
    q_ref,
    k_ref,
    v_ref,
    all_ref,
    bias_ref,
):
    fill_bias(bias_ref, start_ref)
    piece_gradients(
        d_proj_ref[...],
        w_out_ref[...],
        q_ref,
        k_ref,
        v_ref,
        lse_ref,
        bias_ref,
        cos_ref[...],
        sin_ref[...],
        all_ref,
    )


def run_back_far(*ins):
    rows, feat = ins[0].shape
    piece = ins[5].shape[0]
    width = padded(piece)
    return call_whole(
        back_far_kernel,
        "back_far",
        ins,
        [jax.ShapeDtypeStruct((rows, 3 * width), jnp.bfloat16)],
        [pltpu.VMEM((rows, rows), jnp.float32)],
        rows * width * (2 * feat + 10 * rows),
        rows * rows * piece // HD,
    )[0]


def back_rows_kernel(
    all_ref,
    d_resid_ref,
    term_ref,
    place_own_ref,
    place_other_ref,
    wq_ref,
    wk_ref,
    wv_ref,
    give_ref,
    keep_ref,
    d_half_ref,
    sum_ref,
):
    width = all_ref.shape[1] // 3
    whole = jnp.concatenate([pad_rows(w[...], width) for w in (wq_ref, wk_ref, wv_ref)], axis=0)
    sum_ref[...] = matmul(all_ref[...], whole)
    total = (term_ref[...] + sum_ref[...]).astype(jnp.bfloat16)
    give_ref[...] = matmul_at(place_other_ref[...], total).astype(jnp.bfloat16)
    keep_ref[...] = matmul_at(place_own_ref[...], total).astype(jnp.bfloat16)
    d_resid = d_resid_ref[...]
    high = d_resid.astype(jnp.bfloat16)
    low = (d_resid - high.astype(jnp.float32)).astype(jnp.bfloat16)
    d_half_ref[...] = matmul_at(place_own_ref[...], high) + matmul_at(place_own_ref[...], low)


def run_back_rows(*ins):
    rows, width = ins[0].shape
    feat = ins[1].shape[1]
    half = ins[3].shape[1]
    outs = [
        jax.ShapeDtypeStruct((half, feat), jnp.bfloat16),
        jax.ShapeDtypeStruct((half, feat), jnp.bfloat16),
        jax.ShapeDtypeStruct((half, feat), jnp.float32),
    ]
    return call_whole(
        back_rows_kernel,
        "back_rows",
        ins,
        outs,
        [pltpu.VMEM((rows, feat), jnp.float32)],
        2 * rows * width * feat + 8 * rows * half * feat,
    )


def body(
    tokens,
    order,
    lengths,
    routes,
    attn_gain,
    w_query,
    w_key,
    w_value,
    w_out,
    ffn_gain,
    w_router,
    shared_gate,
    shared_up,
    shared_down,
    expert_gate,
    expert_up,
    expert_down,
    cotangent,
):
    row_count, feat_width = tokens.shape
    group_count = lax.axis_size("expert")
    share_rows = row_count // group_count
    half_share = share_rows // 2
    half_rows = row_count // 2
    my_group = lax.axis_index("expert")
    my_tensor = lax.axis_index("tensor")
    bit_low = lax.rem(my_tensor, 2)
    bit_high = my_tensor // 2
    slab_dev = expert_gate.shape[0]
    slab_total = slab_dev * group_count
    replicas = max(1, slab_total // EXPERTS)
    half_slots = slab_dev * CAP // 2
    row_ids = jnp.arange(row_count, dtype=jnp.int32)
    earlier = (row_ids[:, None] < row_ids[None, :]).astype(jnp.bfloat16)

    local_order = lax.dynamic_slice_in_dim(order, my_group * row_count, row_count, 0)
    groups = jnp.arange(group_count, dtype=jnp.int32)
    dest_group = local_order // row_count
    dest_onehot = (groups[:, None] == dest_group[None, :]).astype(jnp.bfloat16)
    dest_before = matmul(dest_onehot, earlier)
    send_rank = jnp.sum(dest_onehot.astype(jnp.float32) * dest_before, axis=0).astype(jnp.int32)
    send_half = send_rank // half_share
    send_slot = send_half * half_rows + dest_group * half_share + send_rank % half_share
    send_pick = send_slot[None, :] == (
        bit_low * half_rows + jnp.arange(half_rows, dtype=jnp.int32)[:, None]
    )
    send_pick = send_pick.astype(jnp.bfloat16)
    in_tokens = exchange(select(send_pick, tokens))
    cot_send, in_tokens = tie(select(send_pick, cotangent), in_tokens)
    in_cot = exchange(cot_send)

    near_weights = (w_query.T, w_key.T, w_value.T)
    far_weights = tuple(far_swap(weight) for weight in near_weights)
    out_far = far_swap(after(w_out, far_weights[1]))
    tokens_other = core_swap(in_tokens)
    turn = my_tensor.reshape(1)

    all_order = order.reshape(group_count, row_count)
    mine = all_order // row_count == my_group
    arrive_rank = matmul(mine.astype(jnp.bfloat16), earlier).astype(jnp.int32)
    arrive_rank = jnp.where(mine, arrive_rank, -1)
    landing = all_order - my_group * row_count
    target = jnp.sum(
        jnp.where(
            arrive_rank[:, None, :] == jnp.arange(share_rows, dtype=jnp.int32)[None, :, None],
            landing[:, None, :],
            0,
        ),
        axis=-1,
    )
    target = target.reshape(group_count, 2, half_share).transpose(1, 0, 2).reshape(2, half_rows)
    target_own = lax.dynamic_index_in_dim(target, bit_low, 0, keepdims=False)
    target_other = lax.dynamic_index_in_dim(target, 1 - bit_low, 0, keepdims=False)
    place_own = (row_ids[:, None] == target_own[None, :]).astype(jnp.bfloat16)
    place_other = (row_ids[:, None] == target_other[None, :]).astype(jnp.bfloat16)

    expert_ids = jnp.arange(EXPERTS, dtype=jnp.int32)
    member_one = expert_ids[:, None] == routes[None, :, 0]
    member_two = expert_ids[:, None] == routes[None, :, 1]
    member = member_one | member_two
    slot_rank = matmul(member.astype(jnp.bfloat16), earlier).astype(jnp.int32)
    slot_rank = jnp.where(member, slot_rank, -1)

    block = (half_slots + 16) // 16 * 16
    ranks = jnp.repeat(slot_rank, replicas, axis=0).reshape(group_count, slab_dev, row_count)
    ranks = lax.dynamic_index_in_dim(ranks, bit_low * half_slots // CAP, 1, keepdims=False)
    slot_ids = jnp.arange(block, dtype=jnp.int32)
    slots = bit_low * half_slots % CAP + slot_ids
    slots = jnp.where(slot_ids < half_slots, slots, -2)
    slots_cube = (ranks[:, None, :] == slots[None, :, None]).astype(jnp.bfloat16)
    slots_one = slots_cube.reshape(group_count * block, row_count)

    quarter = block // 2
    slots_part = lax.dynamic_slice_in_dim(slots_cube, bit_high * quarter, quarter, 1)
    slots_part = slots_part.reshape(-1, row_count)
    cot_pick_own = select(slots_part, place_own)
    cot_pick_other = select(slots_part, place_other)

    seq_lengths = lengths[0]
    seq_ends = jnp.cumsum(seq_lengths)
    passed = row_ids[:, None] >= seq_ends[None, :]
    sequence_segment = jnp.sum(passed.astype(jnp.int32), axis=1)
    position = row_ids - jnp.sum(jnp.where(passed, seq_lengths[None, :], 0), axis=1)
    half_size = HD // 2
    lanes = jnp.arange(128, dtype=jnp.int32)
    frequency = ROPE_BASE ** (-(lanes % half_size).astype(jnp.float32) / half_size)
    angles = position.astype(jnp.float32)[:, None] * frequency[None, :]
    cos_table = jnp.cos(angles)
    sin_table = jnp.where(lanes % HD < half_size, -1.0, 1.0) * jnp.sin(angles)
    seq_start = jnp.broadcast_to((row_ids - position)[:, None], (row_count, 128))
    gain_one = attn_gain.astype(jnp.float32)[None, :]
    gain_two = ffn_gain.astype(jnp.float32)[None, :]
    tables = (cos_table, sin_table, seq_start)
    grouped, hidden_one, *near_heads, near_mixed, near_lse = run_attention(
        True,
        (in_tokens, tokens_other, place_own, place_other, gain_one, *near_weights, *tables),
    )
    near_swapped = core_swap(near_mixed)
    far_weights = after(far_weights, near_mixed)
    *far_heads, far_mixed, far_lse = run_attention(False, (hidden_one, *far_weights, *tables))
    far_swapped = core_swap(far_mixed)
    out_pieces = (w_out, core_swap(w_out), out_far, core_swap(out_far))
    in_cot = after(in_cot, far_mixed)
    cot_half = core_swap(in_cot)
    cot_part = matmul(cot_pick_own, in_cot) + matmul(cot_pick_other, cot_half)
    cot_part = cot_part.astype(jnp.bfloat16)
    far_swapped = after(far_swapped, cot_part)
    cot_part = exchange(cot_part)

    dest_slab = jnp.arange(group_count, dtype=jnp.int32) * slab_dev + bit_low * half_slots // CAP
    dest_expert = dest_slab // replicas
    first_here = (routes[None, :, 0] == dest_expert[:, None]).astype(jnp.float32)
    second_here = (routes[None, :, 1] == dest_expert[:, None]).astype(jnp.float32)
    one_of = member_one.astype(jnp.float32)
    two_of = member_two.astype(jnp.float32)
    router_rows = w_router.T
    resid_two, hidden_two, sent, gate_weights = run_middle(
        half_slots,
        block,
        turn,
        near_mixed,
        near_swapped,
        far_mixed,
        far_swapped,
        grouped,
        *out_pieces,
        gain_two,
        router_rows,
        slots_one,
        one_of,
        two_of,
        first_here,
        second_here,
    )
    hidden_rows = exchange(after(sent, cot_part))
    cot_part = cot_part.reshape(group_count, quarter, feat_width)
    cot_own = in_order(bit_high, cot_part, far_swap(cot_part), 1).reshape(-1, feat_width)
    cot_other = core_swap(cot_own)
    grouped_cot = matmul(place_own, after(in_cot, sent)) + matmul(place_other, cot_half)
    grouped_cot = grouped_cot.astype(jnp.bfloat16)
    hidden_late = after(hidden_two, cot_part)

    gate_shared = matmul(hidden_two, shared_gate)
    up_shared = matmul(hidden_late, shared_up)
    act_shared = silu_value(gate_shared)
    shared_mid = (act_shared * up_shared).astype(jnp.bfloat16)
    shared_out = matmul(shared_mid, shared_down)
    d_mid_shared = matmul_bt(grouped_cot, shared_down)
    d_up_shared = (d_mid_shared * act_shared).astype(jnp.bfloat16)
    d_gate_shared = (d_mid_shared * up_shared * silu_slope(gate_shared)).astype(jnp.bfloat16)
    d_both = jnp.concatenate([d_gate_shared, d_up_shared], axis=1)
    early = GroupSum(
        jnp.concatenate([matmul_at(d_both, hidden_late), matmul_at(shared_mid, grouped_cot)], axis=0)
    )
    early.start()
    d_gate_shared, d_up_shared, shared_out, resid_late, _ = tie(
        d_gate_shared, d_up_shared, shared_out, resid_two, early.given
    )
    d_hidden_shared = matmul_bt(d_gate_shared, shared_gate) + matmul_bt(d_up_shared, shared_up)
    shared_send = shared_out.astype(jnp.bfloat16)
    shared_own = matmul_at(place_own, shared_send)
    shared_other = matmul_at(place_other, shared_send)
    resid_high, resid_low = three_parts(resid_late)[:2]
    resid_half = matmul_at(place_own, resid_high) + matmul_at(place_own, resid_low)
    hidden_rows = after(
        hidden_rows, cot_other, d_hidden_shared, shared_own, shared_other, resid_half
    )
    rows_other = core_swap(hidden_rows)
    early.end(d_hidden_shared, shared_own, shared_other, resid_half)
    early.start()
    rows_other = after(rows_other, early.given)

    which_own = (bit_low * half_slots // CAP).reshape(1)
    which_other = ((1 - bit_low) * half_slots // CAP).reshape(1)
    weights_here = (expert_gate, expert_up, expert_down, half_slots, block)
    back_given, out_given, mid_other, dg_other, du_other = run_expert(
        which_other, rows_other, cot_other, *weights_here
    )
    early.end(back_given)
    early.start()
    back_given = after(back_given, early.given)
    hidden_rows = after(hidden_rows, back_given)
    back_kept, out_kept, mid_own, dg_own, du_own = run_expert(
        which_own, hidden_rows, cot_own, *weights_here
    )
    stack_own = (hidden_rows, cot_own, mid_own, dg_own, du_own)
    stack_other = (rows_other, cot_other, mid_other, dg_other, du_other)

    back_sum = back_kept.astype(jnp.float32) + core_swap(back_given).astype(jnp.float32)
    back_sum = back_sum.reshape(group_count, block, feat_width)
    lines = back_sum[:, half_slots, :384].reshape(group_count, 3, 128)
    lines = jnp.stack(three_parts(jnp.sum(lines, axis=1)), axis=1).astype(jnp.float32)
    lines = jnp.pad(lines.reshape(group_count, 1, 384), ((0, 0), (0, 0), (0, feat_width - 384)))
    back_sum = jnp.where(slot_ids[None, :, None] == half_slots, lines, back_sum)
    back_send = back_sum.astype(jnp.bfloat16).reshape(-1, feat_width)
    back_own = exchange(back_send)
    early.end(back_send)
    while early.stage < early.bits:
        early.start()
        early.end()
    out_sum = pair_sum(out_kept, after(out_given, back_send, early.part))
    out_sum = out_sum.reshape(group_count, block, feat_width)
    out_kept = lax.dynamic_slice_in_dim(out_sum, bit_high * quarter, quarter, 1)
    out_given = lax.dynamic_slice_in_dim(out_sum, (1 - bit_high) * quarter, quarter, 1)
    out_send = out_kept.astype(jnp.float32) + far_swap(out_given).astype(jnp.float32)
    out_send = out_send.astype(jnp.bfloat16).reshape(-1, feat_width)
    if slab_dev == 2:
        own_late = after(stack_own[0], out_given)
        stack_own = (own_late,) + stack_own[1:]
        g_expert_gate, g_expert_up, g_expert_down = run_weights(bit_low, stack_own, stack_other)
    else:
        wide = [jnp.concatenate(pair, axis=0) for pair in zip(stack_own, stack_other)]
        g_expert_gate = matmul_at(wide[0], wide[3])[None]
        g_expert_up = matmul_at(wide[0], wide[4])[None]
        g_expert_down = matmul_at(wide[2], wide[1])[None]


    back_own = after(back_own, g_expert_gate, out_send)
    d_hidden_part = (matmul_at(slots_one, back_own) + d_hidden_shared).astype(jnp.bfloat16)
    kept = lax.dynamic_slice_in_dim(d_hidden_part, bit_low * half_rows, half_rows, 0)
    given = lax.dynamic_slice_in_dim(d_hidden_part, (1 - bit_low) * half_rows, half_rows, 0)
    dg_lines = back_own.reshape(group_count, block, feat_width)[:, half_slots, :384]
    dg_lines = dg_lines.reshape(group_count, 3, 128)[:, :, :block]
    dg_of = jnp.einsum("dps,dsr->dpr", dg_lines, slots_cube, preferred_element_type=jnp.float32)
    dg_of = jnp.sum(dg_of, axis=1)
    dg_part = jnp.stack(
        [jnp.sum(first_here * dg_of, axis=0), jnp.sum(second_here * dg_of, axis=0)], axis=0
    )
    dg_part = jnp.pad(dg_part, ((0, 6), (0, 0)))
    dg_part = dg_part + core_swap(dg_part)
    pair = pair_sum(kept, given)
    early.start(pair)
    far, early.came, dg_far = tie(far_swap(pair), early.came, far_swap(dg_part))
    d_hidden_half = (pair.astype(jnp.float32) + far.astype(jnp.float32)).astype(jnp.bfloat16)
    early.end(d_hidden_half)
    out_own = exchange(after(out_send, d_hidden_half))
    d_hidden_other = core_swap(d_hidden_half)
    dg_part = dg_part + dg_far
    d_resid, d_proj, g_ffn_gain, g_router, late, term = run_back_near(
        turn,
        d_hidden_half,
        d_hidden_other,
        dg_part,
        gate_weights,
        one_of,
        two_of,
        router_rows,
        resid_two,
        hidden_two,
        grouped_cot,
        gain_two,
        hidden_one,
        near_mixed,
        seq_start,
        cos_table,
        sin_table,
        near_lse,
        w_out,
        *near_heads,
        *near_weights,
    )
    early.start(d_proj)
    late = GroupSum(late, True)
    late.start()
    ffn_rows = after(out_own, late.given)
    ffn_given = (matmul_at(cot_pick_other, ffn_rows) + shared_other).astype(jnp.bfloat16)
    ffn_kept = (matmul_at(cot_pick_own, ffn_rows) + shared_own).astype(jnp.bfloat16)
    ffn_pair = pair_sum(ffn_kept, ffn_given)
    ffn_half = ffn_pair.astype(jnp.float32) + far_swap(ffn_pair).astype(jnp.float32)
    output_send = (resid_half + ffn_half).astype(jnp.bfloat16)
    far_all = run_back_far(
        after(d_proj, ffn_pair),
        seq_start,
        cos_table,
        sin_table,
        far_lse,
        out_far,
        *far_heads,
    )
    late.end(far_all)
    late.start()
    early.end(far_all)
    early.start_first(4)
    d_one_given, d_one_kept, d_resid_half = run_back_rows(
        after(far_all, output_send, late.given),
        d_resid,
        term,
        place_own,
        place_other,
        *far_weights,
    )
    late.end(d_one_given)
    late.start()
    early.first, d_one_given = tie(early.first, d_one_given)
    early.start_second()
    d_one = d_one_kept.astype(jnp.float32) + core_swap(d_one_given).astype(jnp.float32)
    resid = in_tokens.astype(jnp.float32)
    scale_one = rms_scale(resid)
    normed_one = resid * scale_one
    e_one = d_one * gain_one
    shift_one = jnp.mean(e_one * normed_one, axis=-1, keepdims=True)
    d_tokens_send = (d_resid_half + scale_one * (e_one - normed_one * shift_one)).astype(jnp.bfloat16)
    g_attn_gain = jnp.sum(d_one * normed_one, axis=0, keepdims=True)
    both_send = jnp.concatenate(
        [
            d_tokens_send.reshape(group_count, half_share, feat_width),
            output_send.reshape(group_count, half_share, feat_width),
        ],
        axis=1,
    )
    small = jnp.concatenate([g_router, g_ffn_gain, g_attn_gain + core_swap(g_attn_gain)], axis=0)
    small = jnp.pad(small, ((0, -small.shape[0] % 8), (0, 0)))
    late.end(both_send)
    late.start()
    late.end()
    both_own = exchange(after(both_send, late.part))
    small = after(small, late.part)
    small = small + group_swap(small, 0)
    late.start(small)
    early.end_second(late.part)

    for step in range(1, group_count.bit_length() - 1):
        small = small + group_swap(small, step)
    g_router = small[:EXPERTS].T
    g_ffn_gain = small[EXPERTS]
    g_attn_gain = small[EXPERTS + 1]
    late = late.finish().astype(jnp.float32)
    shared = early.finish(late).astype(jnp.float32)
    hidden_s = shared_gate.shape[1]
    g_shared_gate = shared[:hidden_s].T
    g_shared_up = shared[hidden_s : 2 * hidden_s].T
    g_shared_down = shared[2 * hidden_s :]
    head_rows = w_out.shape[0]
    g_query = late[:head_rows].T
    g_key = late[head_rows : 2 * head_rows].T
    g_value = late[2 * head_rows : 3 * head_rows].T
    g_out = late[3 * head_rows :]
    both_own = after(
        both_own, g_query, g_key, g_value, g_out, g_shared_gate, g_shared_up, g_shared_down, small
    )
    both_other = core_swap(both_own)

    unsend = (send_slot[:, None] == row_ids[None, :]).astype(jnp.bfloat16)

    def arrive_back(part):
        own = both_own[:, part].reshape(half_rows, feat_width)
        other = both_other[:, part].reshape(half_rows, feat_width)
        return select(unsend, in_order(bit_low, own, other))

    d_tokens = arrive_back(slice(0, half_share))
    output = arrive_back(slice(half_share, 2 * half_share))
    return (
        output,
        d_tokens,
        g_attn_gain,
        g_query,
        g_key,
        g_value,
        g_out,
        g_ffn_gain,
        g_router,
        g_shared_gate,
        g_shared_up,
        g_shared_down,
        g_expert_gate,
        g_expert_up,
        g_expert_down,
    )


def solution(mesh):
    return jax.shard_map(
        body,
        mesh=mesh,
        in_specs=(
            P("expert", None),
            P(),
            P("expert", None),
            P("expert", None),
            P(),
            P(None, "tensor"),
            P(None, "tensor"),
            P(None, "tensor"),
            P("tensor", None),
            P(),
            P(),
            P(None, "tensor"),
            P(None, "tensor"),
            P("tensor", None),
            P("expert", None, "tensor"),
            P("expert", None, "tensor"),
            P("expert", "tensor", None),
            P("expert", None),
        ),
        out_specs=(
            P("expert", None),
            P("expert", None),
            P(),
            P(None, "tensor"),
            P(None, "tensor"),
            P(None, "tensor"),
            P("tensor", None),
            P(),
            P(),
            P(None, "tensor"),
            P(None, "tensor"),
            P("tensor", None),
            P("expert", None, "tensor"),
            P("expert", None, "tensor"),
            P("expert", "tensor", None),
        ),
        check_vma=False,
    )
```

```python
import functools

import jax
import jax.numpy as jnp
from jax import lax
from jax.experimental import pallas as pl
from jax.experimental.pallas import tpu as pltpu
from jax.sharding import PartitionSpec as P

HD = 64
EXPERTS = 16
CAP = 120


EPSILON = 1e-05
ROPE_BASE = 10000.0
MASKED = -1e30


def rms_scale(values):
    return lax.rsqrt(jnp.mean(values * values, axis=-1, keepdims=True) + EPSILON)


def matmul(left_side, right_side):
    return jnp.dot(left_side, right_side, preferred_element_type=jnp.float32)


def matmul_bt(left_side, right_side):
    return lax.dot_general(
        left_side, right_side, (((1,), (1,)), ((), ())), preferred_element_type=jnp.float32
    )


def matmul_at(left_side, right_side):
    return lax.dot_general(
        left_side, right_side, (((0,), (0,)), ((), ())), preferred_element_type=jnp.float32
    )


def silu_value(gate_in):
    return gate_in * jax.nn.sigmoid(gate_in)


def silu_slope(gate_in):
    sigma = jax.nn.sigmoid(gate_in)
    return sigma * (1.0 + gate_in * (1.0 - sigma))


def tie(*values):
    return lax.optimization_barrier(values)


def core_swap(values):
    return lax.ppermute(values, "tensor", [(i, i ^ 1) for i in range(4)])


def far_swap(values):
    return lax.ppermute(values, "tensor", [(i, i ^ 2) for i in range(4)])


def exchange(values):
    return lax.all_to_all(values, "expert", split_axis=0, concat_axis=0, tiled=True)


def in_order(bit, own, other, axis=0):
    return jnp.where(
        bit == 0,
        jnp.concatenate([own, other], axis=axis),
        jnp.concatenate([other, own], axis=axis),
    )


def gather_four(bit_low, bit_high, own, axis):
    far = far_swap(own)
    near = core_swap(own)
    far_near = core_swap(far)
    here = in_order(bit_low, own, near, axis)
    there = in_order(bit_low, far, far_near, axis)
    return in_order(bit_high, here, there, axis)


def select(onehot, values):
    return jnp.dot(onehot, values, preferred_element_type=jnp.float32).astype(jnp.bfloat16)


def pair_sum(kept, given):
    return (kept.astype(jnp.float32) + core_swap(given).astype(jnp.float32)).astype(jnp.bfloat16)


def after(values, *anchors):
    return lax.optimization_barrier((values, *anchors))[0]


def group_swap(values, step):
    size = lax.axis_size("expert")
    return lax.ppermute(values, "expert", [(i, i ^ (1 << step)) for i in range(size)])


class GroupSum:
    def __init__(self, values, whole_last=False):
        self.bits = lax.axis_size("expert").bit_length() - 1
        self.steps = list(range(self.bits)) + list(reversed(range(self.bits)))
        if whole_last:
            self.steps[self.bits - 1 : self.bits + 1] = [self.bits - 1]
        self.halvings = self.bits - 1 if whole_last else self.bits
        self.whole_last = whole_last
        self.me = lax.axis_index("expert")
        self.shape = values.shape
        pieces = 1 << self.halvings
        self.part = values.astype(jnp.bfloat16).reshape(pieces, -1, values.shape[1])
        self.stage = 0
        self.pending = False
        self.prepare()

    def prepare(self):
        if self.stage < self.halvings:
            bit = (self.me >> self.stage) & 1
            pairs = self.part.reshape((-1, 2) + self.part.shape[1:])
            self.kept = lax.dynamic_index_in_dim(pairs, bit, 1, keepdims=False)
            self.given = lax.dynamic_index_in_dim(pairs, 1 - bit, 1, keepdims=False)
        else:
            self.kept = self.given = self.part

    def start_first(self, share):
        self.cut = self.given.shape[1] // share
        self.first = group_swap(self.given[:, : self.cut], self.steps[self.stage])

    def start_second(self, *anchors):
        self.first, second = tie(self.first, self.given[:, self.cut :], *anchors)[:2]
        self.second = group_swap(second, self.steps[self.stage])

    def end_second(self, *anchors):
        self.came = jnp.concatenate([self.first, after(self.second, *anchors)], axis=1)
        self.end()

    def done(self):
        return self.stage == len(self.steps)

    def start(self, *anchors):
        self.pending = True
        self.came = group_swap(after(self.given, *anchors), self.steps[self.stage])

    def end(self, *anchors):
        came = after(self.came, *anchors)
        self.pending = False
        if self.stage < self.bits:
            total = self.kept.astype(jnp.float32) + came.astype(jnp.float32)
            self.part = total.astype(jnp.bfloat16)
        else:
            bit = (self.me >> self.steps[self.stage]) & 1
            both = in_order(bit, self.part[:, None], came[:, None], 1)
            self.part = both.reshape((-1,) + self.part.shape[1:])
        self.stage += 1
        if not self.done():
            self.prepare()

    def finish(self, *anchors):
        while not self.done():
            if not self.pending:
                self.start()
            self.end(*anchors)
        return self.part.reshape(self.shape)


def three_parts(values):
    high = lax.reduce_precision(values, 8, 7)
    rest = values - high
    middle = lax.reduce_precision(rest, 8, 7)
    return [part.astype(jnp.bfloat16) for part in (high, middle, rest - middle)]


def expert_kernel(
    half_slots,
    block,
    which_ref,
    rows_ref,
    cot_ref,
    gate_ref,
    up_ref,
    down_ref,
    back_ref,
    out_ref,
    mid_ref,
    d_gate_ref,
    d_up_ref,
):
    rows = rows_ref[...]
    count = rows.shape[0]
    gate_w, up_w, down_w = (gate_ref[0], up_ref[0], down_ref[0])
    gate_lin = matmul(rows, gate_w)
    up_lin = matmul(rows, up_w)
    raw = matmul_bt(cot_ref[...], down_w)
    sigma = 1.0 / (1.0 + jnp.exp(-gate_lin))
    act = gate_lin * sigma
    mid = act * up_lin
    scalar = jnp.sum(raw * mid, axis=1, keepdims=True)
    lanes = lax.broadcasted_iota(jnp.int32, (block, 128), 1)
    subs = lax.broadcasted_iota(jnp.int32, (block, 128), 0)
    diagonal = (lanes == subs) & (lanes < half_slots)
    last = 16
    at = half_slots - (block - last)
    sub_last = lax.broadcasted_iota(jnp.int32, (last, 128), 0)
    gates = []
    for b in range(count // block):
        tail = rows_ref[(b + 1) * block - last : (b + 1) * block, 0:384].astype(jnp.float32)
        total = tail[:, 0:128] + tail[:, 128:256] + tail[:, 256:384]
        line = jnp.sum(jnp.where(sub_last == at, total, 0.0), axis=0, keepdims=True)
        gates.append(jnp.sum(jnp.where(diagonal, line, 0.0), axis=1, keepdims=True))
    gate = jnp.concatenate(gates, axis=0) if len(gates) > 1 else gates[0]
    d_act = raw * gate
    d_up = (d_act * act).astype(jnp.bfloat16)
    d_gate = (d_act * up_lin * (sigma * (1.0 + gate_lin * (1.0 - sigma)))).astype(jnp.bfloat16)
    mid_g = (mid * gate).astype(jnp.bfloat16)
    mid_ref[...] = mid_g
    d_gate_ref[...] = d_gate
    d_up_ref[...] = d_up
    back = matmul_bt(d_gate, gate_w) + matmul_bt(d_up, up_w)
    back_ref[...] = back.astype(jnp.bfloat16)
    for b in range(count // block):
        part = jnp.where(diagonal, scalar[b * block : (b + 1) * block], 0.0)
        line = jnp.sum(part, axis=0, keepdims=True)
        high = line.astype(jnp.bfloat16).astype(jnp.float32)
        rest = line - high
        middle = rest.astype(jnp.bfloat16).astype(jnp.float32)
        for i, piece in enumerate((high, middle, rest - middle)):
            old = back[(b + 1) * block - last : (b + 1) * block, i * 128 : (i + 1) * 128]
            back_ref[(b + 1) * block - last : (b + 1) * block, i * 128 : (i + 1) * 128] = jnp.where(
                sub_last == at, piece, old
            ).astype(jnp.bfloat16)
    out_ref[...] = matmul(mid_g, down_w).astype(jnp.bfloat16)


def run_expert(which, rows, cots, gate_w, up_w, down_w, half_slots, block):
    count, feat = rows.shape
    hidden = gate_w.shape[2]
    step_rows = min(256, count)
    row_spec = pl.BlockSpec((step_rows, feat), lambda i, w: (i, 0))
    mid_spec = pl.BlockSpec((step_rows, hidden), lambda i, w: (i, 0))
    return pl.pallas_call(
        functools.partial(expert_kernel, half_slots, block),
        grid_spec=pltpu.PrefetchScalarGridSpec(
            num_scalar_prefetch=1,
            grid=(count // step_rows,),
            in_specs=[
                row_spec,
                row_spec,
                pl.BlockSpec((1, feat, hidden), lambda i, w: (w[0], 0, 0)),
                pl.BlockSpec((1, feat, hidden), lambda i, w: (w[0], 0, 0)),
                pl.BlockSpec((1, hidden, feat), lambda i, w: (w[0], 0, 0)),
            ],
            out_specs=[row_spec, row_spec, mid_spec, mid_spec, mid_spec],
        ),
        out_shape=[jax.ShapeDtypeStruct((count, feat), jnp.bfloat16)] * 2
        + [jax.ShapeDtypeStruct((count, hidden), jnp.bfloat16)] * 3,
        compiler_params=pltpu.CompilerParams(vmem_limit_bytes=50 << 20),
        cost_estimate=pl.CostEstimate(
            flops=12 * count * feat * hidden,
            bytes_accessed=8 * count * feat + 6 * feat * hidden + 6 * count * hidden,
            transcendentals=count * hidden,
        ),
        name="expert_rows",
    )(which, rows, cots, gate_w, up_w, down_w)


def weight_kernel(
    which_ref,
    rows_own,
    rows_other,
    cot_own,
    cot_other,
    mid_own,
    mid_other,
    dg_own,
    dg_other,
    du_own,
    du_other,
    g_gate_ref,
    g_up_ref,
    g_down_ref,
):
    def fill(rows, cots, mid, d_gate, d_up):
        turned = rows[...].T
        g_gate_ref[0] = matmul(turned, d_gate[...])
        g_up_ref[0] = matmul(turned, d_up[...])
        g_down_ref[0] = matmul_at(mid[...], cots[...])

    @pl.when(pl.program_id(0) == 0)
    def _():
        fill(rows_own, cot_own, mid_own, dg_own, du_own)

    @pl.when(pl.program_id(0) == 1)
    def _():
        fill(rows_other, cot_other, mid_other, dg_other, du_other)


def run_weights(bit_low, own, other):
    count, feat = own[0].shape
    hidden = own[2].shape[1]
    width = min(256, hidden)
    whole = pl.BlockSpec((count, feat), lambda s, j, w: (0, 0))
    first = pl.BlockSpec((count, width), lambda s, j, w: (0, jnp.where(s == 0, j, 0)))
    second = pl.BlockSpec((count, width), lambda s, j, w: (0, jnp.where(s == 1, j, 0)))

    def slab(s, w):
        return jnp.where(s == 0, w[0], 1 - w[0])

    wide = pl.BlockSpec((1, feat, width), lambda s, j, w: (slab(s, w), 0, j))
    tall = pl.BlockSpec((1, width, feat), lambda s, j, w: (slab(s, w), j, 0))
    return pl.pallas_call(
        weight_kernel,
        grid_spec=pltpu.PrefetchScalarGridSpec(
            num_scalar_prefetch=1,
            grid=(2, hidden // width),
            in_specs=[whole, whole, whole, whole, first, second, first, second, first, second],
            out_specs=[wide, wide, tall],
        ),
        out_shape=[
            jax.ShapeDtypeStruct((2, feat, hidden), jnp.float32),
            jax.ShapeDtypeStruct((2, feat, hidden), jnp.float32),
            jax.ShapeDtypeStruct((2, hidden, feat), jnp.float32),
        ],
        compiler_params=pltpu.CompilerParams(vmem_limit_bytes=56 << 20),
        cost_estimate=pl.CostEstimate(
            flops=12 * count * feat * hidden,
            bytes_accessed=8 * count * feat + 12 * count * hidden + 24 * feat * hidden,
            transcendentals=0,
        ),
        name="expert_weights",
    )(
        bit_low.reshape(1),
        own[0],
        other[0],
        own[1],
        other[1],
        own[2],
        other[2],
        own[3],
        other[3],
        own[4],
        other[4],
    )


def swap_halves(values):
    lanes = lax.broadcasted_iota(jnp.int32, values.shape, 1)
    return jnp.where(lanes % HD < HD // 2, pltpu.roll(values, 96, 1), pltpu.roll(values, 32, 1))


def fill_bias(bias_ref, start_ref):
    rows = bias_ref.shape[0]
    row_at = lax.broadcasted_iota(jnp.int32, (rows, 128), 0)
    lane_at = lax.broadcasted_iota(jnp.int32, (rows, 128), 1)
    start = start_ref[...]
    for part in range(rows // 128):
        key_at = lane_at + part * 128
        allowed = (key_at >= start) & (key_at <= row_at)
        bias_ref[:, part * 128 : part * 128 + 128] = jnp.where(allowed, 0.0, MASKED)


def fixed(shape):
    return pl.BlockSpec(shape, lambda *_: tuple(0 for _ in shape))


def pad_rows(piece, rows):
    return jnp.concatenate([piece, jnp.zeros((rows - piece.shape[0], piece.shape[1]), piece.dtype)], 0)


def heads_of(piece_rows, pair):
    return min(2, (piece_rows - pair * 128) // HD)


def attend_piece(hidden, weights, cos, sin, bias_ref, outs):
    q_ref, k_ref, v_ref, mixed_ref, lse_ref = outs
    rows = hidden.shape[0]
    width = q_ref.shape[1]
    span = 256
    lane_ids = lax.broadcasted_iota(jnp.int32, (rows, 128), 1)
    lse_ref[...] = jnp.zeros_like(lse_ref)
    linear = matmul_bt(
        hidden, jnp.concatenate([pad_rows(weight[...], width) for weight in weights], axis=0)
    )
    for pair in range(width // 128):
        at = slice(pair * 128, pair * 128 + 128)
        q_lin = linear[:, pair * 128 : pair * 128 + 128]
        k_lin = linear[:, width + pair * 128 : width + pair * 128 + 128]
        v_pair = linear[:, 2 * width + pair * 128 : 2 * width + pair * 128 + 128]
        v_pair = v_pair.astype(jnp.bfloat16)
        q_pair = (q_lin * cos + swap_halves(q_lin) * sin).astype(jnp.bfloat16)
        k_pair = (k_lin * cos + swap_halves(k_lin) * sin).astype(jnp.bfloat16)
        q_ref[:, at] = q_pair
        k_ref[:, at] = k_pair
        v_ref[:, at] = v_pair
        q_scaled = q_pair * jnp.bfloat16(HD ** (-0.5))
        zero = jnp.zeros_like(q_scaled)
        q_heads = [jnp.where(lane_ids < HD, q_scaled, zero), jnp.where(lane_ids < HD, zero, q_scaled)]
        q_heads = q_heads[: heads_of(weights[0].shape[0], pair)]
        for start in range(0, rows, span):
            end = start + span
            ids = lane_ids[start:end]
            mixed = None
            for head, q_head in enumerate(q_heads):
                scores = matmul_bt(q_head[start:end], k_pair[:end]) + bias_ref[start:end, :end]
                top = jnp.max(scores, axis=-1, keepdims=True)
                raised = jnp.exp(scores - top)
                total = jnp.sum(raised, axis=-1, keepdims=True)
                out = matmul(raised.astype(jnp.bfloat16), v_pair[:end]) / total
                mixed = out if mixed is None else jnp.where(ids < HD, mixed, out)
                lse = top + jnp.log(total)
                lse_ref[start:end, :] = jnp.where(
                    ids == pair * 2 + head, lse, lse_ref[start:end, :]
                )
            mixed_ref[start:end, at] = mixed.astype(jnp.bfloat16)


def attention_near_kernel(
    own_ref,
    other_ref,
    place_own_ref,
    place_other_ref,
    gain_ref,
    wq_ref,
    wk_ref,
    wv_ref,
    cos_ref,
    sin_ref,
    start_ref,
    grouped_ref,
    hidden_ref,
    q_ref,
    k_ref,
    v_ref,
    mixed_ref,
    lse_ref,
    bias_ref,
):
    fill_bias(bias_ref, start_ref)
    placed = matmul(place_own_ref[...], own_ref[...])
    placed = placed + matmul(place_other_ref[...], other_ref[...])
    grouped_ref[...] = placed.astype(jnp.bfloat16)
    hidden_ref[...] = (placed * rms_scale(placed) * gain_ref[...]).astype(jnp.bfloat16)
    attend_piece(
        hidden_ref[...],
        (wq_ref, wk_ref, wv_ref),
        cos_ref[...],
        sin_ref[...],
        bias_ref,
        (q_ref, k_ref, v_ref, mixed_ref, lse_ref),
    )


def attention_far_kernel(
    hidden_ref,
    wq_ref,
    wk_ref,
    wv_ref,
    cos_ref,
    sin_ref,
    start_ref,
    q_ref,
    k_ref,
    v_ref,
    mixed_ref,
    lse_ref,
    bias_ref,
):
    fill_bias(bias_ref, start_ref)
    attend_piece(
        hidden_ref[...],
        (wq_ref, wk_ref, wv_ref),
        cos_ref[...],
        sin_ref[...],
        bias_ref,
        (q_ref, k_ref, v_ref, mixed_ref, lse_ref),
    )


def call_whole(kernel, name, ins, outs, scratch, flops, transcendentals=0, prefetch=()):
    moved = sum(array.size * array.dtype.itemsize for array in (*ins, *outs))
    return pl.pallas_call(
        kernel,
        grid_spec=pltpu.PrefetchScalarGridSpec(
            num_scalar_prefetch=len(prefetch),
            grid=(1,),
            in_specs=[fixed(array.shape) for array in ins],
            out_specs=[fixed(out.shape) for out in outs],
            scratch_shapes=scratch,
        ),
        out_shape=list(outs),
        compiler_params=pltpu.CompilerParams(vmem_limit_bytes=56 << 20),
        cost_estimate=pl.CostEstimate(
            flops=flops, bytes_accessed=moved, transcendentals=transcendentals
        ),
        name=name,
    )(*prefetch, *ins)


def padded(piece_rows):
    return -(-piece_rows // 128) * 128


def run_attention(near, ins):
    rows = ins[-1].shape[0]
    feat = ins[0].shape[1]
    piece = ins[-4].shape[0]
    width = padded(piece)
    outs = [jax.ShapeDtypeStruct((rows, feat), jnp.bfloat16)] * (2 if near else 0)
    outs = outs + [jax.ShapeDtypeStruct((rows, width), jnp.bfloat16)] * 4
    outs = outs + [jax.ShapeDtypeStruct((rows, 128), jnp.float32)]
    return call_whole(
        attention_near_kernel if near else attention_far_kernel,
        "attention_near" if near else "attention_far",
        ins,
        outs,
        [pltpu.VMEM((rows, rows), jnp.float32)],
        6 * rows * feat * width + 4 * rows * rows * width + (2 * rows * rows * feat if near else 0),
        rows * rows * piece // HD,
    )


def middle_kernel(
    half_slots,
    block,
    turn_ref,
    m0_ref,
    m1_ref,
    m2_ref,
    m3_ref,
    grouped_ref,
    o0_ref,
    o1_ref,
    o2_ref,
    o3_ref,
    gain_ref,
    router_ref,
    slots_ref,
    one_ref,
    two_ref,
    first_ref,
    second_ref,
    resid_ref,
    hidden_ref,
    sent_ref,
    weight_ref,
    mixed_ref,
    whole_ref,
):
    mixed = (m0_ref, m1_ref, m2_ref, m3_ref)
    parts = (o0_ref, o1_ref, o2_ref, o3_ref)
    width = m0_ref.shape[1]
    for turn in range(4):

        @pl.when(turn_ref[0] == turn)
        def _():
            for i in range(4):
                mixed_ref[:, i * width : (i + 1) * width] = mixed[i ^ turn][...]
                whole_ref[i * width : (i + 1) * width, :] = pad_rows(parts[i ^ turn][...], width)

    resid = grouped_ref[...].astype(jnp.float32) + matmul(mixed_ref[...], whole_ref[...])
    resid_ref[...] = resid
    hidden = (resid * rms_scale(resid) * gain_ref[...]).astype(jnp.bfloat16)
    hidden_ref[...] = hidden
    logits = matmul_bt(router_ref[...], hidden)
    chosen_one = jnp.sum(one_ref[...] * logits, axis=0, keepdims=True)
    chosen_two = jnp.sum(two_ref[...] * logits, axis=0, keepdims=True)
    top = jnp.maximum(chosen_one, chosen_two)
    raised_one = jnp.exp(chosen_one - top)
    raised_two = jnp.exp(chosen_two - top)
    weight_one = raised_one / (raised_one + raised_two)
    weight_two = raised_two / (raised_one + raised_two)
    weight_ref[0:1, :] = weight_one
    weight_ref[1:2, :] = weight_two
    gate_of = first_ref[...] * weight_one + second_ref[...] * weight_two
    high = gate_of.astype(jnp.bfloat16).astype(jnp.float32)
    rest = gate_of - high
    middle = rest.astype(jnp.bfloat16).astype(jnp.float32)
    three = jnp.concatenate([high, middle, rest - middle], axis=0).astype(jnp.bfloat16)
    lines = matmul_bt(three, slots_ref[...])
    dests = first_ref.shape[0]
    last = 16
    at = half_slots - (block - last)
    sub_last = lax.broadcasted_iota(jnp.int32, (last, block), 0)
    chunk = 256
    for base in range(0, slots_ref.shape[0], chunk):
        rows = matmul(slots_ref[base : base + chunk, :], hidden)
        sent_ref[base : base + chunk, :] = rows.astype(jnp.bfloat16)
        for inner in range(block, chunk + 1, block):
            dest = (base + inner) // block - 1
            for i in range(3):
                line = lines[i * dests + dest : i * dests + dest + 1, dest * block : (dest + 1) * block]
                old = rows[inner - last : inner, i * 128 : i * 128 + block]
                sent_ref[base + inner - last : base + inner, i * 128 : i * 128 + block] = jnp.where(
                    sub_last == at, line, old
                ).astype(jnp.bfloat16)


def run_middle(half_slots, block, turn, *ins):
    rows, width = ins[0].shape
    feat = ins[4].shape[1]
    slots = ins[11]
    outs = [
        jax.ShapeDtypeStruct((rows, feat), jnp.float32),
        jax.ShapeDtypeStruct((rows, feat), jnp.bfloat16),
        jax.ShapeDtypeStruct((slots.shape[0], feat), jnp.bfloat16),
        jax.ShapeDtypeStruct((8, rows), jnp.float32),
    ]
    return call_whole(
        functools.partial(middle_kernel, half_slots, block),
        "middle",
        ins,
        outs,
        [pltpu.VMEM((rows, 4 * width), jnp.bfloat16), pltpu.VMEM((4 * width, feat), jnp.bfloat16)],
        2 * rows * feat * (4 * width + slots.shape[0]),
        4 * rows,
        (turn,),
    )


def piece_gradients(d_proj, w_out, q_ref, k_ref, v_ref, lse_ref, bias_ref, cos, sin, all_ref):
    rows, width = q_ref.shape
    span = 256
    scale = HD ** (-0.5)
    lane_ids = lax.broadcasted_iota(jnp.int32, (rows, 128), 1)
    d_all = matmul_bt(d_proj, pad_rows(w_out, width)).astype(jnp.bfloat16)
    blocks = rows // span

    def unturn(values):
        return (values * cos - swap_halves(values) * sin).astype(jnp.bfloat16)

    for pair in range(width // 128):
        at = slice(pair * 128, pair * 128 + 128)
        k = k_ref[:, at]
        v = v_ref[:, at]
        q_scaled = q_ref[:, at] * jnp.bfloat16(scale)
        d_mixed = d_all[:, at]
        zero = jnp.zeros_like(q_scaled)
        d_q = [jnp.zeros((span, 128), jnp.float32) for _ in range(blocks)]
        d_k = [jnp.zeros((span, 128), jnp.float32) for _ in range(blocks)]
        d_v = [jnp.zeros((span, 128), jnp.float32) for _ in range(blocks)]
        for head in range(heads_of(w_out.shape[0], pair)):
            mask = (lane_ids < HD) if head == 0 else (lane_ids >= HD)
            q_head = jnp.where(mask, q_scaled, zero)
            k_head = jnp.where(mask, k, zero)
            d_head = jnp.where(mask, d_mixed, zero)
            which = pair * 2 + head
            for block in range(blocks):
                start, end = block * span, block * span + span
                lse = jnp.sum(
                    jnp.where(lane_ids[start:end] == which, lse_ref[start:end, :], 0.0),
                    axis=-1,
                    keepdims=True,
                )
                scores = matmul_bt(q_head[start:end], k[:end]) + bias_ref[start:end, :end]
                probs = jnp.exp(scores - lse)
                d_probs = matmul_bt(d_head[start:end], v[:end])
                inner = jnp.sum(probs * d_probs, axis=-1, keepdims=True)
                d_scores = (probs * (d_probs - inner)).astype(jnp.bfloat16)
                probs = probs.astype(jnp.bfloat16)
                d_q[block] = d_q[block] + matmul(d_scores, k_head[:end])
                key_term = matmul_at(d_scores, q_head[start:end])
                value_term = matmul_at(probs, d_head[start:end])
                for other in range(block + 1):
                    part = slice(other * span, other * span + span)
                    d_k[other] = d_k[other] + key_term[part]
                    d_v[other] = d_v[other] + value_term[part]
        at_k = slice(width + pair * 128, width + pair * 128 + 128)
        at_v = slice(2 * width + pair * 128, 2 * width + pair * 128 + 128)
        all_ref[:, at] = unturn(jnp.concatenate(d_q, axis=0) * scale)
        all_ref[:, at_k] = unturn(jnp.concatenate(d_k, axis=0))
        all_ref[:, at_v] = jnp.concatenate(d_v, axis=0).astype(jnp.bfloat16)


def back_near_kernel(
    turn_ref,
    dh_own_ref,
    dh_other_ref,
    dg_ref,
    weight_ref,
    one_ref,
    two_ref,
    router_ref,
    resid_ref,
    hidden_two_ref,
    cot_ref,
    gain_ref,
    hidden_ref,
    mixed_ref,
    start_ref,
    cos_ref,
    sin_ref,
    lse_ref,
    w_out_ref,
    q_ref,
    k_ref,
    v_ref,
    wq_ref,
    wk_ref,
    wv_ref,
    d_resid_ref,
    d_proj_ref,
    g_ffn_ref,
    g_router_ref,
    late_ref,
    term_ref,
    bias_ref,
    all_ref,
    dh_ref,
):
    half = dh_own_ref.shape[0]

    @pl.when(turn_ref[0] % 2 == 0)
    def _():
        dh_ref[:half, :] = dh_own_ref[...]
        dh_ref[half:, :] = dh_other_ref[...]

    @pl.when(turn_ref[0] % 2 == 1)
    def _():
        dh_ref[:half, :] = dh_other_ref[...]
        dh_ref[half:, :] = dh_own_ref[...]

    fill_bias(bias_ref, start_ref)
    weight_one, weight_two = (weight_ref[0:1, :], weight_ref[1:2, :])
    d_one, d_two = (dg_ref[0:1, :], dg_ref[1:2, :])
    inner = weight_one * d_one + weight_two * d_two
    d_logits = one_ref[...] * (weight_one * (d_one - inner))
    d_logits = d_logits + two_ref[...] * (weight_two * (d_two - inner))
    d_logits = d_logits.astype(jnp.bfloat16)
    g_router_ref[...] = matmul(d_logits, hidden_two_ref[...])
    d_rows = dh_ref[...].astype(jnp.float32) + matmul_at(d_logits, router_ref[...])
    resid = resid_ref[...]
    scale = rms_scale(resid)
    normed = resid * scale
    g_ffn_ref[...] = jnp.sum(d_rows * normed, axis=0, keepdims=True)
    grown = d_rows * gain_ref[...]
    shift = jnp.mean(grown * normed, axis=-1, keepdims=True)
    d_resid = cot_ref[...].astype(jnp.float32) + scale * (grown - normed * shift)
    d_resid_ref[...] = d_resid
    d_proj_ref[...] = d_resid.astype(jnp.bfloat16)
    piece_gradients(
        d_proj_ref[...],
        w_out_ref[...],
        q_ref,
        k_ref,
        v_ref,
        lse_ref,
        bias_ref,
        cos_ref[...],
        sin_ref[...],
        all_ref,
    )
    piece, width = (w_out_ref.shape[0], q_ref.shape[1])
    grads = matmul_at(all_ref[...], hidden_ref[...]).astype(jnp.bfloat16)
    for i in range(3):
        late_ref[i * piece : (i + 1) * piece, :] = grads[i * width : i * width + piece, :]
    g_out = matmul_at(mixed_ref[...], d_proj_ref[...]).astype(jnp.bfloat16)
    late_ref[3 * piece : 4 * piece, :] = g_out[:piece, :]
    whole = jnp.concatenate([pad_rows(w[...], width) for w in (wq_ref, wk_ref, wv_ref)], axis=0)
    term_ref[...] = matmul(all_ref[...], whole)


def run_back_near(turn, *ins):
    rows, feat = ins[7].shape
    piece = ins[17].shape[0]
    width = padded(piece)
    outs = [
        jax.ShapeDtypeStruct((rows, feat), jnp.float32),
        jax.ShapeDtypeStruct((rows, feat), jnp.bfloat16),
        jax.ShapeDtypeStruct((1, feat), jnp.float32),
        jax.ShapeDtypeStruct((EXPERTS, feat), jnp.float32),
        jax.ShapeDtypeStruct((4 * piece, feat), jnp.bfloat16),
        jax.ShapeDtypeStruct((rows, feat), jnp.float32),
    ]
    return call_whole(
        back_near_kernel,
        "back_near",
        ins,
        outs,
        [
            pltpu.VMEM((rows, rows), jnp.float32),
            pltpu.VMEM((rows, 3 * width), jnp.bfloat16),
            pltpu.VMEM((rows, feat), jnp.bfloat16),
        ],
        rows * width * (16 * feat + 10 * rows),
        rows * rows * piece // HD,
        (turn,),
    )


def back_far_kernel(
    d_proj_ref,
    start_ref,
    cos_ref,
    sin_ref,
    lse_ref,
    w_out_ref,
    q_ref,
    k_ref,
    v_ref,
    all_ref,
    bias_ref,
):
    fill_bias(bias_ref, start_ref)
    piece_gradients(
        d_proj_ref[...],
        w_out_ref[...],
        q_ref,
        k_ref,
        v_ref,
        lse_ref,
        bias_ref,
        cos_ref[...],
        sin_ref[...],
        all_ref,
    )


def run_back_far(*ins):
    rows, feat = ins[0].shape
    piece = ins[5].shape[0]
    width = padded(piece)
    return call_whole(
        back_far_kernel,
        "back_far",
        ins,
        [jax.ShapeDtypeStruct((rows, 3 * width), jnp.bfloat16)],
        [pltpu.VMEM((rows, rows), jnp.float32)],
        rows * width * (2 * feat + 10 * rows),
        rows * rows * piece // HD,
    )[0]


def back_rows_kernel(
    all_ref,
    d_resid_ref,
    term_ref,
    place_own_ref,
    place_other_ref,
    wq_ref,
    wk_ref,
    wv_ref,
    give_ref,
    keep_ref,
    d_half_ref,
    sum_ref,
):
    width = all_ref.shape[1] // 3
    whole = jnp.concatenate([pad_rows(w[...], width) for w in (wq_ref, wk_ref, wv_ref)], axis=0)
    sum_ref[...] = matmul(all_ref[...], whole)
    total = (term_ref[...] + sum_ref[...]).astype(jnp.bfloat16)
    give_ref[...] = matmul_at(place_other_ref[...], total).astype(jnp.bfloat16)
    keep_ref[...] = matmul_at(place_own_ref[...], total).astype(jnp.bfloat16)
    d_resid = d_resid_ref[...]
    high = d_resid.astype(jnp.bfloat16)
    low = (d_resid - high.astype(jnp.float32)).astype(jnp.bfloat16)
    d_half_ref[...] = matmul_at(place_own_ref[...], high) + matmul_at(place_own_ref[...], low)


def run_back_rows(*ins):
    rows, width = ins[0].shape
    feat = ins[1].shape[1]
    half = ins[3].shape[1]
    outs = [
        jax.ShapeDtypeStruct((half, feat), jnp.bfloat16),
        jax.ShapeDtypeStruct((half, feat), jnp.bfloat16),
        jax.ShapeDtypeStruct((half, feat), jnp.float32),
    ]
    return call_whole(
        back_rows_kernel,
        "back_rows",
        ins,
        outs,
        [pltpu.VMEM((rows, feat), jnp.float32)],
        2 * rows * width * feat + 8 * rows * half * feat,
    )


def body(
    tokens,
    order,
    lengths,
    routes,
    attn_gain,
    w_query,
    w_key,
    w_value,
    w_out,
    ffn_gain,
    w_router,
    shared_gate,
    shared_up,
    shared_down,
    expert_gate,
    expert_up,
    expert_down,
    cotangent,
):
    row_count, feat_width = tokens.shape
    group_count = lax.axis_size("expert")
    share_rows = row_count // group_count
    half_share = share_rows // 2
    half_rows = row_count // 2
    my_group = lax.axis_index("expert")
    my_tensor = lax.axis_index("tensor")
    bit_low = lax.rem(my_tensor, 2)
    bit_high = my_tensor // 2
    slab_dev = expert_gate.shape[0]
    slab_total = slab_dev * group_count
    replicas = max(1, slab_total // EXPERTS)
    half_slots = slab_dev * CAP // 2
    row_ids = jnp.arange(row_count, dtype=jnp.int32)
    earlier = (row_ids[:, None] < row_ids[None, :]).astype(jnp.bfloat16)

    local_order = lax.dynamic_slice_in_dim(order, my_group * row_count, row_count, 0)
    groups = jnp.arange(group_count, dtype=jnp.int32)
    dest_group = local_order // row_count
    dest_onehot = (groups[:, None] == dest_group[None, :]).astype(jnp.bfloat16)
    dest_before = matmul(dest_onehot, earlier)
    send_rank = jnp.sum(dest_onehot.astype(jnp.float32) * dest_before, axis=0).astype(jnp.int32)
    send_half = send_rank // half_share
    send_slot = send_half * half_rows + dest_group * half_share + send_rank % half_share
    send_pick = send_slot[None, :] == (
        bit_low * half_rows + jnp.arange(half_rows, dtype=jnp.int32)[:, None]
    )
    send_pick = send_pick.astype(jnp.bfloat16)
    in_tokens = exchange(select(send_pick, tokens))
    cot_send, in_tokens = tie(select(send_pick, cotangent), in_tokens)
    in_cot = exchange(cot_send)

    near_weights = (w_query.T, w_key.T, w_value.T)
    far_weights = tuple(far_swap(weight) for weight in near_weights)
    out_far = far_swap(after(w_out, far_weights[1]))
    tokens_other = core_swap(in_tokens)
    turn = my_tensor.reshape(1)

    all_order = order.reshape(group_count, row_count)
    mine = all_order // row_count == my_group
    arrive_rank = matmul(mine.astype(jnp.bfloat16), earlier).astype(jnp.int32)
    arrive_rank = jnp.where(mine, arrive_rank, -1)
    landing = all_order - my_group * row_count
    target = jnp.sum(
        jnp.where(
            arrive_rank[:, None, :] == jnp.arange(share_rows, dtype=jnp.int32)[None, :, None],
            landing[:, None, :],
            0,
        ),
        axis=-1,
    )
    target = target.reshape(group_count, 2, half_share).transpose(1, 0, 2).reshape(2, half_rows)
    target_own = lax.dynamic_index_in_dim(target, bit_low, 0, keepdims=False)
    target_other = lax.dynamic_index_in_dim(target, 1 - bit_low, 0, keepdims=False)
    place_own = (row_ids[:, None] == target_own[None, :]).astype(jnp.bfloat16)
    place_other = (row_ids[:, None] == target_other[None, :]).astype(jnp.bfloat16)

    expert_ids = jnp.arange(EXPERTS, dtype=jnp.int32)
    member_one = expert_ids[:, None] == routes[None, :, 0]
    member_two = expert_ids[:, None] == routes[None, :, 1]
    member = member_one | member_two
    slot_rank = matmul(member.astype(jnp.bfloat16), earlier).astype(jnp.int32)
    slot_rank = jnp.where(member, slot_rank, -1)

    block = (half_slots + 16) // 16 * 16
    ranks = jnp.repeat(slot_rank, replicas, axis=0).reshape(group_count, slab_dev, row_count)
    ranks = lax.dynamic_index_in_dim(ranks, bit_low * half_slots // CAP, 1, keepdims=False)
    slot_ids = jnp.arange(block, dtype=jnp.int32)
    slots = bit_low * half_slots % CAP + slot_ids
    slots = jnp.where(slot_ids < half_slots, slots, -2)
    slots_cube = (ranks[:, None, :] == slots[None, :, None]).astype(jnp.bfloat16)
    slots_one = slots_cube.reshape(group_count * block, row_count)

    quarter = block // 2
    slots_part = lax.dynamic_slice_in_dim(slots_cube, bit_high * quarter, quarter, 1)
    slots_part = slots_part.reshape(-1, row_count)
    cot_pick_own = select(slots_part, place_own)
    cot_pick_other = select(slots_part, place_other)

    seq_lengths = lengths[0]
    seq_ends = jnp.cumsum(seq_lengths)
    passed = row_ids[:, None] >= seq_ends[None, :]
    sequence_segment = jnp.sum(passed.astype(jnp.int32), axis=1)
    position = row_ids - jnp.sum(jnp.where(passed, seq_lengths[None, :], 0), axis=1)
    half_size = HD // 2
    lanes = jnp.arange(128, dtype=jnp.int32)
    frequency = ROPE_BASE ** (-(lanes % half_size).astype(jnp.float32) / half_size)
    angles = position.astype(jnp.float32)[:, None] * frequency[None, :]
    cos_table = jnp.cos(angles)
    sin_table = jnp.where(lanes % HD < half_size, -1.0, 1.0) * jnp.sin(angles)
    seq_start = jnp.broadcast_to((row_ids - position)[:, None], (row_count, 128))
    gain_one = attn_gain.astype(jnp.float32)[None, :]
    gain_two = ffn_gain.astype(jnp.float32)[None, :]
    tables = (cos_table, sin_table, seq_start)
    grouped, hidden_one, *near_heads, near_mixed, near_lse = run_attention(
        True,
        (in_tokens, tokens_other, place_own, place_other, gain_one, *near_weights, *tables),
    )
    near_swapped = core_swap(near_mixed)
    far_weights = after(far_weights, near_mixed)
    *far_heads, far_mixed, far_lse = run_attention(False, (hidden_one, *far_weights, *tables))
    far_swapped = core_swap(far_mixed)
    out_pieces = (w_out, core_swap(w_out), out_far, core_swap(out_far))
    in_cot = after(in_cot, far_mixed)
    cot_half = core_swap(in_cot)
    cot_part = matmul(cot_pick_own, in_cot) + matmul(cot_pick_other, cot_half)
    cot_part = cot_part.astype(jnp.bfloat16)
    far_swapped = after(far_swapped, cot_part)
    cot_part = exchange(cot_part)

    dest_slab = jnp.arange(group_count, dtype=jnp.int32) * slab_dev + bit_low * half_slots // CAP
    dest_expert = dest_slab // replicas
    first_here = (routes[None, :, 0] == dest_expert[:, None]).astype(jnp.float32)
    second_here = (routes[None, :, 1] == dest_expert[:, None]).astype(jnp.float32)
    one_of = member_one.astype(jnp.float32)
    two_of = member_two.astype(jnp.float32)
    router_rows = w_router.T
    resid_two, hidden_two, sent, gate_weights = run_middle(
        half_slots,
        block,
        turn,
        near_mixed,
        near_swapped,
        far_mixed,
        far_swapped,
        grouped,
        *out_pieces,
        gain_two,
        router_rows,
        slots_one,
        one_of,
        two_of,
        first_here,
        second_here,
    )
    hidden_rows = exchange(after(sent, cot_part))
    cot_part = cot_part.reshape(group_count, quarter, feat_width)
    cot_own = in_order(bit_high, cot_part, far_swap(cot_part), 1).reshape(-1, feat_width)
    cot_other = core_swap(cot_own)
    grouped_cot = matmul(place_own, after(in_cot, sent)) + matmul(place_other, cot_half)
    grouped_cot = grouped_cot.astype(jnp.bfloat16)
    hidden_late = after(hidden_two, cot_part)

    gate_shared = matmul(hidden_two, shared_gate)
    up_shared = matmul(hidden_late, shared_up)
    act_shared = silu_value(gate_shared)
    shared_mid = (act_shared * up_shared).astype(jnp.bfloat16)
    shared_out = matmul(shared_mid, shared_down)
    d_mid_shared = matmul_bt(grouped_cot, shared_down)
    d_up_shared = (d_mid_shared * act_shared).astype(jnp.bfloat16)
    d_gate_shared = (d_mid_shared * up_shared * silu_slope(gate_shared)).astype(jnp.bfloat16)
    d_both = jnp.concatenate([d_gate_shared, d_up_shared], axis=1)
    early = GroupSum(
        jnp.concatenate([matmul_at(d_both, hidden_late), matmul_at(shared_mid, grouped_cot)], axis=0)
    )
    early.start()
    d_gate_shared, d_up_shared, shared_out, resid_late, _ = tie(
        d_gate_shared, d_up_shared, shared_out, resid_two, early.given
    )
    d_hidden_shared = matmul_bt(d_gate_shared, shared_gate) + matmul_bt(d_up_shared, shared_up)
    shared_send = shared_out.astype(jnp.bfloat16)
    shared_own = matmul_at(place_own, shared_send)
    shared_other = matmul_at(place_other, shared_send)
    resid_high, resid_low = three_parts(resid_late)[:2]
    resid_half = matmul_at(place_own, resid_high) + matmul_at(place_own, resid_low)
    hidden_rows = after(
        hidden_rows, cot_other, d_hidden_shared, shared_own, shared_other, resid_half
    )
    rows_other = core_swap(hidden_rows)
    early.end(d_hidden_shared, shared_own, shared_other, resid_half)
    early.start()
    rows_other = after(rows_other, early.given)

    which_own = (bit_low * half_slots // CAP).reshape(1)
    which_other = ((1 - bit_low) * half_slots // CAP).reshape(1)
    weights_here = (expert_gate, expert_up, expert_down, half_slots, block)
    back_given, out_given, mid_other, dg_other, du_other = run_expert(
        which_other, rows_other, cot_other, *weights_here
    )
    early.end(back_given)
    early.start()
    back_given = after(back_given, early.given)
    hidden_rows = after(hidden_rows, back_given)
    back_kept, out_kept, mid_own, dg_own, du_own = run_expert(
        which_own, hidden_rows, cot_own, *weights_here
    )
    stack_own = (hidden_rows, cot_own, mid_own, dg_own, du_own)
    stack_other = (rows_other, cot_other, mid_other, dg_other, du_other)

    back_sum = back_kept.astype(jnp.float32) + core_swap(back_given).astype(jnp.float32)
    back_sum = back_sum.reshape(group_count, block, feat_width)
    lines = back_sum[:, half_slots, :384].reshape(group_count, 3, 128)
    lines = jnp.stack(three_parts(jnp.sum(lines, axis=1)), axis=1).astype(jnp.float32)
    lines = jnp.pad(lines.reshape(group_count, 1, 384), ((0, 0), (0, 0), (0, feat_width - 384)))
    back_sum = jnp.where(slot_ids[None, :, None] == half_slots, lines, back_sum)
    back_send = back_sum.astype(jnp.bfloat16).reshape(-1, feat_width)
    back_own = exchange(back_send)
    early.end(back_send)
    while early.stage < early.bits:
        early.start()
        early.end()
    out_sum = pair_sum(out_kept, after(out_given, back_send, early.part))
    out_sum = out_sum.reshape(group_count, block, feat_width)
    out_kept = lax.dynamic_slice_in_dim(out_sum, bit_high * quarter, quarter, 1)
    out_given = lax.dynamic_slice_in_dim(out_sum, (1 - bit_high) * quarter, quarter, 1)
    out_send = out_kept.astype(jnp.float32) + far_swap(out_given).astype(jnp.float32)
    out_send = out_send.astype(jnp.bfloat16).reshape(-1, feat_width)
    if slab_dev == 2:
        own_late = after(stack_own[0], out_given)
        stack_own = (own_late,) + stack_own[1:]
        g_expert_gate, g_expert_up, g_expert_down = run_weights(bit_low, stack_own, stack_other)
    else:
        wide = [jnp.concatenate(pair, axis=0) for pair in zip(stack_own, stack_other)]
        g_expert_gate = matmul_at(wide[0], wide[3])[None]
        g_expert_up = matmul_at(wide[0], wide[4])[None]
        g_expert_down = matmul_at(wide[2], wide[1])[None]


    halves = [
        tuple(
            lax.dynamic_slice_in_dim(values, bit * half_rows, half_rows, axis)
            for values, axis in ((slots_one, 1), (d_hidden_shared, 0))
        )
        for bit in (1 - bit_low, bit_low)
    ]
    back_own, *halves = tie(back_own, *halves, g_expert_gate, out_send)[:3]
    given, kept = (
        (matmul_at(slots, back_own) + shared).astype(jnp.bfloat16) for slots, shared in halves
    )
    kept = after(kept, given)
    dg_lines = back_own.reshape(group_count, block, feat_width)[:, half_slots, :384]
    dg_lines = dg_lines.reshape(group_count, 3, 128)[:, :, :block]
    dg_of = jnp.einsum("dps,dsr->dpr", dg_lines, slots_cube, preferred_element_type=jnp.float32)
    dg_of = jnp.sum(dg_of, axis=1)
    dg_part = jnp.stack(
        [jnp.sum(first_here * dg_of, axis=0), jnp.sum(second_here * dg_of, axis=0)], axis=0
    )
    dg_part = jnp.pad(dg_part, ((0, 6), (0, 0)))
    dg_part = dg_part + core_swap(dg_part)
    pair = pair_sum(kept, given)
    early.start(pair)
    far, early.came, dg_far = tie(far_swap(pair), early.came, far_swap(dg_part))
    d_hidden_half = (pair.astype(jnp.float32) + far.astype(jnp.float32)).astype(jnp.bfloat16)
    early.end(d_hidden_half)
    out_own = exchange(after(out_send, d_hidden_half))
    d_hidden_other = core_swap(d_hidden_half)
    dg_part = dg_part + dg_far
    d_resid, d_proj, g_ffn_gain, g_router, late, term = run_back_near(
        turn,
        d_hidden_half,
        d_hidden_other,
        dg_part,
        gate_weights,
        one_of,
        two_of,
        router_rows,
        resid_two,
        hidden_two,
        grouped_cot,
        gain_two,
        hidden_one,
        near_mixed,
        seq_start,
        cos_table,
        sin_table,
        near_lse,
        w_out,
        *near_heads,
        *near_weights,
    )
    early.start(d_proj)
    late = GroupSum(late, True)
    late.start()
    ffn_rows = after(out_own, late.given)
    ffn_given = (matmul_at(cot_pick_other, ffn_rows) + shared_other).astype(jnp.bfloat16)
    ffn_kept = (matmul_at(cot_pick_own, ffn_rows) + shared_own).astype(jnp.bfloat16)
    ffn_pair = pair_sum(ffn_kept, ffn_given)
    ffn_half = ffn_pair.astype(jnp.float32) + far_swap(ffn_pair).astype(jnp.float32)
    output_send = (resid_half + ffn_half).astype(jnp.bfloat16)
    far_all = run_back_far(
        after(d_proj, ffn_pair),
        seq_start,
        cos_table,
        sin_table,
        far_lse,
        out_far,
        *far_heads,
    )
    late.end(far_all)
    late.start()
    early.end(far_all)
    early.start_first(4)
    d_one_given, d_one_kept, d_resid_half = run_back_rows(
        after(far_all, output_send, late.given),
        d_resid,
        term,
        place_own,
        place_other,
        *far_weights,
    )
    late.end(d_one_given)
    late.start()
    early.first, d_one_given = tie(early.first, d_one_given)
    d_one = d_one_kept.astype(jnp.float32) + core_swap(d_one_given).astype(jnp.float32)
    resid = in_tokens.astype(jnp.float32)
    scale_one = rms_scale(resid)
    normed_one = resid * scale_one
    e_one = d_one * gain_one
    shift_one = jnp.mean(e_one * normed_one, axis=-1, keepdims=True)
    d_tokens_send = (d_resid_half + scale_one * (e_one - normed_one * shift_one)).astype(jnp.bfloat16)
    g_attn_gain = jnp.sum(d_one * normed_one, axis=0, keepdims=True)
    both_send = jnp.concatenate(
        [
            d_tokens_send.reshape(group_count, half_share, feat_width),
            output_send.reshape(group_count, half_share, feat_width),
        ],
        axis=1,
    )
    small = jnp.concatenate([g_router, g_ffn_gain, g_attn_gain + core_swap(g_attn_gain)], axis=0)
    small = jnp.pad(small, ((0, -small.shape[0] % 8), (0, 0)))
    small = small + group_swap(small, 0)
    early.start_second(small)
    late.came, both_send, small_came = tie(late.came, both_send, group_swap(small, 1))
    small = small + small_came
    late.end()
    late.start()
    late.came, small_came = tie(late.came, group_swap(small, 2))
    small = small + small_came
    for step in range(3, group_count.bit_length() - 1):
        small = small + group_swap(small, step)
    late.end()
    both_own = exchange(after(both_send, late.part))
    late.start()
    early.end_second(late.part)
    g_router = small[:EXPERTS].T
    g_ffn_gain = small[EXPERTS]
    g_attn_gain = small[EXPERTS + 1]
    late = late.finish().astype(jnp.float32)
    shared = early.finish(late).astype(jnp.float32)
    hidden_s = shared_gate.shape[1]
    g_shared_gate = shared[:hidden_s].T
    g_shared_up = shared[hidden_s : 2 * hidden_s].T
    g_shared_down = shared[2 * hidden_s :]
    head_rows = w_out.shape[0]
    g_query = late[:head_rows].T
    g_key = late[head_rows : 2 * head_rows].T
    g_value = late[2 * head_rows : 3 * head_rows].T
    g_out = late[3 * head_rows :]
    both_own = after(
        both_own, g_query, g_key, g_value, g_out, g_shared_gate, g_shared_up, g_shared_down, small
    )
    both_other = core_swap(both_own)

    unsend = (send_slot[:, None] == row_ids[None, :]).astype(jnp.bfloat16)

    def arrive_back(part):
        own = both_own[:, part].reshape(half_rows, feat_width)
        other = both_other[:, part].reshape(half_rows, feat_width)
        return select(unsend, in_order(bit_low, own, other))

    d_tokens = arrive_back(slice(0, half_share))
    output = arrive_back(slice(half_share, 2 * half_share))
    return (
        output,
        d_tokens,
        g_attn_gain,
        g_query,
        g_key,
        g_value,
        g_out,
        g_ffn_gain,
        g_router,
        g_shared_gate,
        g_shared_up,
        g_shared_down,
        g_expert_gate,
        g_expert_up,
        g_expert_down,
    )


def solution(mesh):
    return jax.shard_map(
        body,
        mesh=mesh,
        in_specs=(
            P("expert", None),
            P(),
            P("expert", None),
            P("expert", None),
            P(),
            P(None, "tensor"),
            P(None, "tensor"),
            P(None, "tensor"),
            P("tensor", None),
            P(),
            P(),
            P(None, "tensor"),
            P(None, "tensor"),
            P("tensor", None),
            P("expert", None, "tensor"),
            P("expert", None, "tensor"),
            P("expert", "tensor", None),
            P("expert", None),
        ),
        out_specs=(
            P("expert", None),
            P("expert", None),
            P(),
            P(None, "tensor"),
            P(None, "tensor"),
            P(None, "tensor"),
            P("tensor", None),
            P(),
            P(),
            P(None, "tensor"),
            P(None, "tensor"),
            P("tensor", None),
            P("expert", None, "tensor"),
            P("expert", None, "tensor"),
            P("expert", "tensor", None),
        ),
        check_vma=False,
    )
```

```python
import functools

import jax
import jax.numpy as jnp
from jax import lax
from jax.experimental import pallas as pl
from jax.experimental.pallas import tpu as pltpu
from jax.sharding import PartitionSpec as P

HD = 64
EXPERTS = 16
CAP = 120


EPSILON = 1e-05
ROPE_BASE = 10000.0
MASKED = -1e30


def rms_scale(values):
    return lax.rsqrt(jnp.mean(values * values, axis=-1, keepdims=True) + EPSILON)


def matmul(left_side, right_side):
    return jnp.dot(left_side, right_side, preferred_element_type=jnp.float32)


def matmul_bt(left_side, right_side):
    return lax.dot_general(
        left_side, right_side, (((1,), (1,)), ((), ())), preferred_element_type=jnp.float32
    )


def matmul_at(left_side, right_side):
    return lax.dot_general(
        left_side, right_side, (((0,), (0,)), ((), ())), preferred_element_type=jnp.float32
    )


def silu_value(gate_in):
    return gate_in * jax.nn.sigmoid(gate_in)


def silu_slope(gate_in):
    sigma = jax.nn.sigmoid(gate_in)
    return sigma * (1.0 + gate_in * (1.0 - sigma))


def tie(*values):
    return lax.optimization_barrier(values)


def core_swap(values):
    return lax.ppermute(values, "tensor", [(i, i ^ 1) for i in range(4)])


def far_swap(values):
    return lax.ppermute(values, "tensor", [(i, i ^ 2) for i in range(4)])


def exchange(values):
    return lax.all_to_all(values, "expert", split_axis=0, concat_axis=0, tiled=True)


def in_order(bit, own, other, axis=0):
    return jnp.where(
        bit == 0,
        jnp.concatenate([own, other], axis=axis),
        jnp.concatenate([other, own], axis=axis),
    )


def gather_four(bit_low, bit_high, own, axis):
    far = far_swap(own)
    near = core_swap(own)
    far_near = core_swap(far)
    here = in_order(bit_low, own, near, axis)
    there = in_order(bit_low, far, far_near, axis)
    return in_order(bit_high, here, there, axis)


def select(onehot, values):
    return jnp.dot(onehot, values, preferred_element_type=jnp.float32).astype(jnp.bfloat16)


def pair_sum(kept, given):
    return (kept.astype(jnp.float32) + core_swap(given).astype(jnp.float32)).astype(jnp.bfloat16)


def after(values, *anchors):
    return lax.optimization_barrier((values, *anchors))[0]


def group_swap(values, step):
    size = lax.axis_size("expert")
    return lax.ppermute(values, "expert", [(i, i ^ (1 << step)) for i in range(size)])


class GroupSum:
    def __init__(self, values, whole_last=False):
        self.bits = lax.axis_size("expert").bit_length() - 1
        self.steps = list(range(self.bits)) + list(reversed(range(self.bits)))
        if whole_last:
            self.steps[self.bits - 1 : self.bits + 1] = [self.bits - 1]
        self.halvings = self.bits - 1 if whole_last else self.bits
        self.whole_last = whole_last
        self.me = lax.axis_index("expert")
        self.shape = values.shape
        pieces = 1 << self.halvings
        self.part = values.astype(jnp.bfloat16).reshape(pieces, -1, values.shape[1])
        self.stage = 0
        self.pending = False
        self.prepare()

    def prepare(self):
        if self.stage < self.halvings:
            bit = (self.me >> self.stage) & 1
            pairs = self.part.reshape((-1, 2) + self.part.shape[1:])
            self.kept = lax.dynamic_index_in_dim(pairs, bit, 1, keepdims=False)
            self.given = lax.dynamic_index_in_dim(pairs, 1 - bit, 1, keepdims=False)
        else:
            self.kept = self.given = self.part

    def start_first(self, share):
        self.cut = self.given.shape[1] // share
        self.first = group_swap(self.given[:, : self.cut], self.steps[self.stage])

    def start_second(self, *anchors):
        self.first, second = tie(self.first, self.given[:, self.cut :], *anchors)[:2]
        self.second = group_swap(second, self.steps[self.stage])

    def end_second(self, *anchors):
        self.came = jnp.concatenate([self.first, after(self.second, *anchors)], axis=1)
        self.end()

    def done(self):
        return self.stage == len(self.steps)

    def start(self, *anchors):
        self.pending = True
        self.came = group_swap(after(self.given, *anchors), self.steps[self.stage])

    def end(self, *anchors):
        came = after(self.came, *anchors)
        self.pending = False
        if self.stage < self.bits:
            total = self.kept.astype(jnp.float32) + came.astype(jnp.float32)
            self.part = total.astype(jnp.bfloat16)
        else:
            bit = (self.me >> self.steps[self.stage]) & 1
            both = in_order(bit, self.part[:, None], came[:, None], 1)
            self.part = both.reshape((-1,) + self.part.shape[1:])
        self.stage += 1
        if not self.done():
            self.prepare()

    def finish(self, *anchors):
        while not self.done():
            if not self.pending:
                self.start()
            self.end(*anchors)
        return self.part.reshape(self.shape)


def three_parts(values):
    high = lax.reduce_precision(values, 8, 7)
    rest = values - high
    middle = lax.reduce_precision(rest, 8, 7)
    return [part.astype(jnp.bfloat16) for part in (high, middle, rest - middle)]


def expert_kernel(
    half_slots,
    block,
    which_ref,
    rows_ref,
    cot_ref,
    gate_ref,
    up_ref,
    down_ref,
    back_ref,
    out_ref,
    mid_ref,
    d_gate_ref,
    d_up_ref,
):
    rows = rows_ref[...]
    count = rows.shape[0]
    gate_w, up_w, down_w = (gate_ref[0], up_ref[0], down_ref[0])
    gate_lin = matmul(rows, gate_w)
    up_lin = matmul(rows, up_w)
    raw = matmul_bt(cot_ref[...], down_w)
    sigma = 1.0 / (1.0 + jnp.exp(-gate_lin))
    act = gate_lin * sigma
    mid = act * up_lin
    scalar = jnp.sum(raw * mid, axis=1, keepdims=True)
    lanes = lax.broadcasted_iota(jnp.int32, (block, 128), 1)
    subs = lax.broadcasted_iota(jnp.int32, (block, 128), 0)
    diagonal = (lanes == subs) & (lanes < half_slots)
    last = 16
    at = half_slots - (block - last)
    sub_last = lax.broadcasted_iota(jnp.int32, (last, 128), 0)
    gates = []
    for b in range(count // block):
        tail = rows_ref[(b + 1) * block - last : (b + 1) * block, 0:384].astype(jnp.float32)
        total = tail[:, 0:128] + tail[:, 128:256] + tail[:, 256:384]
        line = jnp.sum(jnp.where(sub_last == at, total, 0.0), axis=0, keepdims=True)
        gates.append(jnp.sum(jnp.where(diagonal, line, 0.0), axis=1, keepdims=True))
    gate = jnp.concatenate(gates, axis=0) if len(gates) > 1 else gates[0]
    d_act = raw * gate
    d_up = (d_act * act).astype(jnp.bfloat16)
    d_gate = (d_act * up_lin * (sigma * (1.0 + gate_lin * (1.0 - sigma)))).astype(jnp.bfloat16)
    mid_g = (mid * gate).astype(jnp.bfloat16)
    mid_ref[...] = mid_g
    d_gate_ref[...] = d_gate
    d_up_ref[...] = d_up
    back = matmul_bt(d_gate, gate_w) + matmul_bt(d_up, up_w)
    back_ref[...] = back.astype(jnp.bfloat16)
    for b in range(count // block):
        part = jnp.where(diagonal, scalar[b * block : (b + 1) * block], 0.0)
        line = jnp.sum(part, axis=0, keepdims=True)
        high = line.astype(jnp.bfloat16).astype(jnp.float32)
        rest = line - high
        middle = rest.astype(jnp.bfloat16).astype(jnp.float32)
        for i, piece in enumerate((high, middle, rest - middle)):
            old = back[(b + 1) * block - last : (b + 1) * block, i * 128 : (i + 1) * 128]
            back_ref[(b + 1) * block - last : (b + 1) * block, i * 128 : (i + 1) * 128] = jnp.where(
                sub_last == at, piece, old
            ).astype(jnp.bfloat16)
    out_ref[...] = matmul(mid_g, down_w).astype(jnp.bfloat16)


def run_expert(which, rows, cots, gate_w, up_w, down_w, half_slots, block):
    count, feat = rows.shape
    hidden = gate_w.shape[2]
    step_rows = min(256, count)
    row_spec = pl.BlockSpec((step_rows, feat), lambda i, w: (i, 0))
    mid_spec = pl.BlockSpec((step_rows, hidden), lambda i, w: (i, 0))
    return pl.pallas_call(
        functools.partial(expert_kernel, half_slots, block),
        grid_spec=pltpu.PrefetchScalarGridSpec(
            num_scalar_prefetch=1,
            grid=(count // step_rows,),
            in_specs=[
                row_spec,
                row_spec,
                pl.BlockSpec((1, feat, hidden), lambda i, w: (w[0], 0, 0)),
                pl.BlockSpec((1, feat, hidden), lambda i, w: (w[0], 0, 0)),
                pl.BlockSpec((1, hidden, feat), lambda i, w: (w[0], 0, 0)),
            ],
            out_specs=[row_spec, row_spec, mid_spec, mid_spec, mid_spec],
        ),
        out_shape=[jax.ShapeDtypeStruct((count, feat), jnp.bfloat16)] * 2
        + [jax.ShapeDtypeStruct((count, hidden), jnp.bfloat16)] * 3,
        compiler_params=pltpu.CompilerParams(vmem_limit_bytes=50 << 20),
        cost_estimate=pl.CostEstimate(
            flops=12 * count * feat * hidden,
            bytes_accessed=8 * count * feat + 6 * feat * hidden + 6 * count * hidden,
            transcendentals=count * hidden,
        ),
        name="expert_rows",
    )(which, rows, cots, gate_w, up_w, down_w)


def weight_kernel(
    which_ref,
    rows_own,
    rows_other,
    cot_own,
    cot_other,
    mid_own,
    mid_other,
    dg_own,
    dg_other,
    du_own,
    du_other,
    g_gate_ref,
    g_up_ref,
    g_down_ref,
):
    def fill(rows, cots, mid, d_gate, d_up):
        turned = rows[...].T
        g_gate_ref[0] = matmul(turned, d_gate[...])
        g_up_ref[0] = matmul(turned, d_up[...])
        g_down_ref[0] = matmul_at(mid[...], cots[...])

    @pl.when(pl.program_id(0) == 0)
    def _():
        fill(rows_own, cot_own, mid_own, dg_own, du_own)

    @pl.when(pl.program_id(0) == 1)
    def _():
        fill(rows_other, cot_other, mid_other, dg_other, du_other)


def run_weights(bit_low, own, other):
    count, feat = own[0].shape
    hidden = own[2].shape[1]
    width = min(256, hidden)
    whole = pl.BlockSpec((count, feat), lambda s, j, w: (0, 0))
    first = pl.BlockSpec((count, width), lambda s, j, w: (0, jnp.where(s == 0, j, 0)))
    second = pl.BlockSpec((count, width), lambda s, j, w: (0, jnp.where(s == 1, j, 0)))

    def slab(s, w):
        return jnp.where(s == 0, w[0], 1 - w[0])

    wide = pl.BlockSpec((1, feat, width), lambda s, j, w: (slab(s, w), 0, j))
    tall = pl.BlockSpec((1, width, feat), lambda s, j, w: (slab(s, w), j, 0))
    return pl.pallas_call(
        weight_kernel,
        grid_spec=pltpu.PrefetchScalarGridSpec(
            num_scalar_prefetch=1,
            grid=(2, hidden // width),
            in_specs=[whole, whole, whole, whole, first, second, first, second, first, second],
            out_specs=[wide, wide, tall],
        ),
        out_shape=[
            jax.ShapeDtypeStruct((2, feat, hidden), jnp.float32),
            jax.ShapeDtypeStruct((2, feat, hidden), jnp.float32),
            jax.ShapeDtypeStruct((2, hidden, feat), jnp.float32),
        ],
        compiler_params=pltpu.CompilerParams(vmem_limit_bytes=56 << 20),
        cost_estimate=pl.CostEstimate(
            flops=12 * count * feat * hidden,
            bytes_accessed=8 * count * feat + 12 * count * hidden + 24 * feat * hidden,
            transcendentals=0,
        ),
        name="expert_weights",
    )(
        bit_low.reshape(1),
        own[0],
        other[0],
        own[1],
        other[1],
        own[2],
        other[2],
        own[3],
        other[3],
        own[4],
        other[4],
    )


def swap_halves(values):
    lanes = lax.broadcasted_iota(jnp.int32, values.shape, 1)
    return jnp.where(lanes % HD < HD // 2, pltpu.roll(values, 96, 1), pltpu.roll(values, 32, 1))


def fill_bias(bias_ref, start_ref):
    rows = bias_ref.shape[0]
    row_at = lax.broadcasted_iota(jnp.int32, (rows, 128), 0)
    lane_at = lax.broadcasted_iota(jnp.int32, (rows, 128), 1)
    start = start_ref[...]
    for part in range(rows // 128):
        key_at = lane_at + part * 128
        allowed = (key_at >= start) & (key_at <= row_at)
        bias_ref[:, part * 128 : part * 128 + 128] = jnp.where(allowed, 0.0, MASKED)


def fixed(shape):
    return pl.BlockSpec(shape, lambda *_: tuple(0 for _ in shape))


def pad_rows(piece, rows):
    return jnp.concatenate([piece, jnp.zeros((rows - piece.shape[0], piece.shape[1]), piece.dtype)], 0)


def heads_of(piece_rows, pair):
    return min(2, (piece_rows - pair * 128) // HD)


def attend_piece(hidden, weights, cos, sin, bias_ref, outs):
    q_ref, k_ref, v_ref, mixed_ref, lse_ref = outs
    rows = hidden.shape[0]
    width = q_ref.shape[1]
    span = 256
    lane_ids = lax.broadcasted_iota(jnp.int32, (rows, 128), 1)
    lse_ref[...] = jnp.zeros_like(lse_ref)
    linear = matmul_bt(
        hidden, jnp.concatenate([pad_rows(weight[...], width) for weight in weights], axis=0)
    )
    for pair in range(width // 128):
        at = slice(pair * 128, pair * 128 + 128)
        q_lin = linear[:, pair * 128 : pair * 128 + 128]
        k_lin = linear[:, width + pair * 128 : width + pair * 128 + 128]
        v_pair = linear[:, 2 * width + pair * 128 : 2 * width + pair * 128 + 128]
        v_pair = v_pair.astype(jnp.bfloat16)
        q_pair = (q_lin * cos + swap_halves(q_lin) * sin).astype(jnp.bfloat16)
        k_pair = (k_lin * cos + swap_halves(k_lin) * sin).astype(jnp.bfloat16)
        q_ref[:, at] = q_pair
        k_ref[:, at] = k_pair
        v_ref[:, at] = v_pair
        q_scaled = q_pair * jnp.bfloat16(HD ** (-0.5))
        zero = jnp.zeros_like(q_scaled)
        q_heads = [jnp.where(lane_ids < HD, q_scaled, zero), jnp.where(lane_ids < HD, zero, q_scaled)]
        q_heads = q_heads[: heads_of(weights[0].shape[0], pair)]
        for start in range(0, rows, span):
            end = start + span
            ids = lane_ids[start:end]
            mixed = None
            for head, q_head in enumerate(q_heads):
                scores = matmul_bt(q_head[start:end], k_pair[:end]) + bias_ref[start:end, :end]
                top = jnp.max(scores, axis=-1, keepdims=True)
                raised = jnp.exp(scores - top)
                total = jnp.sum(raised, axis=-1, keepdims=True)
                out = matmul(raised.astype(jnp.bfloat16), v_pair[:end]) / total
                mixed = out if mixed is None else jnp.where(ids < HD, mixed, out)
                lse = top + jnp.log(total)
                lse_ref[start:end, :] = jnp.where(
                    ids == pair * 2 + head, lse, lse_ref[start:end, :]
                )
            mixed_ref[start:end, at] = mixed.astype(jnp.bfloat16)


def attention_near_kernel(
    own_ref,
    other_ref,
    place_own_ref,
    place_other_ref,
    gain_ref,
    wq_ref,
    wk_ref,
    wv_ref,
    cos_ref,
    sin_ref,
    start_ref,
    grouped_ref,
    hidden_ref,
    q_ref,
    k_ref,
    v_ref,
    mixed_ref,
    lse_ref,
    bias_ref,
):
    fill_bias(bias_ref, start_ref)
    placed = matmul(place_own_ref[...], own_ref[...])
    placed = placed + matmul(place_other_ref[...], other_ref[...])
    grouped_ref[...] = placed.astype(jnp.bfloat16)
    hidden_ref[...] = (placed * rms_scale(placed) * gain_ref[...]).astype(jnp.bfloat16)
    attend_piece(
        hidden_ref[...],
        (wq_ref, wk_ref, wv_ref),
        cos_ref[...],
        sin_ref[...],
        bias_ref,
        (q_ref, k_ref, v_ref, mixed_ref, lse_ref),
    )


def attention_far_kernel(
    hidden_ref,
    wq_ref,
    wk_ref,
    wv_ref,
    cos_ref,
    sin_ref,
    start_ref,
    q_ref,
    k_ref,
    v_ref,
    mixed_ref,
    lse_ref,
    bias_ref,
):
    fill_bias(bias_ref, start_ref)
    attend_piece(
        hidden_ref[...],
        (wq_ref, wk_ref, wv_ref),
        cos_ref[...],
        sin_ref[...],
        bias_ref,
        (q_ref, k_ref, v_ref, mixed_ref, lse_ref),
    )


def call_whole(kernel, name, ins, outs, scratch, flops, transcendentals=0, prefetch=()):
    moved = sum(array.size * array.dtype.itemsize for array in (*ins, *outs))
    return pl.pallas_call(
        kernel,
        grid_spec=pltpu.PrefetchScalarGridSpec(
            num_scalar_prefetch=len(prefetch),
            grid=(1,),
            in_specs=[fixed(array.shape) for array in ins],
            out_specs=[fixed(out.shape) for out in outs],
            scratch_shapes=scratch,
        ),
        out_shape=list(outs),
        compiler_params=pltpu.CompilerParams(vmem_limit_bytes=56 << 20),
        cost_estimate=pl.CostEstimate(
            flops=flops, bytes_accessed=moved, transcendentals=transcendentals
        ),
        name=name,
    )(*prefetch, *ins)


def padded(piece_rows):
    return -(-piece_rows // 128) * 128


def run_attention(near, ins):
    rows = ins[-1].shape[0]
    feat = ins[0].shape[1]
    piece = ins[-4].shape[0]
    width = padded(piece)
    outs = [jax.ShapeDtypeStruct((rows, feat), jnp.bfloat16)] * (2 if near else 0)
    outs = outs + [jax.ShapeDtypeStruct((rows, width), jnp.bfloat16)] * 4
    outs = outs + [jax.ShapeDtypeStruct((rows, 128), jnp.float32)]
    return call_whole(
        attention_near_kernel if near else attention_far_kernel,
        "attention_near" if near else "attention_far",
        ins,
        outs,
        [pltpu.VMEM((rows, rows), jnp.float32)],
        6 * rows * feat * width + 4 * rows * rows * width + (2 * rows * rows * feat if near else 0),
        rows * rows * piece // HD,
    )


def middle_kernel(
    half_slots,
    block,
    turn_ref,
    m0_ref,
    m1_ref,
    m2_ref,
    m3_ref,
    grouped_ref,
    o0_ref,
    o1_ref,
    o2_ref,
    o3_ref,
    gain_ref,
    router_ref,
    slots_ref,
    one_ref,
    two_ref,
    first_ref,
    second_ref,
    resid_ref,
    hidden_ref,
    sent_ref,
    weight_ref,
    mixed_ref,
    whole_ref,
):
    mixed = (m0_ref, m1_ref, m2_ref, m3_ref)
    parts = (o0_ref, o1_ref, o2_ref, o3_ref)
    width = m0_ref.shape[1]
    for turn in range(4):

        @pl.when(turn_ref[0] == turn)
        def _():
            for i in range(4):
                mixed_ref[:, i * width : (i + 1) * width] = mixed[i ^ turn][...]
                whole_ref[i * width : (i + 1) * width, :] = pad_rows(parts[i ^ turn][...], width)

    resid = grouped_ref[...].astype(jnp.float32) + matmul(mixed_ref[...], whole_ref[...])
    resid_ref[...] = resid
    hidden = (resid * rms_scale(resid) * gain_ref[...]).astype(jnp.bfloat16)
    hidden_ref[...] = hidden
    logits = matmul_bt(router_ref[...], hidden)
    chosen_one = jnp.sum(one_ref[...] * logits, axis=0, keepdims=True)
    chosen_two = jnp.sum(two_ref[...] * logits, axis=0, keepdims=True)
    top = jnp.maximum(chosen_one, chosen_two)
    raised_one = jnp.exp(chosen_one - top)
    raised_two = jnp.exp(chosen_two - top)
    weight_one = raised_one / (raised_one + raised_two)
    weight_two = raised_two / (raised_one + raised_two)
    weight_ref[0:1, :] = weight_one
    weight_ref[1:2, :] = weight_two
    gate_of = first_ref[...] * weight_one + second_ref[...] * weight_two
    high = gate_of.astype(jnp.bfloat16).astype(jnp.float32)
    rest = gate_of - high
    middle = rest.astype(jnp.bfloat16).astype(jnp.float32)
    three = jnp.concatenate([high, middle, rest - middle], axis=0).astype(jnp.bfloat16)
    lines = matmul_bt(three, slots_ref[...])
    dests = first_ref.shape[0]
    last = 16
    at = half_slots - (block - last)
    sub_last = lax.broadcasted_iota(jnp.int32, (last, block), 0)
    chunk = 256
    for base in range(0, slots_ref.shape[0], chunk):
        rows = matmul(slots_ref[base : base + chunk, :], hidden)
        sent_ref[base : base + chunk, :] = rows.astype(jnp.bfloat16)
        for inner in range(block, chunk + 1, block):
            dest = (base + inner) // block - 1
            for i in range(3):
                line = lines[i * dests + dest : i * dests + dest + 1, dest * block : (dest + 1) * block]
                old = rows[inner - last : inner, i * 128 : i * 128 + block]
                sent_ref[base + inner - last : base + inner, i * 128 : i * 128 + block] = jnp.where(
                    sub_last == at, line, old
                ).astype(jnp.bfloat16)


def run_middle(half_slots, block, turn, *ins):
    rows, width = ins[0].shape
    feat = ins[4].shape[1]
    slots = ins[11]
    outs = [
        jax.ShapeDtypeStruct((rows, feat), jnp.float32),
        jax.ShapeDtypeStruct((rows, feat), jnp.bfloat16),
        jax.ShapeDtypeStruct((slots.shape[0], feat), jnp.bfloat16),
        jax.ShapeDtypeStruct((8, rows), jnp.float32),
    ]
    return call_whole(
        functools.partial(middle_kernel, half_slots, block),
        "middle",
        ins,
        outs,
        [pltpu.VMEM((rows, 4 * width), jnp.bfloat16), pltpu.VMEM((4 * width, feat), jnp.bfloat16)],
        2 * rows * feat * (4 * width + slots.shape[0]),
        4 * rows,
        (turn,),
    )


def piece_gradients(d_proj, w_out, q_ref, k_ref, v_ref, lse_ref, bias_ref, cos, sin, all_ref):
    rows, width = q_ref.shape
    span = 256
    scale = HD ** (-0.5)
    lane_ids = lax.broadcasted_iota(jnp.int32, (rows, 128), 1)
    d_all = matmul_bt(d_proj, pad_rows(w_out, width)).astype(jnp.bfloat16)
    blocks = rows // span

    def unturn(values):
        return (values * cos - swap_halves(values) * sin).astype(jnp.bfloat16)

    for pair in range(width // 128):
        at = slice(pair * 128, pair * 128 + 128)
        k = k_ref[:, at]
        v = v_ref[:, at]
        q_scaled = q_ref[:, at] * jnp.bfloat16(scale)
        d_mixed = d_all[:, at]
        zero = jnp.zeros_like(q_scaled)
        d_q = [jnp.zeros((span, 128), jnp.float32) for _ in range(blocks)]
        d_k = [jnp.zeros((span, 128), jnp.float32) for _ in range(blocks)]
        d_v = [jnp.zeros((span, 128), jnp.float32) for _ in range(blocks)]
        for head in range(heads_of(w_out.shape[0], pair)):
            mask = (lane_ids < HD) if head == 0 else (lane_ids >= HD)
            q_head = jnp.where(mask, q_scaled, zero)
            k_head = jnp.where(mask, k, zero)
            d_head = jnp.where(mask, d_mixed, zero)
            which = pair * 2 + head
            for block in range(blocks):
                start, end = block * span, block * span + span
                lse = jnp.sum(
                    jnp.where(lane_ids[start:end] == which, lse_ref[start:end, :], 0.0),
                    axis=-1,
                    keepdims=True,
                )
                scores = matmul_bt(q_head[start:end], k[:end]) + bias_ref[start:end, :end]
                probs = jnp.exp(scores - lse)
                d_probs = matmul_bt(d_head[start:end], v[:end])
                inner = jnp.sum(probs * d_probs, axis=-1, keepdims=True)
                d_scores = (probs * (d_probs - inner)).astype(jnp.bfloat16)
                probs = probs.astype(jnp.bfloat16)
                d_q[block] = d_q[block] + matmul(d_scores, k_head[:end])
                key_term = matmul_at(d_scores, q_head[start:end])
                value_term = matmul_at(probs, d_head[start:end])
                for other in range(block + 1):
                    part = slice(other * span, other * span + span)
                    d_k[other] = d_k[other] + key_term[part]
                    d_v[other] = d_v[other] + value_term[part]
        at_k = slice(width + pair * 128, width + pair * 128 + 128)
        at_v = slice(2 * width + pair * 128, 2 * width + pair * 128 + 128)
        all_ref[:, at] = unturn(jnp.concatenate(d_q, axis=0) * scale)
        all_ref[:, at_k] = unturn(jnp.concatenate(d_k, axis=0))
        all_ref[:, at_v] = jnp.concatenate(d_v, axis=0).astype(jnp.bfloat16)


def back_near_kernel(
    turn_ref,
    dh_own_ref,
    dh_other_ref,
    dg_ref,
    weight_ref,
    one_ref,
    two_ref,
    router_ref,
    resid_ref,
    hidden_two_ref,
    cot_ref,
    gain_ref,
    hidden_ref,
    mixed_ref,
    start_ref,
    cos_ref,
    sin_ref,
    lse_ref,
    w_out_ref,
    q_ref,
    k_ref,
    v_ref,
    wq_ref,
    wk_ref,
    wv_ref,
    d_resid_ref,
    d_proj_ref,
    g_ffn_ref,
    g_router_ref,
    late_ref,
    term_ref,
    bias_ref,
    all_ref,
    dh_ref,
):
    half = dh_own_ref.shape[0]

    @pl.when(turn_ref[0] % 2 == 0)
    def _():
        dh_ref[:half, :] = dh_own_ref[...]
        dh_ref[half:, :] = dh_other_ref[...]

    @pl.when(turn_ref[0] % 2 == 1)
    def _():
        dh_ref[:half, :] = dh_other_ref[...]
        dh_ref[half:, :] = dh_own_ref[...]

    fill_bias(bias_ref, start_ref)
    weight_one, weight_two = (weight_ref[0:1, :], weight_ref[1:2, :])
    d_one, d_two = (dg_ref[0:1, :], dg_ref[1:2, :])
    inner = weight_one * d_one + weight_two * d_two
    d_logits = one_ref[...] * (weight_one * (d_one - inner))
    d_logits = d_logits + two_ref[...] * (weight_two * (d_two - inner))
    d_logits = d_logits.astype(jnp.bfloat16)
    g_router_ref[...] = matmul(d_logits, hidden_two_ref[...])
    d_rows = dh_ref[...].astype(jnp.float32) + matmul_at(d_logits, router_ref[...])
    resid = resid_ref[...]
    scale = rms_scale(resid)
    normed = resid * scale
    g_ffn_ref[...] = jnp.sum(d_rows * normed, axis=0, keepdims=True)
    grown = d_rows * gain_ref[...]
    shift = jnp.mean(grown * normed, axis=-1, keepdims=True)
    d_resid = cot_ref[...].astype(jnp.float32) + scale * (grown - normed * shift)
    d_resid_ref[...] = d_resid
    d_proj_ref[...] = d_resid.astype(jnp.bfloat16)
    piece_gradients(
        d_proj_ref[...],
        w_out_ref[...],
        q_ref,
        k_ref,
        v_ref,
        lse_ref,
        bias_ref,
        cos_ref[...],
        sin_ref[...],
        all_ref,
    )
    piece, width = (w_out_ref.shape[0], q_ref.shape[1])
    grads = matmul_at(all_ref[...], hidden_ref[...]).astype(jnp.bfloat16)
    for i in range(3):
        late_ref[i * piece : (i + 1) * piece, :] = grads[i * width : i * width + piece, :]
    g_out = matmul_at(mixed_ref[...], d_proj_ref[...]).astype(jnp.bfloat16)
    late_ref[3 * piece : 4 * piece, :] = g_out[:piece, :]
    whole = jnp.concatenate([pad_rows(w[...], width) for w in (wq_ref, wk_ref, wv_ref)], axis=0)
    term_ref[...] = matmul(all_ref[...], whole)


def run_back_near(turn, *ins):
    rows, feat = ins[7].shape
    piece = ins[17].shape[0]
    width = padded(piece)
    outs = [
        jax.ShapeDtypeStruct((rows, feat), jnp.float32),
        jax.ShapeDtypeStruct((rows, feat), jnp.bfloat16),
        jax.ShapeDtypeStruct((1, feat), jnp.float32),
        jax.ShapeDtypeStruct((EXPERTS, feat), jnp.float32),
        jax.ShapeDtypeStruct((4 * piece, feat), jnp.bfloat16),
        jax.ShapeDtypeStruct((rows, feat), jnp.float32),
    ]
    return call_whole(
        back_near_kernel,
        "back_near",
        ins,
        outs,
        [
            pltpu.VMEM((rows, rows), jnp.float32),
            pltpu.VMEM((rows, 3 * width), jnp.bfloat16),
            pltpu.VMEM((rows, feat), jnp.bfloat16),
        ],
        rows * width * (16 * feat + 10 * rows),
        rows * rows * piece // HD,
        (turn,),
    )


def back_far_kernel(
    d_proj_ref,
    start_ref,
    cos_ref,
    sin_ref,
    lse_ref,
    w_out_ref,
    q_ref,
    k_ref,
    v_ref,
    all_ref,
    bias_ref,
):
    fill_bias(bias_ref, start_ref)
    piece_gradients(
        d_proj_ref[...],
        w_out_ref[...],
        q_ref,
        k_ref,
        v_ref,
        lse_ref,
        bias_ref,
        cos_ref[...],
        sin_ref[...],
        all_ref,
    )


def run_back_far(*ins):
    rows, feat = ins[0].shape
    piece = ins[5].shape[0]
    width = padded(piece)
    return call_whole(
        back_far_kernel,
        "back_far",
        ins,
        [jax.ShapeDtypeStruct((rows, 3 * width), jnp.bfloat16)],
        [pltpu.VMEM((rows, rows), jnp.float32)],
        rows * width * (2 * feat + 10 * rows),
        rows * rows * piece // HD,
    )[0]


def back_rows_kernel(
    all_ref,
    d_resid_ref,
    term_ref,
    place_own_ref,
    place_other_ref,
    wq_ref,
    wk_ref,
    wv_ref,
    give_ref,
    keep_ref,
    d_half_ref,
    sum_ref,
):
    width = all_ref.shape[1] // 3
    whole = jnp.concatenate([pad_rows(w[...], width) for w in (wq_ref, wk_ref, wv_ref)], axis=0)
    sum_ref[...] = matmul(all_ref[...], whole)
    total = (term_ref[...] + sum_ref[...]).astype(jnp.bfloat16)
    give_ref[...] = matmul_at(place_other_ref[...], total).astype(jnp.bfloat16)
    keep_ref[...] = matmul_at(place_own_ref[...], total).astype(jnp.bfloat16)
    d_resid = d_resid_ref[...]
    high = d_resid.astype(jnp.bfloat16)
    low = (d_resid - high.astype(jnp.float32)).astype(jnp.bfloat16)
    d_half_ref[...] = matmul_at(place_own_ref[...], high) + matmul_at(place_own_ref[...], low)


def run_back_rows(*ins):
    rows, width = ins[0].shape
    feat = ins[1].shape[1]
    half = ins[3].shape[1]
    outs = [
        jax.ShapeDtypeStruct((half, feat), jnp.bfloat16),
        jax.ShapeDtypeStruct((half, feat), jnp.bfloat16),
        jax.ShapeDtypeStruct((half, feat), jnp.float32),
    ]
    return call_whole(
        back_rows_kernel,
        "back_rows",
        ins,
        outs,
        [pltpu.VMEM((rows, feat), jnp.float32)],
        2 * rows * width * feat + 8 * rows * half * feat,
    )


def body(
    tokens,
    order,
    lengths,
    routes,
    attn_gain,
    w_query,
    w_key,
    w_value,
    w_out,
    ffn_gain,
    w_router,
    shared_gate,
    shared_up,
    shared_down,
    expert_gate,
    expert_up,
    expert_down,
    cotangent,
):
    row_count, feat_width = tokens.shape
    group_count = lax.axis_size("expert")
    share_rows = row_count // group_count
    half_share = share_rows // 2
    half_rows = row_count // 2
    my_group = lax.axis_index("expert")
    my_tensor = lax.axis_index("tensor")
    bit_low = lax.rem(my_tensor, 2)
    bit_high = my_tensor // 2
    slab_dev = expert_gate.shape[0]
    slab_total = slab_dev * group_count
    replicas = max(1, slab_total // EXPERTS)
    half_slots = slab_dev * CAP // 2
    row_ids = jnp.arange(row_count, dtype=jnp.int32)
    earlier = (row_ids[:, None] < row_ids[None, :]).astype(jnp.bfloat16)

    local_order = lax.dynamic_slice_in_dim(order, my_group * row_count, row_count, 0)
    groups = jnp.arange(group_count, dtype=jnp.int32)
    dest_group = local_order // row_count
    dest_onehot = (groups[:, None] == dest_group[None, :]).astype(jnp.bfloat16)
    dest_before = matmul(dest_onehot, earlier)
    send_rank = jnp.sum(dest_onehot.astype(jnp.float32) * dest_before, axis=0).astype(jnp.int32)
    send_half = send_rank // half_share
    send_slot = send_half * half_rows + dest_group * half_share + send_rank % half_share
    send_pick = send_slot[None, :] == (
        bit_low * half_rows + jnp.arange(half_rows, dtype=jnp.int32)[:, None]
    )
    send_pick = send_pick.astype(jnp.bfloat16)
    in_tokens = exchange(select(send_pick, tokens))
    cot_send, in_tokens = tie(select(send_pick, cotangent), in_tokens)
    in_cot = exchange(cot_send)

    near_weights = (w_query.T, w_key.T, w_value.T)
    far_weights = tuple(far_swap(weight) for weight in near_weights)
    out_far = far_swap(after(w_out, far_weights[1]))
    tokens_other = core_swap(in_tokens)
    turn = my_tensor.reshape(1)

    all_order = order.reshape(group_count, row_count)
    mine = all_order // row_count == my_group
    arrive_rank = matmul(mine.astype(jnp.bfloat16), earlier).astype(jnp.int32)
    arrive_rank = jnp.where(mine, arrive_rank, -1)
    landing = all_order - my_group * row_count
    target = jnp.sum(
        jnp.where(
            arrive_rank[:, None, :] == jnp.arange(share_rows, dtype=jnp.int32)[None, :, None],
            landing[:, None, :],
            0,
        ),
        axis=-1,
    )
    target = target.reshape(group_count, 2, half_share).transpose(1, 0, 2).reshape(2, half_rows)
    target_own = lax.dynamic_index_in_dim(target, bit_low, 0, keepdims=False)
    target_other = lax.dynamic_index_in_dim(target, 1 - bit_low, 0, keepdims=False)
    place_own = (row_ids[:, None] == target_own[None, :]).astype(jnp.bfloat16)
    place_other = (row_ids[:, None] == target_other[None, :]).astype(jnp.bfloat16)

    expert_ids = jnp.arange(EXPERTS, dtype=jnp.int32)
    member_one = expert_ids[:, None] == routes[None, :, 0]
    member_two = expert_ids[:, None] == routes[None, :, 1]
    member = member_one | member_two
    slot_rank = matmul(member.astype(jnp.bfloat16), earlier).astype(jnp.int32)
    slot_rank = jnp.where(member, slot_rank, -1)

    block = (half_slots + 16) // 16 * 16
    ranks = jnp.repeat(slot_rank, replicas, axis=0).reshape(group_count, slab_dev, row_count)
    ranks = lax.dynamic_index_in_dim(ranks, bit_low * half_slots // CAP, 1, keepdims=False)
    slot_ids = jnp.arange(block, dtype=jnp.int32)
    slots = bit_low * half_slots % CAP + slot_ids
    slots = jnp.where(slot_ids < half_slots, slots, -2)
    slots_cube = (ranks[:, None, :] == slots[None, :, None]).astype(jnp.bfloat16)
    slots_one = slots_cube.reshape(group_count * block, row_count)

    quarter = block // 2
    slots_part = lax.dynamic_slice_in_dim(slots_cube, bit_high * quarter, quarter, 1)
    slots_part = slots_part.reshape(-1, row_count)
    cot_pick_own = select(slots_part, place_own)
    cot_pick_other = select(slots_part, place_other)

    seq_lengths = lengths[0]
    seq_ends = jnp.cumsum(seq_lengths)
    passed = row_ids[:, None] >= seq_ends[None, :]
    sequence_segment = jnp.sum(passed.astype(jnp.int32), axis=1)
    position = row_ids - jnp.sum(jnp.where(passed, seq_lengths[None, :], 0), axis=1)
    half_size = HD // 2
    lanes = jnp.arange(128, dtype=jnp.int32)
    frequency = ROPE_BASE ** (-(lanes % half_size).astype(jnp.float32) / half_size)
    angles = position.astype(jnp.float32)[:, None] * frequency[None, :]
    cos_table = jnp.cos(angles)
    sin_table = jnp.where(lanes % HD < half_size, -1.0, 1.0) * jnp.sin(angles)
    seq_start = jnp.broadcast_to((row_ids - position)[:, None], (row_count, 128))
    gain_one = attn_gain.astype(jnp.float32)[None, :]
    gain_two = ffn_gain.astype(jnp.float32)[None, :]
    tables = (cos_table, sin_table, seq_start)
    grouped, hidden_one, *near_heads, near_mixed, near_lse = run_attention(
        True,
        (in_tokens, tokens_other, place_own, place_other, gain_one, *near_weights, *tables),
    )
    near_swapped = core_swap(near_mixed)
    far_weights = after(far_weights, near_mixed)
    *far_heads, far_mixed, far_lse = run_attention(False, (hidden_one, *far_weights, *tables))
    far_swapped = core_swap(far_mixed)
    out_pieces = (w_out, core_swap(w_out), out_far, core_swap(out_far))
    in_cot = after(in_cot, far_mixed)
    cot_half = core_swap(in_cot)
    cot_part = matmul(cot_pick_own, in_cot) + matmul(cot_pick_other, cot_half)
    cot_part = cot_part.astype(jnp.bfloat16)
    far_swapped = after(far_swapped, cot_part)
    cot_part = exchange(cot_part)

    dest_slab = jnp.arange(group_count, dtype=jnp.int32) * slab_dev + bit_low * half_slots // CAP
    dest_expert = dest_slab // replicas
    first_here = (routes[None, :, 0] == dest_expert[:, None]).astype(jnp.float32)
    second_here = (routes[None, :, 1] == dest_expert[:, None]).astype(jnp.float32)
    one_of = member_one.astype(jnp.float32)
    two_of = member_two.astype(jnp.float32)
    router_rows = w_router.T
    resid_two, hidden_two, sent, gate_weights = run_middle(
        half_slots,
        block,
        turn,
        near_mixed,
        near_swapped,
        far_mixed,
        far_swapped,
        grouped,
        *out_pieces,
        gain_two,
        router_rows,
        slots_one,
        one_of,
        two_of,
        first_here,
        second_here,
    )
    hidden_rows = exchange(after(sent, cot_part))
    cot_part = cot_part.reshape(group_count, quarter, feat_width)
    cot_own = in_order(bit_high, cot_part, far_swap(cot_part), 1).reshape(-1, feat_width)
    cot_other = core_swap(cot_own)
    grouped_cot = matmul(place_own, after(in_cot, sent)) + matmul(place_other, cot_half)
    grouped_cot = grouped_cot.astype(jnp.bfloat16)
    hidden_late = after(hidden_two, cot_part)

    gate_shared = matmul(hidden_two, shared_gate)
    up_shared = matmul(hidden_late, shared_up)
    act_shared = silu_value(gate_shared)
    shared_mid = (act_shared * up_shared).astype(jnp.bfloat16)
    shared_out = matmul(shared_mid, shared_down)
    d_mid_shared = matmul_bt(grouped_cot, shared_down)
    d_up_shared = (d_mid_shared * act_shared).astype(jnp.bfloat16)
    d_gate_shared = (d_mid_shared * up_shared * silu_slope(gate_shared)).astype(jnp.bfloat16)
    d_both = jnp.concatenate([d_gate_shared, d_up_shared], axis=1)
    early = GroupSum(
        jnp.concatenate([matmul_at(d_both, hidden_late), matmul_at(shared_mid, grouped_cot)], axis=0)
    )
    early.start()
    d_gate_shared, d_up_shared, shared_out, resid_late, _ = tie(
        d_gate_shared, d_up_shared, shared_out, resid_two, early.given
    )
    d_hidden_shared = matmul_bt(d_gate_shared, shared_gate) + matmul_bt(d_up_shared, shared_up)
    shared_send = shared_out.astype(jnp.bfloat16)
    shared_own = matmul_at(place_own, shared_send)
    shared_other = matmul_at(place_other, shared_send)
    resid_high, resid_low = three_parts(resid_late)[:2]
    resid_half = matmul_at(place_own, resid_high) + matmul_at(place_own, resid_low)
    hidden_rows = after(
        hidden_rows, cot_other, d_hidden_shared, shared_own, shared_other, resid_half
    )
    rows_other = core_swap(hidden_rows)
    early.end(d_hidden_shared, shared_own, shared_other, resid_half)
    early.start()
    rows_other = after(rows_other, early.given)

    which_own = (bit_low * half_slots // CAP).reshape(1)
    which_other = ((1 - bit_low) * half_slots // CAP).reshape(1)
    weights_here = (expert_gate, expert_up, expert_down, half_slots, block)
    back_given, out_given, mid_other, dg_other, du_other = run_expert(
        which_other, rows_other, cot_other, *weights_here
    )
    early.end(back_given)
    early.start()
    back_given = after(back_given, early.given)
    hidden_rows = after(hidden_rows, back_given)
    back_kept, out_kept, mid_own, dg_own, du_own = run_expert(
        which_own, hidden_rows, cot_own, *weights_here
    )
    stack_own = (hidden_rows, cot_own, mid_own, dg_own, du_own)
    stack_other = (rows_other, cot_other, mid_other, dg_other, du_other)

    back_sum = back_kept.astype(jnp.float32) + core_swap(back_given).astype(jnp.float32)
    back_sum = back_sum.reshape(group_count, block, feat_width)
    lines = back_sum[:, half_slots, :384].reshape(group_count, 3, 128)
    lines = jnp.stack(three_parts(jnp.sum(lines, axis=1)), axis=1).astype(jnp.float32)
    lines = jnp.pad(lines.reshape(group_count, 1, 384), ((0, 0), (0, 0), (0, feat_width - 384)))
    back_sum = jnp.where(slot_ids[None, :, None] == half_slots, lines, back_sum)
    back_send = back_sum.astype(jnp.bfloat16).reshape(-1, feat_width)
    back_own = exchange(back_send)
    early.end(back_send)
    while early.stage < early.bits:
        early.start()
        early.end()
    out_sum = pair_sum(out_kept, after(out_given, back_send, early.part))
    out_sum = out_sum.reshape(group_count, block, feat_width)
    out_kept = lax.dynamic_slice_in_dim(out_sum, bit_high * quarter, quarter, 1)
    out_given = lax.dynamic_slice_in_dim(out_sum, (1 - bit_high) * quarter, quarter, 1)
    out_send = out_kept.astype(jnp.float32) + far_swap(out_given).astype(jnp.float32)
    out_send = out_send.astype(jnp.bfloat16).reshape(-1, feat_width)
    if slab_dev == 2:
        own_late = after(stack_own[0], out_given)
        stack_own = (own_late,) + stack_own[1:]
        g_expert_gate, g_expert_up, g_expert_down = run_weights(bit_low, stack_own, stack_other)
    else:
        wide = [jnp.concatenate(pair, axis=0) for pair in zip(stack_own, stack_other)]
        g_expert_gate = matmul_at(wide[0], wide[3])[None]
        g_expert_up = matmul_at(wide[0], wide[4])[None]
        g_expert_down = matmul_at(wide[2], wide[1])[None]


    halves = [
        tuple(
            lax.dynamic_slice_in_dim(values, bit * half_rows, half_rows, axis)
            for values, axis in ((slots_one, 1), (d_hidden_shared, 0))
        )
        for bit in (1 - bit_low, bit_low)
    ]
    back_own, *halves = tie(back_own, *halves, g_expert_gate, out_send)[:3]
    given, kept = (
        (matmul_at(slots, back_own) + shared).astype(jnp.bfloat16) for slots, shared in halves
    )
    kept = after(kept, given)
    dg_lines = back_own.reshape(group_count, block, feat_width)[:, half_slots, :384]
    dg_lines = dg_lines.reshape(group_count, 3, 128)[:, :, :block]
    dg_of = jnp.einsum("dps,dsr->dpr", dg_lines, slots_cube, preferred_element_type=jnp.float32)
    dg_of = jnp.sum(dg_of, axis=1)
    dg_part = jnp.stack(
        [jnp.sum(first_here * dg_of, axis=0), jnp.sum(second_here * dg_of, axis=0)], axis=0
    )
    dg_part = jnp.pad(dg_part, ((0, 6), (0, 0)))
    dg_part = dg_part + core_swap(dg_part)
    pair = pair_sum(kept, given)
    early.start(pair)
    far, early.came, dg_far = tie(far_swap(pair), early.came, far_swap(dg_part))
    d_hidden_half = (pair.astype(jnp.float32) + far.astype(jnp.float32)).astype(jnp.bfloat16)
    early.end(d_hidden_half)
    out_own = exchange(after(out_send, d_hidden_half))
    d_hidden_other = core_swap(d_hidden_half)
    dg_part = dg_part + dg_far
    d_resid, d_proj, g_ffn_gain, g_router, late, term = run_back_near(
        turn,
        d_hidden_half,
        d_hidden_other,
        dg_part,
        gate_weights,
        one_of,
        two_of,
        router_rows,
        resid_two,
        hidden_two,
        grouped_cot,
        gain_two,
        hidden_one,
        near_mixed,
        seq_start,
        cos_table,
        sin_table,
        near_lse,
        w_out,
        *near_heads,
        *near_weights,
    )
    early.start(d_proj)
    late = GroupSum(late, True)
    late.start()
    ffn_rows = after(out_own, late.given)
    ffn_given = (matmul_at(cot_pick_other, ffn_rows) + shared_other).astype(jnp.bfloat16)
    ffn_kept = (matmul_at(cot_pick_own, ffn_rows) + shared_own).astype(jnp.bfloat16)
    ffn_pair = pair_sum(ffn_kept, ffn_given)
    ffn_half = ffn_pair.astype(jnp.float32) + far_swap(ffn_pair).astype(jnp.float32)
    output_send = (resid_half + ffn_half).astype(jnp.bfloat16)
    far_all = run_back_far(
        after(d_proj, ffn_pair),
        seq_start,
        cos_table,
        sin_table,
        far_lse,
        out_far,
        *far_heads,
    )
    late.end(far_all)
    late.start()
    early.end(far_all)
    early.start_first(4)
    d_one_given, d_one_kept, d_resid_half = run_back_rows(
        after(far_all, output_send, late.given),
        d_resid,
        term,
        place_own,
        place_other,
        *far_weights,
    )
    late.end(d_one_given)
    late.start()
    early.first, d_one_given = tie(early.first, d_one_given)
    d_one = d_one_kept.astype(jnp.float32) + core_swap(d_one_given).astype(jnp.float32)
    resid = in_tokens.astype(jnp.float32)
    scale_one = rms_scale(resid)
    normed_one = resid * scale_one
    e_one = d_one * gain_one
    shift_one = jnp.mean(e_one * normed_one, axis=-1, keepdims=True)
    d_tokens_send = (d_resid_half + scale_one * (e_one - normed_one * shift_one)).astype(jnp.bfloat16)
    g_attn_gain = jnp.sum(d_one * normed_one, axis=0, keepdims=True)
    both_send = jnp.concatenate(
        [
            d_tokens_send.reshape(group_count, half_share, feat_width),
            output_send.reshape(group_count, half_share, feat_width),
        ],
        axis=1,
    )
    small = jnp.concatenate([g_router, g_ffn_gain, g_attn_gain + core_swap(g_attn_gain)], axis=0)
    small = jnp.pad(small, ((0, -small.shape[0] % 8), (0, 0)))
    small = small + group_swap(small, 0)
    early.start_second(small)
    late.came, both_send, small_came = tie(late.came, both_send, group_swap(small, 1))
    small = small + small_came
    late.end()
    late.start()
    late.came, small_came, both_send = tie(late.came, group_swap(small, 2), both_send)
    both_own = exchange(both_send)
    small = small + small_came
    for step in range(3, group_count.bit_length() - 1):
        small = small + group_swap(small, step)
    late.end()
    late.start()
    early.end_second(late.part)
    g_router = small[:EXPERTS].T
    g_ffn_gain = small[EXPERTS]
    g_attn_gain = small[EXPERTS + 1]
    late = late.finish().astype(jnp.float32)
    shared = early.finish(late).astype(jnp.float32)
    hidden_s = shared_gate.shape[1]
    g_shared_gate = shared[:hidden_s].T
    g_shared_up = shared[hidden_s : 2 * hidden_s].T
    g_shared_down = shared[2 * hidden_s :]
    head_rows = w_out.shape[0]
    g_query = late[:head_rows].T
    g_key = late[head_rows : 2 * head_rows].T
    g_value = late[2 * head_rows : 3 * head_rows].T
    g_out = late[3 * head_rows :]
    both_own = after(
        both_own, g_query, g_key, g_value, g_out, g_shared_gate, g_shared_up, g_shared_down, small
    )
    both_other = core_swap(both_own)

    unsend = (send_slot[:, None] == row_ids[None, :]).astype(jnp.bfloat16)

    def arrive_back(part):
        own = both_own[:, part].reshape(half_rows, feat_width)
        other = both_other[:, part].reshape(half_rows, feat_width)
        return select(unsend, in_order(bit_low, own, other))

    d_tokens = arrive_back(slice(0, half_share))
    output = arrive_back(slice(half_share, 2 * half_share))
    return (
        output,
        d_tokens,
        g_attn_gain,
        g_query,
        g_key,
        g_value,
        g_out,
        g_ffn_gain,
        g_router,
        g_shared_gate,
        g_shared_up,
        g_shared_down,
        g_expert_gate,
        g_expert_up,
        g_expert_down,
    )


def solution(mesh):
    return jax.shard_map(
        body,
        mesh=mesh,
        in_specs=(
            P("expert", None),
            P(),
            P("expert", None),
            P("expert", None),
            P(),
            P(None, "tensor"),
            P(None, "tensor"),
            P(None, "tensor"),
            P("tensor", None),
            P(),
            P(),
            P(None, "tensor"),
            P(None, "tensor"),
            P("tensor", None),
            P("expert", None, "tensor"),
            P("expert", None, "tensor"),
            P("expert", "tensor", None),
            P("expert", None),
        ),
        out_specs=(
            P("expert", None),
            P("expert", None),
            P(),
            P(None, "tensor"),
            P(None, "tensor"),
            P(None, "tensor"),
            P("tensor", None),
            P(),
            P(),
            P(None, "tensor"),
            P(None, "tensor"),
            P("tensor", None),
            P("expert", None, "tensor"),
            P("expert", None, "tensor"),
            P("expert", "tensor", None),
        ),
        check_vma=False,
    )
```
